32 devices in a mesh: row: 8 (over z, core), col: 2 (over y), feat: 2 (over x).
Axes of the slice: x: 2, y: 2, z: 4, core: 2. Of those that a mesh axis runs over, the one named last changes fastest.
Arguments:
- features: bfloat16 [8192, 256], P(('col', 'row'), 'feat'), may hold values from -6 to 6
- tile_rows: int32 [8, 2, 256], P('row', 'col'), may hold values from 0 to 7, as said below
- tile_cols: int32 [8, 2, 256], P('row', 'col'), may hold values from 0 to 31
- tile_count: int32 [8, 2], P('row', 'col'), may hold values from 64 to 256, as said below
- tile_values: bfloat16 [8, 2, 256, 128, 128], P('row', 'col'), may hold values from -0.21875 to 0.21875
- weights: bfloat16 [256, 256], replicated, may hold values from -0.375 to 0.375
- cotangent: bfloat16 [8192, 256], P(('row', 'col'), 'feat'), may hold values from -6 to 6
Outputs:
- activated: bfloat16 [8192, 256], P(('row', 'col'), 'feat')
- feature_grad: bfloat16 [8192, 256], P(('col', 'row'), 'feat')
- weight_grad: float32 [256, 256], P('feat')
The draws below stay inside these ranges and needn't reach their ends.
Inputs may be any that keep to these rules, and one draw needn't show every extreme that they name: `tile_rows`: block rows of a cell, unevenly loaded. `tile_count`: some cell has all 256 slots live.
All inputs are finite; a program needn't handle non-finite values.
Results may differ from the reference program's by a relative error of at most 0.027.
Values may be sent and summed in bfloat16 or wider, within the bound.
No kernel may reach another device: no remote copies, remote signals or barrier semaphores. Data moves between devices by JAX's collectives and lax.ppermute only.
A program may use at most 128 MiB of HBM per device.

```python
import jax
import jax.numpy as jnp
from jax import lax

F = 256
TILE = 128
BLK = 4
TILES = 256
NODES = 8192
RB = 8
CB = 32
N_ROW = 8
N_COL = 2


def draw_tile_rows(key, part):
    first_key, second_key, order_key = jax.random.split(jax.random.fold_in(key, 11), 3)
    first = jax.random.randint(first_key, (N_ROW, N_COL, TILES), 0, BLK * N_COL)
    second = jax.random.randint(second_key, (N_ROW, N_COL, TILES), 0, BLK * N_COL)
    lower = jnp.minimum(first, second)
    ordering = jax.random.permutation(order_key, BLK * N_COL)
    return ordering[lower].astype(jnp.int32)


def draw_tile_cols(key, part):
    return jax.random.randint(jax.random.fold_in(key, 12), (N_ROW, N_COL, TILES), 0, BLK * N_ROW).astype(jnp.int32)


def draw_tile_count(key, part):
    count_key, pick_key = jax.random.split(jax.random.fold_in(key, 13), 2)
    counts = jax.random.randint(count_key, (N_ROW * N_COL,), TILES // 4, TILES + 1)
    chosen = jax.random.randint(pick_key, (), 0, N_ROW * N_COL)
    filled = jnp.where(jnp.arange(N_ROW * N_COL) == chosen, TILES, counts)
    return filled.reshape(N_ROW, N_COL).astype(jnp.int32)


def shard_levels(stream_key, shape, cuts, low, high):
    gain = 1.0
    for axis_at, shards_of in cuts:
        draws = jax.random.uniform(jax.random.fold_in(jax.random.fold_in(stream_key, 6), axis_at), (shards_of,), jnp.float32, low / len(cuts), high / len(cuts))
        gain = gain * jnp.repeat(jnp.exp(draws), shape[axis_at] // shards_of).reshape((-1,) + (1,) * (len(shape) - 1 - axis_at))
    return gain


def noise(own_key, extent, scale, bound, shards=(), dtype=jnp.bfloat16):
    array = scale * jax.random.normal(own_key, extent, jnp.float32)
    if shards:
        array = array * shard_levels(own_key, extent, shards, -0.22, 0.18)
    return jnp.clip(array, -bound, bound).astype(dtype)


def setup_inputs(seed: int = 0) -> dict:
    keys = jax.random.split(jax.random.key(seed), 8)
    return {
        "features": noise(keys[0], (NODES, F), 1.0, 6.0, ((0, 16), (1, 2))),
        "tile_rows": draw_tile_rows(jax.random.fold_in(keys[7], 71), 0),
        "tile_cols": draw_tile_cols(jax.random.fold_in(keys[7], 71), 0),
        "tile_count": draw_tile_count(jax.random.fold_in(keys[7], 71), 0),
        "tile_values": noise(keys[4], (N_ROW, N_COL, TILES, TILE, TILE), ((BLK / (0.6 * TILES * TILE)) ** 0.5), 0.21875, ((0, 8), (1, 2))),
        "weights": noise(keys[5], (F, F), F ** -0.5, 0.375),
        "cotangent": noise(keys[6], (NODES, F), 1.0, 6.0, ((0, 16), (1, 2))),
    }


def round_once(values):
    rounded = lax.optimization_barrier(values.astype(jnp.bfloat16))
    return rounded.astype(jnp.float32)


def forward_cell(cell_tiles, cell_rows, cell_cols, cell_count, group_feats):
    live_mask = (jnp.arange(TILES) < cell_count).astype(jnp.float32)
    gathered = group_feats[cell_cols].astype(jnp.float32)
    products = jnp.einsum("tij,tjf->tif", cell_tiles.astype(jnp.float32), gathered) * live_mask[:, None, None]
    partial_value = jnp.zeros((RB, TILE, F), jnp.float32).at[cell_rows].add(products)
    return round_once(partial_value)


def backward_cell(cell_tiles, cell_rows, cell_cols, cell_count, group_spread):
    live_mask = (jnp.arange(TILES) < cell_count).astype(jnp.float32)
    gathered = group_spread[cell_rows].astype(jnp.float32)
    products = jnp.einsum("tji,tjf->tif", cell_tiles.astype(jnp.float32), gathered) * live_mask[:, None, None]
    partial_value = jnp.zeros((CB, TILE, F), jnp.float32).at[cell_cols].add(products)
    return round_once(partial_value)


def reference(features, tile_rows, tile_cols, tile_count, tile_values, weights, cotangent):
    feat_groups = features.reshape(N_COL, CB, TILE, F)

    def over_rows(unused, inputs):
        row_tiles, row_rows, row_cols, row_count = inputs

        def over_cols(running, cell_in):
            cell_tiles, cell_rows, cell_cols, cell_count, group_feats = cell_in
            return running + forward_cell(cell_tiles, cell_rows, cell_cols, cell_count, group_feats), None

        running, _ = lax.scan(over_cols, jnp.zeros((RB, TILE, F), jnp.float32),
                              (row_tiles, row_rows, row_cols, row_count, feat_groups))
        return unused, running

    _, stacked = lax.scan(over_rows, jnp.float32(0.0), (tile_values, tile_rows, tile_cols, tile_count))
    aggregated = stacked.reshape(NODES, F).astype(jnp.bfloat16)
    hidden = jnp.dot(aggregated, weights, preferred_element_type=jnp.float32)
    negative = jnp.minimum(hidden, 0.0)
    activated = jnp.where(hidden > 0, hidden, jnp.expm1(negative)).astype(jnp.bfloat16)
    slope_factor = jnp.where(hidden > 0, 1.0, jnp.exp(negative))
    grad_out = (cotangent.astype(jnp.float32) * slope_factor).astype(jnp.bfloat16)
    weight_grad = jnp.dot(aggregated.T, grad_out, preferred_element_type=jnp.float32) * (NODES ** -0.5)
    spread = jnp.dot(grad_out, weights.T, preferred_element_type=jnp.float32).astype(jnp.bfloat16)
    spread_groups = spread.reshape(N_ROW, RB, TILE, F)

    def back_rows(running, inputs):
        row_tiles, row_rows, row_cols, row_count, group_spread = inputs

        def back_cols(inner, cell_in):
            cell_tiles, cell_rows, cell_cols, cell_count, col_index = cell_in
            term = backward_cell(cell_tiles, cell_rows, cell_cols, cell_count, group_spread)
            return inner.at[col_index].add(term), None

        running, _ = lax.scan(back_cols, running,
                              (row_tiles, row_rows, row_cols, row_count, jnp.arange(N_COL).astype(jnp.int32)))
        return running, None

    back_total, _ = lax.scan(back_rows, jnp.zeros((N_COL, CB, TILE, F), jnp.float32),
                             (tile_values, tile_rows, tile_cols, tile_count, spread_groups))
    feature_grad = back_total.reshape(NODES, F).astype(jnp.bfloat16)
    return activated, feature_grad, weight_grad
```

```python
import functools

import jax
import jax.numpy as jnp
from jax import lax
from jax.experimental import pallas as pl
from jax.experimental.pallas import tpu as pltpu
from jax.sharding import PartitionSpec as P

F32 = jnp.float32
BF16 = jnp.bfloat16
VMEM_LIMIT = 48 * 1024 * 1024


def params(*semantics):
    return pltpu.CompilerParams(vmem_limit_bytes=VMEM_LIMIT)


def vmem():
    return pl.BlockSpec(memory_space=pltpu.VMEM)


def smem():
    return pl.BlockSpec(memory_space=pltpu.SMEM)


def densify_kernel(
    dims, info, rows, cols, count, tiles, out, buffer, head, following, sems
):
    n_z, n_col, blocks, slots, groups = dims
    chunk = pl.program_id(0)
    per_chunk = n_col * blocks * blocks
    per_group = slots // groups

    def copy(g):
        part = pl.ds(g * per_group, per_group)
        return pltpu.make_async_copy(tiles.at[part], buffer.at[part], sems.at[g])

    @pl.when(chunk == 0)
    def _():
        for g in range(groups):
            copy(g).start()
        z, core, c = info[0], info[1], info[2]

        def clear(i, carry):
            head[i] = slots
            return carry

        lax.fori_loop(0, 2 * n_z * per_chunk, clear, 0, unroll=8)
        following[slots] = slots
        buffer[slots] = jnp.zeros(buffer.shape[1:], buffer.dtype)

        def link(slot, carry):
            block_row, block_col = rows[0, 0, slot], cols[0, 0, slot]
            source, owner = block_col // blocks, block_row // blocks
            shift = z - source // 2
            shift = jnp.where(shift < 0, shift + n_z, shift)
            j = 2 * shift + ((source + core) & 1)
            t = c - owner
            t = jnp.where(t < 0, t + n_col, t)
            place = ((j * n_col + t) * blocks + block_row % blocks) * blocks + block_col % blocks
            following[slot] = head[place]
            head[place] = slot
            return carry

        lax.fori_loop(0, count[0, 0], link, 0)
        for g in range(groups):
            copy(g).wait()

    tile = buffer.shape[1]

    def fill(i, carry):
        first = head[chunk * per_chunk + i]
        t = i // (blocks * blocks)
        a = pl.multiple_of((i // blocks) % blocks * tile, tile)
        b = pl.multiple_of(i % blocks * tile, tile)
        where = (0, t, pl.ds(a, tile), pl.ds(b, tile))
        out[where] = buffer[first]
        second = following[first]

        @pl.when(second != slots)
        def _():
            def more(state):
                slot, total = state
                return following[slot], total + buffer[slot].astype(F32)

            _, total = lax.while_loop(
                lambda state: state[0] != slots,
                more,
                (second, buffer[first].astype(F32)),
            )
            out[where] = total.astype(BF16)

        return carry

    lax.fori_loop(0, per_chunk, fill, 0)


def densify(info, rows, cols, count, tiles, n_z, n_col, blocks):
    slots, tile = tiles.shape[0], tiles.shape[1]
    n_src = 2 * n_z
    groups = 8
    side = blocks * tile
    shape = (n_src, n_col, side, side)
    return pl.pallas_call(
        functools.partial(densify_kernel, (n_z, n_col, blocks, slots, groups)),
        grid=(n_src,),
        out_shape=jax.ShapeDtypeStruct(shape, BF16),
        in_specs=[smem(), smem(), smem(), smem(), pl.BlockSpec(memory_space=pl.ANY)],
        out_specs=pl.BlockSpec((1, n_col, side, side), lambda j: (j, 0, 0, 0)),
        scratch_shapes=[
            pltpu.VMEM((slots + 1, tile, tile), BF16),
            pltpu.SMEM((n_src * n_col * blocks * blocks,), jnp.int32),
            pltpu.SMEM((slots + 1,), jnp.int32),
            pltpu.SemaphoreType.DMA((groups,)),
        ],
        compiler_params=params(),
        cost_estimate=pl.CostEstimate(
            flops=0, bytes_accessed=24 * 1024 * 1024, transcendentals=0
        ),
        name="densify",
    )(info, rows, cols, count, tiles)


def forward_kernel(first, a, x0, x1, *rest):

    j = pl.program_id(1)

    @pl.when(j == 0)
    def _():
        value = jnp.dot(a[0, 0], x0[...], preferred_element_type=F32)
        if not first:
            value = value + rest[0][...]
        rest[-1][...] = value

    @pl.when(j == 1)
    def _():
        rest[-1][...] += jnp.dot(a[0, 0], x1[...], preferred_element_type=F32)


def forward(dense, shift, x0, x1, total):
    _, n_col, side, _ = dense.shape
    feats = x0.shape[1]
    first = total is None
    block = pl.BlockSpec((side, feats), lambda t, j: (t, 0))
    return pl.pallas_call(
        functools.partial(forward_kernel, first),
        grid=(n_col, 2),
        out_shape=jax.ShapeDtypeStruct((n_col * side, feats), F32),
        in_specs=[
            pl.BlockSpec((1, 1, side, side), lambda t, j: (2 * shift + j, t, 0, 0)),
            vmem(),
            vmem(),
        ]
        + ([] if first else [block]),
        out_specs=block,
        compiler_params=params(),
        cost_estimate=pl.CostEstimate(
            flops=4 * n_col * side * side * feats,
            bytes_accessed=4 * n_col * side * side,
            transcendentals=0,
        ),
        name="forward",
    )(dense, x0, x1, *([] if first else [total]))


def middle_kernel(n_col, info, weights, cot_own, cot_other, *refs):
    own = refs[:n_col]
    other = refs[n_col : 2 * n_col]
    activated, spread, keep, send = refs[2 * n_col :]
    half = cot_own.shape[1]
    core, f = info[1], info[3]
    mine = pl.ds(pl.multiple_of(f * half, half), half)
    theirs = pl.ds(pl.multiple_of((1 - f) * half, half), half)

    def gather(parts):
        total = parts[0][...].astype(F32)
        for part in parts[1:]:
            total = total + part[...].astype(F32)
        return total.astype(BF16)

    agg_own, agg_other = gather(own), gather(other)

    def hidden(columns):
        return jnp.dot(
            agg_own, weights[mine, columns], preferred_element_type=F32
        ) + jnp.dot(agg_other, weights[theirs, columns], preferred_element_type=F32)

    h = hidden(mine)
    decay = jnp.exp(jnp.minimum(h, 0.0))
    activated[...] = jnp.where(h > 0, h, decay - 1.0).astype(BF16)
    g_own = (cot_own[...].astype(F32) * decay).astype(BF16)
    h = hidden(theirs)
    decay = jnp.exp(jnp.minimum(h, 0.0))
    g_other = (cot_other[...].astype(F32) * decay).astype(BF16)
    across = (((1,), (1,)), ((), ()))
    spread[...] = (
        lax.dot_general(g_own, weights[mine, mine], across, preferred_element_type=F32)
        + lax.dot_general(g_other, weights[mine, theirs], across, preferred_element_type=F32)
    ).astype(BF16)
    down = (((0,), (0,)), ((), ()))
    rows = half // 2
    for columns, g in ((mine, g_own), (theirs, g_other)):
        term = lax.dot_general(agg_own, g, down, preferred_element_type=F32).astype(BF16)

        @pl.when(core == 0)
        def _():
            keep[:, columns] = term[:rows]
            send[:, columns] = term[rows:]

        @pl.when(core == 1)
        def _():
            keep[:, columns] = term[rows:]
            send[:, columns] = term[:rows]


def middle(info, weights, cot_own, cot_other, own, other):
    nodes, half = cot_own.shape
    whole = weights.shape[1]
    n_col = len(own)
    return pl.pallas_call(
        functools.partial(middle_kernel, n_col),
        out_shape=(
            jax.ShapeDtypeStruct((nodes, half), BF16),
            jax.ShapeDtypeStruct((nodes, half), BF16),
            jax.ShapeDtypeStruct((half // 2, whole), BF16),
            jax.ShapeDtypeStruct((half // 2, whole), BF16),
        ),
        in_specs=[smem()] + [vmem()] * (3 + 2 * n_col),
        out_specs=(vmem(),) * 4,
        compiler_params=params(),
        cost_estimate=pl.CostEstimate(
            flops=8 * nodes * half * whole, bytes_accessed=1024 * 1024, transcendentals=nodes * whole
        ),
        name="middle",
    )(info, weights, cot_own, cot_other, *own, *other)


def backward_kernel(n_col, a, *refs):
    pieces, out, turned = refs[:n_col], refs[n_col], refs[n_col + 1]

    @pl.when(pl.program_id(0) == 0)
    def _():
        for t in range(n_col):
            turned[t] = pieces[t][...].astype(F32).T.astype(BF16)

    total = jnp.dot(turned[0], a[0, 0], preferred_element_type=F32)
    for t in range(1, n_col):
        total = total + jnp.dot(turned[t], a[0, t], preferred_element_type=F32)
    out[0] = total.T.astype(BF16)


def backward(dense, parity, pieces):
    n_src, n_col, side, _ = dense.shape
    feats = pieces[0].shape[1]
    n_z = n_src // 2
    return pl.pallas_call(
        functools.partial(backward_kernel, n_col),
        grid=(n_z,),
        out_shape=jax.ShapeDtypeStruct((n_z, side, feats), BF16),
        in_specs=[pl.BlockSpec((1, n_col, side, side), lambda s: (2 * s + parity, 0, 0, 0))]
        + [vmem()] * n_col,
        out_specs=pl.BlockSpec((1, side, feats), lambda s: (s, 0, 0)),
        scratch_shapes=[pltpu.VMEM((n_col, feats, side), BF16)],
        compiler_params=params(),
        cost_estimate=pl.CostEstimate(
            flops=2 * n_z * n_col * side * side * feats,
            bytes_accessed=2 * n_z * n_col * side * side,
            transcendentals=0,
        ),
        name="backward",
    )(dense, *pieces)


def pair_kernel(own, arrived, *outs):
    for s, out in enumerate(outs):
        out[...] = (own[s].astype(F32) + arrived[s].astype(F32)).astype(BF16)


def pair_sums(own, arrived):
    n_z, side, feats = own.shape
    return pl.pallas_call(
        pair_kernel,
        out_shape=(jax.ShapeDtypeStruct((side, feats), BF16),) * n_z,
        in_specs=[vmem()] * 2,
        out_specs=(vmem(),) * n_z,
        compiler_params=params(),
        name="pair_sums",
    )(own, arrived)


def shards(features, tile_rows, tile_cols, tile_count, tile_values, weights, cotangent):
    tile = tile_values.shape[-1]
    n_row, n_col = lax.axis_size("row"), lax.axis_size("col")
    n_z = n_row // 2
    nodes, half = features.shape
    blocks = nodes // tile
    node_total = nodes * n_row * n_col
    r, c, f = lax.axis_index("row"), lax.axis_index("col"), lax.axis_index("feat")
    info = jnp.stack([r // 2, r % 2, c, f]).astype(jnp.int32)

    def sibling(v):
        return lax.ppermute(v, "row", [(i, i ^ 1) for i in range(n_row)])

    def along_z(v, s):
        return lax.ppermute(v, "row", [(i, (i + 2 * s) % n_row) for i in range(n_row)])

    def other_feat(v):
        return lax.ppermute(v, "feat", [(0, 1), (1, 0)])

    def to_group(v, shift, flip):
        pairs = []
        for cc in range(n_col):
            for ff in range(2):
                pairs.append((2 * cc + ff, 2 * ((cc + shift) % n_col) + (ff ^ flip)))
        return lax.ppermute(v, ("col", "feat"), pairs)

    same = [features] + [along_z(features, s) for s in range(1, n_z)]
    cross = [sibling(v) for v in same]
    cot_other = other_feat(cotangent)

    dense = densify(
        info, tile_rows, tile_cols, tile_count, tile_values[0, 0], n_z, n_col, blocks
    )
    total = None
    for s in range(n_z):
        total = forward(dense, s, same[s], cross[s], total)
    parts = total.astype(BF16).reshape(n_col, nodes, half)

    own = [parts[0]] + [to_group(parts[t], -t, 0) for t in range(1, n_col)]
    other = [to_group(parts[t], -t, 1) for t in range(n_col)]
    activated, spread, keep, send = middle(info, weights, cotangent, cot_other, own, other)

    term = (keep.astype(F32) + sibling(send).astype(F32)).astype(BF16)
    pieces = [spread] + [
        lax.ppermute(spread, "col", [(i, (i + t) % n_col) for i in range(n_col)])
        for t in range(1, n_col)
    ]
    gathered = [along_z(term, s) for s in range(1, n_z)]

    odd = backward(dense, 1, pieces)
    arrived = sibling(odd)
    even = backward(dense, 0, pieces)
    sums = pair_sums(even, arrived)
    back = sums[0].astype(F32)
    for s in range(1, n_z):
        back = back + along_z(sums[s], -s).astype(F32)

    grad = term.astype(F32)
    for v in gathered:
        grad = grad + v.astype(F32)
    grad = grad.astype(BF16)
    across = grad.astype(F32)
    for t in range(1, n_col):
        across = across + lax.ppermute(
            grad, "col", [(i, (i + t) % n_col) for i in range(n_col)]
        ).astype(F32)
    kept = across.astype(BF16)
    swapped = sibling(kept)
    lower = jnp.where(r % 2 == 0, kept, swapped)
    upper = jnp.where(r % 2 == 0, swapped, kept)
    weight_grad = jnp.concatenate([lower, upper], axis=0).astype(F32) * node_total ** (-0.5)
    return (activated, back.astype(BF16), weight_grad)


def solution(mesh):
    return jax.shard_map(
        shards,
        mesh=mesh,
        in_specs=(
            P(("col", "row"), "feat"),
            P("row", "col", None),
            P("row", "col", None),
            P("row", "col"),
            P("row", "col", None, None, None),
            P(),
            P(("row", "col"), "feat"),
        ),
        out_specs=(P(("row", "col"), "feat"), P(("col", "row"), "feat"), P("feat", None)),
        check_vma=False,
    )
```

```python
import functools

import jax
import jax.numpy as jnp
from jax import lax
from jax.experimental import pallas as pl
from jax.experimental.pallas import tpu as pltpu
from jax.sharding import PartitionSpec as P

F32 = jnp.float32
BF16 = jnp.bfloat16
MIB = 1024 * 1024


def params(mib=48):
    return pltpu.CompilerParams(vmem_limit_bytes=mib * MIB)


def vmem():
    return pl.BlockSpec(memory_space=pltpu.VMEM)


def smem():
    return pl.BlockSpec(memory_space=pltpu.SMEM)


def place_of(dims, info, block_row, block_col):
    n_z, n_col, blocks = dims
    z, core, c = info[0], info[1], info[2]
    source, owner = block_col // blocks, block_row // blocks
    j = 2 * (z ^ (source // 2)) + ((source + core) & 1)
    t = c - owner
    t = jnp.where(t < 0, t + n_col, t)
    return ((j * n_col + t) * blocks + block_row % blocks) * blocks + block_col % blocks


def densify_kernel(dims, groups, info, rows, cols, count, tiles, out, buffer, total, sems):
    n_z, n_col, blocks = dims
    slots, tile = buffer.shape[0], buffer.shape[1]
    per_group = slots // groups
    places = total.shape[0] - 1
    live = count[0, 0]

    def copy(g):
        part = pl.ds(g * per_group, per_group)
        return pltpu.make_async_copy(tiles.at[part], buffer.at[part], sems.at[g])

    def each_group(action):
        for g in range(groups):

            @pl.when(g * per_group < live)
            def _():
                action(g)

    each_group(lambda g: copy(g).start())

    def clear(i, carry):
        total[i] = jnp.zeros((tile, tile), F32)
        return carry

    lax.fori_loop(0, places, clear, 0, unroll=4)

    def add_group(g):
        copy(g).wait()

        def add(i, carry):
            slot = g * per_group + i
            place = place_of(dims, info, rows[0, 0, slot], cols[0, 0, slot])
            place = jnp.where(slot < live, place, places)
            total[place] += buffer[slot].astype(F32)
            return carry

        lax.fori_loop(0, per_group, add, 0, unroll=4)

    each_group(add_group)

    def settle(j, carry):
        for t in range(n_col):
            for a in range(blocks):
                for b in range(blocks):
                    value = total[((j * n_col + t) * blocks + a) * blocks + b]
                    out[j, t, a * tile : (a + 1) * tile, b * tile : (b + 1) * tile] = value.astype(BF16)
        return carry

    lax.fori_loop(0, 2 * n_z, settle, 0)


def densify(info, rows, cols, count, tiles, n_z, n_col, blocks):
    slots, tile = tiles.shape[0], tiles.shape[1]
    n_src = 2 * n_z
    groups = 8
    side = blocks * tile
    places = n_src * n_col * blocks * blocks
    return pl.pallas_call(
        functools.partial(densify_kernel, (n_z, n_col, blocks), groups),
        out_shape=pltpu.VMEM((n_src, n_col, side, side), BF16),
        in_specs=[smem(), smem(), smem(), smem(), pl.BlockSpec(memory_space=pl.ANY)],
        out_specs=vmem(),
        scratch_shapes=[
            pltpu.VMEM((slots, tile, tile), BF16),
            pltpu.VMEM((places + 1, tile, tile), F32),
            pltpu.SemaphoreType.DMA((groups,)),
        ],
        compiler_params=params(),
        cost_estimate=pl.CostEstimate(
            flops=0, bytes_accessed=24 * 1024 * 1024, transcendentals=0
        ),
        name="densify",
    )(info, rows, cols, count, tiles)


def resident(dense):
    return pltpu.with_memory_space_constraint(dense, pltpu.VMEM)


def hold(arrays, dense):
    n = len(arrays)
    outs = pl.pallas_call(
        lambda *refs: None,
        out_shape=tuple(jax.ShapeDtypeStruct(v.shape, v.dtype) for v in arrays),
        in_specs=[pl.BlockSpec(memory_space=pl.ANY)] * n + [vmem()],
        out_specs=(pl.BlockSpec(memory_space=pl.ANY),) * n,
        input_output_aliases={i: i for i in range(n)},
        compiler_params=params(1),
        name="hold",
    )(*arrays, resident(dense))
    return list(outs)


def forward_kernel(places, last, dense, *refs):
    n = len(places)
    xs, refs = refs[:n], refs[n:]
    n_col, side = dense.shape[1], dense.shape[2]
    outs = refs[-n_col:]
    for t in range(n_col):
        total = jnp.dot(dense[places[0], t], xs[0][...], preferred_element_type=F32)
        for j, x in zip(places[1:], xs[1:]):
            total = total + jnp.dot(dense[j, t], x[...], preferred_element_type=F32)
        if len(refs) > n_col:
            total = total + refs[t][...]
        outs[t][...] = total.astype(BF16) if last else total


def forward(dense, places, xs, totals, last):
    _, n_col, side, _ = dense.shape
    feats = xs[0].shape[1]
    shape = jax.ShapeDtypeStruct((side, feats), BF16 if last else F32)
    return pl.pallas_call(
        functools.partial(forward_kernel, places, last),
        out_shape=(shape,) * n_col,
        in_specs=[vmem()] * (1 + len(xs) + len(totals)),
        out_specs=(vmem(),) * n_col,
        compiler_params=params(24),
        cost_estimate=pl.CostEstimate(
            flops=2 * len(places) * n_col * side * side * feats,
            bytes_accessed=2 * len(places) * n_col * side * side,
            transcendentals=0,
        ),
        name="forward",
    )(resident(dense), *xs, *totals)


def backward_kernel(parity, dense, *refs):
    n_src, n_col = dense.shape[0], dense.shape[1]
    pieces, out = refs[:n_col], refs[n_col]
    turned = [piece[...].astype(F32).T.astype(BF16) for piece in pieces]
    for s in range(n_src // 2):
        total = jnp.dot(turned[0], dense[2 * s + parity, 0], preferred_element_type=F32)
        for t in range(1, n_col):
            total = total + jnp.dot(turned[t], dense[2 * s + parity, t], preferred_element_type=F32)
        out[s] = total.T.astype(BF16)


def backward(dense, parity, pieces):
    n_src, n_col, side, _ = dense.shape
    feats = pieces[0].shape[1]
    n_z = n_src // 2
    return pl.pallas_call(
        functools.partial(backward_kernel, parity),
        out_shape=jax.ShapeDtypeStruct((n_z, side, feats), BF16),
        in_specs=[vmem()] * (1 + n_col),
        out_specs=vmem(),
        compiler_params=params(24),
        cost_estimate=pl.CostEstimate(
            flops=2 * n_z * n_col * side * side * feats,
            bytes_accessed=2 * n_z * n_col * side * side,
            transcendentals=0,
        ),
        name="backward",
    )(resident(dense), *pieces)


def densify_stream_kernel(
    dims, info, rows, cols, count, tiles, out, buffer, head, following, sems
):
    n_z, n_col, blocks, slots, groups = dims
    chunk = pl.program_id(0)
    per_chunk = n_col * blocks * blocks
    per_group = slots // groups

    def copy(g):
        part = pl.ds(g * per_group, per_group)
        return pltpu.make_async_copy(tiles.at[part], buffer.at[part], sems.at[g])

    @pl.when(chunk == 0)
    def _():
        for g in range(groups):
            copy(g).start()

        def clear(i, carry):
            head[i] = slots
            return carry

        lax.fori_loop(0, 2 * n_z * per_chunk, clear, 0, unroll=8)
        following[slots] = slots
        buffer[slots] = jnp.zeros(buffer.shape[1:], buffer.dtype)

        def link(slot, carry):
            block_row, block_col = rows[0, 0, slot], cols[0, 0, slot]
            place = place_of((n_z, n_col, blocks), info, block_row, block_col)
            following[slot] = head[place]
            head[place] = slot
            return carry

        lax.fori_loop(0, count[0, 0], link, 0)
        for g in range(groups):
            copy(g).wait()

    tile = buffer.shape[1]

    def fill(i, carry):
        first = head[chunk * per_chunk + i]
        t = i // (blocks * blocks)
        a = pl.multiple_of((i // blocks) % blocks * tile, tile)
        b = pl.multiple_of(i % blocks * tile, tile)
        where = (0, t, pl.ds(a, tile), pl.ds(b, tile))
        out[where] = buffer[first]
        second = following[first]

        @pl.when(second != slots)
        def _():
            def more(state):
                slot, total = state
                return following[slot], total + buffer[slot].astype(F32)

            _, total = lax.while_loop(
                lambda state: state[0] != slots,
                more,
                (second, buffer[first].astype(F32)),
            )
            out[where] = total.astype(BF16)

        return carry

    lax.fori_loop(0, per_chunk, fill, 0)


def densify_stream(info, rows, cols, count, tiles, n_z, n_col, blocks):
    slots, tile = tiles.shape[0], tiles.shape[1]
    n_src = 2 * n_z
    groups = 8
    side = blocks * tile
    shape = (n_src, n_col, side, side)
    return pl.pallas_call(
        functools.partial(densify_stream_kernel, (n_z, n_col, blocks, slots, groups)),
        grid=(n_src,),
        out_shape=jax.ShapeDtypeStruct(shape, BF16),
        in_specs=[smem(), smem(), smem(), smem(), pl.BlockSpec(memory_space=pl.ANY)],
        out_specs=pl.BlockSpec((1, n_col, side, side), lambda j: (j, 0, 0, 0)),
        scratch_shapes=[
            pltpu.VMEM((slots + 1, tile, tile), BF16),
            pltpu.SMEM((n_src * n_col * blocks * blocks,), jnp.int32),
            pltpu.SMEM((slots + 1,), jnp.int32),
            pltpu.SemaphoreType.DMA((groups,)),
        ],
        compiler_params=params(),
        cost_estimate=pl.CostEstimate(
            flops=0, bytes_accessed=24 * 1024 * 1024, transcendentals=0
        ),
        name="densify",
    )(info, rows, cols, count, tiles)


def forward_stream_kernel(first, a, x0, x1, *rest):

    j = pl.program_id(1)

    @pl.when(j == 0)
    def _():
        value = jnp.dot(a[0, 0], x0[...], preferred_element_type=F32)
        if not first:
            value = value + rest[0][...]
        rest[-1][...] = value

    @pl.when(j == 1)
    def _():
        rest[-1][...] += jnp.dot(a[0, 0], x1[...], preferred_element_type=F32)


def forward_stream(dense, shift, x0, x1, total):
    _, n_col, side, _ = dense.shape
    feats = x0.shape[1]
    first = total is None
    block = pl.BlockSpec((side, feats), lambda t, j: (t, 0))
    return pl.pallas_call(
        functools.partial(forward_stream_kernel, first),
        grid=(n_col, 2),
        out_shape=jax.ShapeDtypeStruct((n_col * side, feats), F32),
        in_specs=[
            pl.BlockSpec((1, 1, side, side), lambda t, j: (2 * shift + j, t, 0, 0)),
            vmem(),
            vmem(),
        ]
        + ([] if first else [block]),
        out_specs=block,
        compiler_params=params(),
        cost_estimate=pl.CostEstimate(
            flops=4 * n_col * side * side * feats,
            bytes_accessed=4 * n_col * side * side,
            transcendentals=0,
        ),
        name="forward",
    )(dense, x0, x1, *([] if first else [total]))


def middle_kernel(n_col, info, weights, cot_own, cot_other, *refs):
    own = refs[:n_col]
    other = refs[n_col : 2 * n_col]
    activated, spread, keep, send = refs[2 * n_col :]
    half = cot_own.shape[1]
    core, f = info[1], info[3]
    mine = pl.ds(pl.multiple_of(f * half, half), half)
    theirs = pl.ds(pl.multiple_of((1 - f) * half, half), half)

    def gather(parts):
        total = parts[0][...].astype(F32)
        for part in parts[1:]:
            total = total + part[...].astype(F32)
        return total.astype(BF16)

    agg_own, agg_other = gather(own), gather(other)

    def hidden(columns):
        return jnp.dot(
            agg_own, weights[mine, columns], preferred_element_type=F32
        ) + jnp.dot(agg_other, weights[theirs, columns], preferred_element_type=F32)

    h = hidden(mine)
    decay = jnp.exp(jnp.minimum(h, 0.0))
    activated[...] = jnp.where(h > 0, h, decay - 1.0).astype(BF16)
    g_own = (cot_own[...].astype(F32) * decay).astype(BF16)
    h = hidden(theirs)
    decay = jnp.exp(jnp.minimum(h, 0.0))
    g_other = (cot_other[...].astype(F32) * decay).astype(BF16)
    across = (((1,), (1,)), ((), ()))
    spread[...] = (
        lax.dot_general(g_own, weights[mine, mine], across, preferred_element_type=F32)
        + lax.dot_general(g_other, weights[mine, theirs], across, preferred_element_type=F32)
    ).astype(BF16)
    down = (((0,), (0,)), ((), ()))
    rows = half // 2
    for columns, g in ((mine, g_own), (theirs, g_other)):
        term = lax.dot_general(agg_own, g, down, preferred_element_type=F32).astype(BF16)

        @pl.when(core == 0)
        def _():
            keep[:, columns] = term[:rows]
            send[:, columns] = term[rows:]

        @pl.when(core == 1)
        def _():
            keep[:, columns] = term[rows:]
            send[:, columns] = term[:rows]


def middle(info, weights, cot_own, cot_other, own, other):
    nodes, half = cot_own.shape
    whole = weights.shape[1]
    n_col = len(own)
    return pl.pallas_call(
        functools.partial(middle_kernel, n_col),
        out_shape=(
            jax.ShapeDtypeStruct((nodes, half), BF16),
            jax.ShapeDtypeStruct((nodes, half), BF16),
            jax.ShapeDtypeStruct((half // 2, whole), BF16),
            jax.ShapeDtypeStruct((half // 2, whole), BF16),
        ),
        in_specs=[smem()] + [vmem()] * (3 + 2 * n_col),
        out_specs=(vmem(),) * 4,
        compiler_params=params(),
        cost_estimate=pl.CostEstimate(
            flops=8 * nodes * half * whole, bytes_accessed=1024 * 1024, transcendentals=nodes * whole
        ),
        name="middle",
    )(info, weights, cot_own, cot_other, *own, *other)


def backward_stream_kernel(n_col, a, *refs):
    pieces, out, turned = refs[:n_col], refs[n_col], refs[n_col + 1]

    @pl.when(pl.program_id(0) == 0)
    def _():
        for t in range(n_col):
            turned[t] = pieces[t][...].astype(F32).T.astype(BF16)

    total = jnp.dot(turned[0], a[0, 0], preferred_element_type=F32)
    for t in range(1, n_col):
        total = total + jnp.dot(turned[t], a[0, t], preferred_element_type=F32)
    out[0] = total.T.astype(BF16)


def backward_stream(dense, parity, pieces):
    n_src, n_col, side, _ = dense.shape
    feats = pieces[0].shape[1]
    n_z = n_src // 2
    return pl.pallas_call(
        functools.partial(backward_stream_kernel, n_col),
        grid=(n_z,),
        out_shape=jax.ShapeDtypeStruct((n_z, side, feats), BF16),
        in_specs=[pl.BlockSpec((1, n_col, side, side), lambda s: (2 * s + parity, 0, 0, 0))]
        + [vmem()] * n_col,
        out_specs=pl.BlockSpec((1, side, feats), lambda s: (s, 0, 0)),
        scratch_shapes=[pltpu.VMEM((n_col, feats, side), BF16)],
        compiler_params=params(),
        cost_estimate=pl.CostEstimate(
            flops=2 * n_z * n_col * side * side * feats,
            bytes_accessed=2 * n_z * n_col * side * side,
            transcendentals=0,
        ),
        name="backward",
    )(dense, *pieces)


def pair_kernel(own, arrived, *outs):
    for s, out in enumerate(outs):
        out[...] = (own[s].astype(F32) + arrived[s].astype(F32)).astype(BF16)


def pair_sums(own, arrived):
    n_z, side, feats = own.shape
    return pl.pallas_call(
        pair_kernel,
        out_shape=(jax.ShapeDtypeStruct((side, feats), BF16),) * n_z,
        in_specs=[vmem()] * 2,
        out_specs=(vmem(),) * n_z,
        compiler_params=params(),
        name="pair_sums",
    )(own, arrived)


def shards(features, tile_rows, tile_cols, tile_count, tile_values, weights, cotangent):
    tile = tile_values.shape[-1]
    n_row, n_col = lax.axis_size("row"), lax.axis_size("col")
    n_z = n_row // 2
    nodes, half = features.shape
    blocks = nodes // tile
    node_total = nodes * n_row * n_col
    r, c, f = lax.axis_index("row"), lax.axis_index("col"), lax.axis_index("feat")
    info = jnp.stack([r // 2, r % 2, c, f]).astype(jnp.int32)

    def sibling(v):
        return lax.ppermute(v, "row", [(i, i ^ 1) for i in range(n_row)])

    def along_z(v, s):
        return lax.ppermute(v, "row", [(i, i ^ (2 * s)) for i in range(n_row)])

    def other_feat(v):
        return lax.ppermute(v, "feat", [(0, 1), (1, 0)])

    def to_group(v, shift, flip):
        pairs = []
        for cc in range(n_col):
            for ff in range(2):
                pairs.append((2 * cc + ff, 2 * ((cc + shift) % n_col) + (ff ^ flip)))
        return lax.ppermute(v, ("col", "feat"), pairs)

    same = [features] + [along_z(features, s) for s in range(1, n_z)]
    cot_other = other_feat(cotangent)
    tiles = tile_values[0, 0]
    cell = (info, tile_rows, tile_cols, tile_count, tiles, n_z, n_col, blocks)
    if 2 * n_z * n_col * (blocks * tile) ** 2 <= 8 * MIB:
        dense = densify(*cell)
        same = [features] + hold(same[1:], dense)
        cross = [sibling(v) for v in same]
        near, far = range(0, n_z // 2), range(n_z // 2, n_z)
        totals = forward(
            dense,
            [2 * s + k for s in near for k in range(2)],
            [v for s in near for v in (same[s], cross[s])],
            (),
            False,
        )
        totals = forward(dense, [2 * s for s in far], [same[s] for s in far], totals, False)
        parts = forward(dense, [2 * s + 1 for s in far], [cross[s] for s in far], totals, True)
        back_of = backward
    else:
        cross = [sibling(v) for v in same]
        dense = densify_stream(*cell)
        total = None
        for s in range(n_z):
            total = forward_stream(dense, s, same[s], cross[s], total)
        parts = total.astype(BF16).reshape(n_col, nodes, half)
        back_of = backward_stream

    own = [parts[0]] + [to_group(parts[t], -t, 0) for t in range(1, n_col)]
    other = [to_group(parts[t], -t, 1) for t in range(n_col)]
    activated, spread, keep, send = middle(info, weights, cotangent, cot_other, own, other)

    term = (keep.astype(F32) + sibling(send).astype(F32)).astype(BF16)
    pieces = [spread] + [
        lax.ppermute(spread, "col", [(i, (i + t) % n_col) for i in range(n_col)])
        for t in range(1, n_col)
    ]
    gathered = [along_z(term, s) for s in range(1, n_z)]

    odd = back_of(dense, 1, pieces)
    arrived = sibling(odd)
    even = back_of(dense, 0, pieces)
    sums = pair_sums(even, arrived)
    back = sums[0].astype(F32)
    for s in range(1, n_z):
        back = back + along_z(sums[s], s).astype(F32)

    grad = term.astype(F32)
    for v in gathered:
        grad = grad + v.astype(F32)
    grad = grad.astype(BF16)
    across = grad.astype(F32)
    for t in range(1, n_col):
        across = across + lax.ppermute(
            grad, "col", [(i, (i + t) % n_col) for i in range(n_col)]
        ).astype(F32)
    kept = across.astype(BF16)
    swapped = sibling(kept)
    lower = jnp.where(r % 2 == 0, kept, swapped)
    upper = jnp.where(r % 2 == 0, swapped, kept)
    weight_grad = jnp.concatenate([lower, upper], axis=0).astype(F32) * node_total ** (-0.5)
    return (activated, back.astype(BF16), weight_grad)


def solution(mesh):
    return jax.shard_map(
        shards,
        mesh=mesh,
        in_specs=(
            P(("col", "row"), "feat"),
            P("row", "col", None),
            P("row", "col", None),
            P("row", "col"),
            P("row", "col", None, None, None),
            P(),
            P(("row", "col"), "feat"),
        ),
        out_specs=(P(("row", "col"), "feat"), P(("col", "row"), "feat"), P("feat", None)),
        check_vma=False,
    )
```

```python
import functools

import jax
import jax.numpy as jnp
from jax import lax
from jax.experimental import pallas as pl
from jax.experimental.pallas import tpu as pltpu
from jax.sharding import PartitionSpec as P

F32 = jnp.float32
BF16 = jnp.bfloat16
MIB = 1024 * 1024
COST = pl.CostEstimate(flops=1, bytes_accessed=1, transcendentals=0)


def params(mib=16):
    return pltpu.CompilerParams(vmem_limit_bytes=mib * MIB)


def vmem():
    return pl.BlockSpec(memory_space=pltpu.VMEM)


def smem():
    return pl.BlockSpec(memory_space=pltpu.SMEM)


def place_of(dims, block_row, block_col):
    n_z, n_col, blocks = dims
    r, c = lax.axis_index("row"), lax.axis_index("col")
    z, core = r // 2, r % 2
    source, owner = block_col // blocks, block_row // blocks
    j = 2 * (z ^ (source // 2)) + ((source + core) & 1)
    t = c - owner
    t = jnp.where(t < 0, t + n_col, t)
    return ((j * n_col + t) * blocks + block_row % blocks) * blocks + block_col % blocks


def densify_kernel(dims, groups, rows, cols, count, tiles, out, buffer, total, sems):
    n_z, n_col, blocks = dims
    slots, tile = buffer.shape[0], buffer.shape[1]
    per_group = slots // groups
    places = total.shape[0] - 1
    live = count[0, 0]

    def copy(g):
        part = pl.ds(g * per_group, per_group)
        return pltpu.make_async_copy(tiles.at[part], buffer.at[part], sems.at[g])

    def each_group(action):
        for g in range(groups):

            @pl.when(g * per_group < live)
            def _():
                action(g)

    each_group(lambda g: copy(g).start())

    def clear(i, carry):
        total[i] = jnp.zeros((tile, tile), F32)
        return carry

    lax.fori_loop(0, places, clear, 0, unroll=4)

    def add_group(g):
        copy(g).wait()

        def add(i, carry):
            slot = g * per_group + i
            place = place_of(dims, rows[0, 0, slot], cols[0, 0, slot])
            place = jnp.where(slot < live, place, places)
            total[place] += buffer[slot].astype(F32)
            return carry

        lax.fori_loop(0, per_group, add, 0, unroll=4)

    each_group(add_group)

    def settle(j, carry):
        for t in range(n_col):
            for a in range(blocks):
                for b in range(blocks):
                    value = total[((j * n_col + t) * blocks + a) * blocks + b]
                    out[j, t, a * tile : (a + 1) * tile, b * tile : (b + 1) * tile] = value.astype(BF16)
        return carry

    lax.fori_loop(0, 2 * n_z, settle, 0)


def densify(rows, cols, count, tiles, n_z, n_col, blocks):
    slots, tile = tiles.shape[0], tiles.shape[1]
    n_src = 2 * n_z
    groups = 8
    side = blocks * tile
    places = n_src * n_col * blocks * blocks
    return pl.pallas_call(
        functools.partial(densify_kernel, (n_z, n_col, blocks), groups),
        out_shape=pltpu.VMEM((n_src, n_col, side, side), BF16),
        in_specs=[smem(), smem(), smem(), pl.BlockSpec(memory_space=pltpu.HBM)],
        out_specs=vmem(),
        scratch_shapes=[
            pltpu.VMEM((slots, tile, tile), BF16),
            pltpu.VMEM((places + 1, tile, tile), F32),
            pltpu.SemaphoreType.DMA((groups,)),
        ],
        compiler_params=params(32),
        cost_estimate=COST,
        name="densify",
    )(in_hbm(rows), in_hbm(cols), count, in_hbm(tiles))


def in_hbm(v):
    return pltpu.with_memory_space_constraint(v, pltpu.HBM)


def resident(dense):
    return pltpu.with_memory_space_constraint(dense, pltpu.VMEM)


def hold(arrays, after):
    n = len(arrays)
    outs = pl.pallas_call(
        lambda *refs: None,
        out_shape=tuple(jax.ShapeDtypeStruct(v.shape, v.dtype) for v in arrays),
        in_specs=[pl.BlockSpec(memory_space=pl.ANY)] * n + [vmem()],
        out_specs=(pl.BlockSpec(memory_space=pl.ANY),) * n,
        input_output_aliases={i: i for i in range(n)},
        compiler_params=params(),
        cost_estimate=COST,
        name="hold",
    )(*arrays, resident(after))
    return list(outs)


def forward_kernel(places, last, dense, *refs):
    n = len(places)
    xs, refs = refs[:n], refs[n:]
    n_col, side = dense.shape[1], dense.shape[2]
    outs = refs[-n_col:]
    for t in range(n_col):
        total = jnp.dot(dense[places[0], t], xs[0][...], preferred_element_type=F32)
        for j, x in zip(places[1:], xs[1:]):
            total = total + jnp.dot(dense[j, t], x[...], preferred_element_type=F32)
        if len(refs) > n_col:
            total = total + refs[t][...]
        outs[t][...] = total.astype(BF16) if last else total


def forward(dense, places, xs, totals, last):
    _, n_col, side, _ = dense.shape
    feats = xs[0].shape[1]
    shape = jax.ShapeDtypeStruct((side, feats), BF16 if last else F32)
    return pl.pallas_call(
        functools.partial(forward_kernel, places, last),
        out_shape=(shape,) * n_col,
        in_specs=[vmem()] * (1 + len(xs) + len(totals)),
        out_specs=(vmem(),) * n_col,
        compiler_params=params(),
        cost_estimate=COST,
        name="forward",
    )(resident(dense), *xs, *totals)


def backward_kernel(dense, *refs):
    n_src, n_col = dense.shape[0], dense.shape[1]
    pieces, outs = refs[:n_col], refs[-2:]
    turned = [piece[...].astype(F32).T.astype(BF16) for piece in pieces]
    for j in range(n_src):
        total = jnp.dot(turned[0], dense[j, 0], preferred_element_type=F32)
        for t in range(1, n_col):
            total = total + jnp.dot(turned[t], dense[j, t], preferred_element_type=F32)
        outs[j % 2][j // 2] = total.T.astype(BF16)


def backward(dense, pieces, after):
    n_src, n_col, side, _ = dense.shape
    feats = pieces[0].shape[1]
    return pl.pallas_call(
        backward_kernel,
        out_shape=(jax.ShapeDtypeStruct((n_src // 2, side, feats), BF16),) * 2,
        in_specs=[vmem()] * (1 + n_col) + [pl.BlockSpec(memory_space=pl.ANY)],
        out_specs=(vmem(),) * 2,
        compiler_params=params(),
        cost_estimate=COST,
        name="backward",
    )(resident(dense), *pieces, after)


def densify_stream_kernel(
    dims, rows, cols, count, tiles, out, buffer, head, following, sems
):
    n_z, n_col, blocks, slots, groups = dims
    chunk = pl.program_id(0)
    per_chunk = n_col * blocks * blocks
    per_group = slots // groups

    def copy(g):
        part = pl.ds(g * per_group, per_group)
        return pltpu.make_async_copy(tiles.at[part], buffer.at[part], sems.at[g])

    @pl.when(chunk == 0)
    def _():
        for g in range(groups):
            copy(g).start()

        def clear(i, carry):
            head[i] = slots
            return carry

        lax.fori_loop(0, 2 * n_z * per_chunk, clear, 0, unroll=8)
        following[slots] = slots
        buffer[slots] = jnp.zeros(buffer.shape[1:], buffer.dtype)

        def link(slot, carry):
            block_row, block_col = rows[0, 0, slot], cols[0, 0, slot]
            place = place_of((n_z, n_col, blocks), block_row, block_col)
            following[slot] = head[place]
            head[place] = slot
            return carry

        lax.fori_loop(0, count[0, 0], link, 0)
        for g in range(groups):
            copy(g).wait()

    tile = buffer.shape[1]

    def fill(i, carry):
        first = head[chunk * per_chunk + i]
        t = i // (blocks * blocks)
        a = pl.multiple_of((i // blocks) % blocks * tile, tile)
        b = pl.multiple_of(i % blocks * tile, tile)
        where = (0, t, pl.ds(a, tile), pl.ds(b, tile))
        out[where] = buffer[first]
        second = following[first]

        @pl.when(second != slots)
        def _():
            def more(state):
                slot, total = state
                return following[slot], total + buffer[slot].astype(F32)

            _, total = lax.while_loop(
                lambda state: state[0] != slots,
                more,
                (second, buffer[first].astype(F32)),
            )
            out[where] = total.astype(BF16)

        return carry

    lax.fori_loop(0, per_chunk, fill, 0)


def densify_stream(rows, cols, count, tiles, n_z, n_col, blocks):
    slots, tile = tiles.shape[0], tiles.shape[1]
    n_src = 2 * n_z
    groups = 8
    side = blocks * tile
    shape = (n_src, n_col, side, side)
    return pl.pallas_call(
        functools.partial(densify_stream_kernel, (n_z, n_col, blocks, slots, groups)),
        grid=(n_src,),
        out_shape=jax.ShapeDtypeStruct(shape, BF16),
        in_specs=[smem(), smem(), smem(), pl.BlockSpec(memory_space=pltpu.HBM)],
        out_specs=pl.BlockSpec((1, n_col, side, side), lambda j: (j, 0, 0, 0)),
        scratch_shapes=[
            pltpu.VMEM((slots + 1, tile, tile), BF16),
            pltpu.SMEM((n_src * n_col * blocks * blocks,), jnp.int32),
            pltpu.SMEM((slots + 1,), jnp.int32),
            pltpu.SemaphoreType.DMA((groups,)),
        ],
        compiler_params=params(32),
        cost_estimate=COST,
        name="densify",
    )(rows, cols, count, tiles)


def forward_stream_kernel(first, a, x0, x1, *rest):

    j = pl.program_id(1)

    @pl.when(j == 0)
    def _():
        value = jnp.dot(a[0, 0], x0[...], preferred_element_type=F32)
        if not first:
            value = value + rest[0][...]
        rest[-1][...] = value

    @pl.when(j == 1)
    def _():
        rest[-1][...] += jnp.dot(a[0, 0], x1[...], preferred_element_type=F32)


def forward_stream(dense, shift, x0, x1, total):
    _, n_col, side, _ = dense.shape
    feats = x0.shape[1]
    first = total is None
    block = pl.BlockSpec((side, feats), lambda t, j: (t, 0))
    return pl.pallas_call(
        functools.partial(forward_stream_kernel, first),
        grid=(n_col, 2),
        out_shape=jax.ShapeDtypeStruct((n_col * side, feats), F32),
        in_specs=[
            pl.BlockSpec((1, 1, side, side), lambda t, j: (2 * shift + j, t, 0, 0)),
            vmem(),
            vmem(),
        ]
        + ([] if first else [block]),
        out_specs=block,
        compiler_params=params(32),
        cost_estimate=COST,
        name="forward",
    )(dense, x0, x1, *([] if first else [total]))


def middle_kernel(n_col, weights, cot_own, cot_other, *refs):
    own = refs[:n_col]
    other = refs[n_col : 2 * n_col]
    spread, activated, agg, g_own, g_other = refs[2 * n_col :]
    half = cot_own.shape[1]
    f = lax.axis_index("feat")
    mine = pl.ds(pl.multiple_of(f * half, half), half)
    theirs = pl.ds(pl.multiple_of((1 - f) * half, half), half)

    def gather(parts):
        total = parts[0][...].astype(F32)
        for part in parts[1:]:
            total = total + part[...].astype(F32)
        return total.astype(BF16)

    top = jnp.concatenate([weights[mine, mine], weights[mine, theirs]], axis=1)
    low = jnp.concatenate([weights[theirs, mine], weights[theirs, theirs]], axis=1)
    agg_own = gather(own)
    agg[...] = agg_own
    both = jnp.concatenate([agg_own, gather(other)], axis=1)
    hidden = jnp.dot(both, jnp.concatenate([top, low], axis=0), preferred_element_type=F32)
    decay = jnp.exp(jnp.minimum(hidden, 0.0))
    cot = jnp.concatenate([cot_own[...], cot_other[...]], axis=1).astype(F32)
    g = (cot * decay).astype(BF16)
    spread[...] = lax.dot_general(
        g, top, (((1,), (1,)), ((), ())), preferred_element_type=F32
    ).astype(BF16)
    g_own[...] = g[:, :half]
    g_other[...] = g[:, half:]
    activated[...] = jnp.where(
        hidden[:, :half] > 0, hidden[:, :half], decay[:, :half] - 1.0
    ).astype(BF16)


def middle(weights, cot_own, cot_other, own, other):
    nodes, half = cot_own.shape
    whole = weights.shape[1]
    n_col = len(own)
    return pl.pallas_call(
        functools.partial(middle_kernel, n_col),
        out_shape=(jax.ShapeDtypeStruct((nodes, half), BF16),) * 5,
        in_specs=[vmem()] * (3 + 2 * n_col),
        out_specs=(vmem(),) * 5,
        compiler_params=params(),
        cost_estimate=COST,
        name="middle",
    )(weights, cot_own, cot_other, *own, *other)


def weight_kernel(agg, g_own, g_other, out):
    half = agg.shape[1]
    f = lax.axis_index("feat")
    turned = agg[...].astype(F32).T.astype(BF16)
    for columns, g in ((f * half, g_own), ((1 - f) * half, g_other)):
        columns = pl.ds(pl.multiple_of(columns, half), half)
        out[:, columns] = jnp.dot(turned, g[...], preferred_element_type=F32).astype(BF16)


def weight_term(agg, g_own, g_other):
    half = agg.shape[1]
    return pl.pallas_call(
        weight_kernel,
        out_shape=jax.ShapeDtypeStruct((half, 2 * half), BF16),
        in_specs=[vmem()] * 3,
        out_specs=vmem(),
        compiler_params=params(),
        cost_estimate=COST,
        name="weight_term",
    )(agg, g_own, g_other)


def backward_stream_kernel(n_col, a, *refs):
    pieces, out, turned = refs[:n_col], refs[-2], refs[-1]

    @pl.when(pl.program_id(0) == 0)
    def _():
        for t in range(n_col):
            turned[t] = pieces[t][...].astype(F32).T.astype(BF16)

    total = jnp.dot(turned[0], a[0, 0], preferred_element_type=F32)
    for t in range(1, n_col):
        total = total + jnp.dot(turned[t], a[0, t], preferred_element_type=F32)
    out[0] = total.T.astype(BF16)


def backward_stream(dense, parity, pieces, after):
    n_src, n_col, side, _ = dense.shape
    feats = pieces[0].shape[1]
    n_z = n_src // 2
    return pl.pallas_call(
        functools.partial(backward_stream_kernel, n_col),
        grid=(n_z,),
        out_shape=jax.ShapeDtypeStruct((n_z, side, feats), BF16),
        in_specs=[pl.BlockSpec((1, n_col, side, side), lambda s: (2 * s + parity, 0, 0, 0))]
        + [vmem()] * n_col
        + [pl.BlockSpec(memory_space=pl.ANY)],
        out_specs=pl.BlockSpec((1, side, feats), lambda s: (s, 0, 0)),
        scratch_shapes=[pltpu.VMEM((n_col, feats, side), BF16)],
        compiler_params=params(32),
        cost_estimate=COST,
        name="backward",
    )(dense, *pieces, after)


def add_kernel(a, b, *rest):
    rest[-1][...] = (a[...].astype(F32) + b[...].astype(F32)).astype(BF16)


def add(a, b, *after):
    return pl.pallas_call(
        add_kernel,
        out_shape=jax.ShapeDtypeStruct(a.shape, BF16),
        in_specs=[vmem()] * 2 + [pl.BlockSpec(memory_space=pl.ANY)] * len(after),
        out_specs=vmem(),
        compiler_params=params(),
        cost_estimate=COST,
        name="add",
    )(a, b, *after)


def pair_kernel(own, arrived, *outs):
    for s, out in enumerate(outs):
        out[...] = (own[s].astype(F32) + arrived[s].astype(F32)).astype(BF16)


def pair_sums(own, arrived):
    n_z, side, feats = own.shape
    return pl.pallas_call(
        pair_kernel,
        out_shape=(jax.ShapeDtypeStruct((side, feats), BF16),) * n_z,
        in_specs=[vmem()] * 2,
        out_specs=(vmem(),) * n_z,
        compiler_params=params(),
        cost_estimate=COST,
        name="pair_sums",
    )(own, arrived)


def shards(features, tile_rows, tile_cols, tile_count, tile_values, weights, cotangent):
    tile = tile_values.shape[-1]
    n_row, n_col = lax.axis_size("row"), lax.axis_size("col")
    n_z = n_row // 2
    nodes, half = features.shape
    blocks = nodes // tile
    node_total = nodes * n_row * n_col
    def sibling(v):
        return lax.ppermute(v, "row", [(i, i ^ 1) for i in range(n_row)])

    def along_z(v, s):
        return lax.ppermute(v, "row", [(i, i ^ (2 * s)) for i in range(n_row)])

    def other_feat(v):
        return lax.ppermute(v, "feat", [(0, 1), (1, 0)])

    def to_group(v, shift, flip):
        pairs = []
        for cc in range(n_col):
            for ff in range(2):
                pairs.append((2 * cc + ff, 2 * ((cc + shift) % n_col) + (ff ^ flip)))
        return lax.ppermute(v, ("col", "feat"), pairs)

    same = [features] + [along_z(features, s) for s in range(1, n_z)]
    cot_other = other_feat(cotangent)
    tiles = tile_values[0, 0]
    cell = (tile_rows, tile_cols, tile_count, tiles, n_z, n_col, blocks)
    if 2 * n_z * n_col * (blocks * tile) ** 2 <= 8 * MIB:
        dense = densify(*cell)
        totals = forward(dense, [0, 1], [features, sibling(features)], (), False)
        *same, cot_other = hold(same[1:] + [cot_other], totals[0])
        cross = [sibling(v) for v in same]
        totals = forward(dense, [2 * s for s in range(1, n_z)], same, totals, False)
        parts = forward(dense, [2 * s + 1 for s in range(1, n_z)], cross, totals, True)
        back_of = backward
    else:
        cross = [sibling(v) for v in same]
        dense = densify_stream(*cell)
        total = None
        for s in range(n_z):
            total = forward_stream(dense, s, same[s], cross[s], total)
        parts = total.astype(BF16).reshape(n_col, nodes, half)

        def back_of(*operands):
            return [backward_stream(operands[0], k, *operands[1:]) for k in range(2)]

    own = [parts[0]] + [to_group(parts[t], -t, 0) for t in range(1, n_col)]
    other = [to_group(parts[t], -t, 1) for t in range(n_col)]
    spread, activated, *rest = middle(weights, cotangent, cot_other, own, other)
    pieces = [spread] + [
        lax.ppermute(spread, "col", [(i, (i + t) % n_col) for i in range(n_col)])
        for t in range(1, n_col)
    ]
    term = weight_term(*rest)
    term = add(term, along_z(term, 1))

    even, odd = back_of(dense, pieces, term)
    arrived = sibling(odd)
    sums = pair_sums(even, arrived)
    if n_z > 2:
        term = add(term, along_z(term, 2), sums[0])
    back = sums[0].astype(F32)
    for s in range(1, n_z):
        back = back + along_z(sums[s], s).astype(F32)

    def finish(_, v):
        for step in range(2, n_z.bit_length() - 1):
            v = add(v, along_z(v, 1 << step))
        total = v.astype(F32)
        for t in range(1, n_col):
            total = total + lax.ppermute(
                v, "col", [(i, (i + t) % n_col) for i in range(n_col)]
            ).astype(F32)
        v = total.astype(BF16)
        return add(v, sibling(v))

    once = lax.optimization_barrier(jnp.int32(1))
    whole = lax.fori_loop(0, once, finish, term)
    weight_grad = whole.astype(F32) * node_total ** (-0.5)
    return (activated, back.astype(BF16), weight_grad)


def solution(mesh):
    return jax.shard_map(
        shards,
        mesh=mesh,
        in_specs=(
            P(("col", "row"), "feat"),
            P("row", "col", None),
            P("row", "col", None),
            P("row", "col"),
            P("row", "col", None, None, None),
            P(),
            P(("row", "col"), "feat"),
        ),
        out_specs=(P(("row", "col"), "feat"), P(("col", "row"), "feat"), P("feat", None)),
        check_vma=False,
    )
```

```python
import functools

import jax
import jax.numpy as jnp
from jax import lax
from jax.experimental import pallas as pl
from jax.experimental.pallas import tpu as pltpu
from jax.sharding import PartitionSpec as P

F32 = jnp.float32
BF16 = jnp.bfloat16
MIB = 1024 * 1024
COST = pl.CostEstimate(flops=1, bytes_accessed=1, transcendentals=0)


def params(mib=16):
    return pltpu.CompilerParams(vmem_limit_bytes=mib * MIB)


def vmem():
    return pl.BlockSpec(memory_space=pltpu.VMEM)


def smem():
    return pl.BlockSpec(memory_space=pltpu.SMEM)


def place_of(dims, block_row, block_col):
    n_z, n_col, blocks = dims
    bits, low = blocks.bit_length() - 1, blocks - 1
    j = (block_col >> bits) ^ lax.axis_index("row")
    t = (lax.axis_index("col") - (block_row >> bits)) & (n_col - 1)
    return ((((j * n_col + t) << bits) | (block_row & low)) << bits) | (block_col & low)


def densify_kernel(dims, groups, rows, cols, count, tiles, out, buffer, total, sems):
    n_z, n_col, blocks = dims
    slots, tile = buffer.shape[0], buffer.shape[1]
    per_group = slots // groups
    places = total.shape[0] - 1
    live = count[0, 0]

    def copy(g):
        part = pl.ds(g * per_group, per_group)
        return pltpu.make_async_copy(tiles.at[part], buffer.at[part], sems.at[g])

    def each_group(action):
        for g in range(groups):

            @pl.when(g * per_group < live)
            def _():
                action(g)

    each_group(lambda g: copy(g).start())

    def clear(i, carry):
        total[i] = jnp.zeros((tile, tile), F32)
        return carry

    lax.fori_loop(0, places, clear, 0, unroll=4)

    def add_group(g):
        copy(g).wait()

        def add(i, carry):
            slot = g * per_group + i
            place = place_of(dims, rows[0, 0, slot], cols[0, 0, slot])
            place = jnp.where(slot < live, place, places)
            total[place] += buffer[slot].astype(F32)
            return carry

        lax.fori_loop(0, per_group, add, 0, unroll=8)

    each_group(add_group)

    def settle(j, carry):
        for t in range(n_col):
            for a in range(blocks):
                for b in range(blocks):
                    value = total[((j * n_col + t) * blocks + a) * blocks + b]
                    out[j, t, a * tile : (a + 1) * tile, b * tile : (b + 1) * tile] = value.astype(BF16)
        return carry

    lax.fori_loop(0, 2 * n_z, settle, 0)


def densify(rows, cols, count, tiles, n_z, n_col, blocks):
    slots, tile = tiles.shape[0], tiles.shape[1]
    n_src = 2 * n_z
    groups = 8
    side = blocks * tile
    places = n_src * n_col * blocks * blocks
    return pl.pallas_call(
        functools.partial(densify_kernel, (n_z, n_col, blocks), groups),
        out_shape=pltpu.VMEM((n_src, n_col, side, side), BF16),
        in_specs=[smem(), smem(), smem(), pl.BlockSpec(memory_space=pltpu.HBM)],
        out_specs=vmem(),
        scratch_shapes=[
            pltpu.VMEM((slots, tile, tile), BF16),
            pltpu.VMEM((places + 1, tile, tile), F32),
            pltpu.SemaphoreType.DMA((groups,)),
        ],
        compiler_params=params(32),
        cost_estimate=COST,
        name="densify",
    )(in_hbm(rows), in_hbm(cols), count, in_hbm(tiles))


def in_hbm(v):
    return pltpu.with_memory_space_constraint(v, pltpu.HBM)


def resident(dense):
    return pltpu.with_memory_space_constraint(dense, pltpu.VMEM)


def hold(arrays, after):
    n = len(arrays)
    outs = pl.pallas_call(
        lambda *refs: None,
        out_shape=tuple(jax.ShapeDtypeStruct(v.shape, v.dtype) for v in arrays),
        in_specs=[pl.BlockSpec(memory_space=pl.ANY)] * n + [vmem()],
        out_specs=(pl.BlockSpec(memory_space=pl.ANY),) * n,
        input_output_aliases={i: i for i in range(n)},
        compiler_params=params(),
        cost_estimate=COST,
        name="hold",
    )(*arrays, resident(after))
    return list(outs)


def forward_kernel(places, last, dense, *refs):
    n = len(places)
    xs, refs = refs[:n], refs[n:]
    n_col, side = dense.shape[1], dense.shape[2]
    outs = refs[-n_col:]
    for t in range(n_col):
        total = jnp.dot(dense[places[0], t], xs[0][...], preferred_element_type=F32)
        for j, x in zip(places[1:], xs[1:]):
            total = total + jnp.dot(dense[j, t], x[...], preferred_element_type=F32)
        if len(refs) > n_col:
            total = total + refs[t][...]
        outs[t][...] = total.astype(BF16) if last else total


def forward(dense, places, xs, totals, last):
    _, n_col, side, _ = dense.shape
    feats = xs[0].shape[1]
    shape = jax.ShapeDtypeStruct((side, feats), BF16 if last else F32)
    return pl.pallas_call(
        functools.partial(forward_kernel, places, last),
        out_shape=(shape,) * n_col,
        in_specs=[vmem()] * (1 + len(xs) + len(totals)),
        out_specs=(vmem(),) * n_col,
        compiler_params=params(),
        cost_estimate=COST,
        name="forward",
    )(resident(dense), *xs, *totals)


def own_kernel(dense, piece, out):
    for j in range(dense.shape[0]):
        out[j] = jnp.dot(piece[...], dense[j, 0], preferred_element_type=F32)


def backward_own(dense, piece):
    n_src, _, side, _ = dense.shape
    return pl.pallas_call(
        own_kernel,
        out_shape=pltpu.VMEM((n_src, piece.shape[0], side), F32),
        in_specs=[vmem()] * 2,
        out_specs=vmem(),
        compiler_params=params(),
        cost_estimate=COST,
        name="backward_own",
    )(resident(dense), piece)


def backward_kernel(dense, own, *refs):
    pieces, outs = refs[: dense.shape[1] - 1], refs[-2:]
    for j in range(dense.shape[0]):
        total = own[j]
        for t, piece in enumerate(pieces):
            total = total + jnp.dot(piece[...], dense[j, t + 1], preferred_element_type=F32)
        outs[j % 2][j // 2] = total.astype(BF16)


def backward(dense, own, pieces, after):
    n_src, n_col, side, _ = dense.shape
    feats = own.shape[1]
    return pl.pallas_call(
        backward_kernel,
        out_shape=(jax.ShapeDtypeStruct((n_src // 2, feats, side), BF16),) * 2,
        in_specs=[vmem()] * (1 + n_col) + [pl.BlockSpec(memory_space=pl.ANY)],
        out_specs=(vmem(),) * 2,
        compiler_params=params(),
        cost_estimate=COST,
        name="backward",
    )(resident(dense), resident(own), *pieces, after)


def densify_stream_kernel(
    dims, rows, cols, count, tiles, out, buffer, head, following, sems
):
    n_z, n_col, blocks, slots, groups = dims
    chunk = pl.program_id(0)
    per_chunk = n_col * blocks * blocks
    per_group = slots // groups

    def copy(g):
        part = pl.ds(g * per_group, per_group)
        return pltpu.make_async_copy(tiles.at[part], buffer.at[part], sems.at[g])

    @pl.when(chunk == 0)
    def _():
        for g in range(groups):
            copy(g).start()

        def clear(i, carry):
            head[i] = slots
            return carry

        lax.fori_loop(0, 2 * n_z * per_chunk, clear, 0, unroll=8)
        following[slots] = slots
        buffer[slots] = jnp.zeros(buffer.shape[1:], buffer.dtype)

        def link(slot, carry):
            block_row, block_col = rows[0, 0, slot], cols[0, 0, slot]
            place = place_of((n_z, n_col, blocks), block_row, block_col)
            following[slot] = head[place]
            head[place] = slot
            return carry

        lax.fori_loop(0, count[0, 0], link, 0)
        for g in range(groups):
            copy(g).wait()

    tile = buffer.shape[1]

    def fill(i, carry):
        first = head[chunk * per_chunk + i]
        t = i // (blocks * blocks)
        a = pl.multiple_of((i // blocks) % blocks * tile, tile)
        b = pl.multiple_of(i % blocks * tile, tile)
        where = (0, t, pl.ds(a, tile), pl.ds(b, tile))
        out[where] = buffer[first]
        second = following[first]

        @pl.when(second != slots)
        def _():
            def more(state):
                slot, total = state
                return following[slot], total + buffer[slot].astype(F32)

            _, total = lax.while_loop(
                lambda state: state[0] != slots,
                more,
                (second, buffer[first].astype(F32)),
            )
            out[where] = total.astype(BF16)

        return carry

    lax.fori_loop(0, per_chunk, fill, 0)


def densify_stream(rows, cols, count, tiles, n_z, n_col, blocks):
    slots, tile = tiles.shape[0], tiles.shape[1]
    n_src = 2 * n_z
    groups = 8
    side = blocks * tile
    shape = (n_src, n_col, side, side)
    return pl.pallas_call(
        functools.partial(densify_stream_kernel, (n_z, n_col, blocks, slots, groups)),
        grid=(n_src,),
        out_shape=jax.ShapeDtypeStruct(shape, BF16),
        in_specs=[smem(), smem(), smem(), pl.BlockSpec(memory_space=pltpu.HBM)],
        out_specs=pl.BlockSpec((1, n_col, side, side), lambda j: (j, 0, 0, 0)),
        scratch_shapes=[
            pltpu.VMEM((slots + 1, tile, tile), BF16),
            pltpu.SMEM((n_src * n_col * blocks * blocks,), jnp.int32),
            pltpu.SMEM((slots + 1,), jnp.int32),
            pltpu.SemaphoreType.DMA((groups,)),
        ],
        compiler_params=params(32),
        cost_estimate=COST,
        name="densify",
    )(rows, cols, count, tiles)


def forward_stream_kernel(first, a, x0, x1, *rest):

    j = pl.program_id(1)

    @pl.when(j == 0)
    def _():
        value = jnp.dot(a[0, 0], x0[...], preferred_element_type=F32)
        if not first:
            value = value + rest[0][...]
        rest[-1][...] = value

    @pl.when(j == 1)
    def _():
        rest[-1][...] += jnp.dot(a[0, 0], x1[...], preferred_element_type=F32)


def forward_stream(dense, shift, x0, x1, total):
    _, n_col, side, _ = dense.shape
    feats = x0.shape[1]
    first = total is None
    block = pl.BlockSpec((side, feats), lambda t, j: (t, 0))
    return pl.pallas_call(
        functools.partial(forward_stream_kernel, first),
        grid=(n_col, 2),
        out_shape=jax.ShapeDtypeStruct((n_col * side, feats), F32),
        in_specs=[
            pl.BlockSpec((1, 1, side, side), lambda t, j: (2 * shift + j, t, 0, 0)),
            vmem(),
            vmem(),
        ]
        + ([] if first else [block]),
        out_specs=block,
        compiler_params=params(32),
        cost_estimate=COST,
        name="forward",
    )(dense, x0, x1, *([] if first else [total]))


def middle_kernel(n_col, weights, cot_own, cot_other, *refs):
    own = refs[:n_col]
    other = refs[n_col : 2 * n_col]
    spread, activated, agg, g_own, g_other = refs[2 * n_col :]
    half = cot_own.shape[1]
    f = lax.axis_index("feat")
    mine = pl.ds(pl.multiple_of(f * half, half), half)
    theirs = pl.ds(pl.multiple_of((1 - f) * half, half), half)

    def gather(parts):
        total = parts[0][...].astype(F32)
        for part in parts[1:]:
            total = total + part[...].astype(F32)
        return total.astype(BF16)

    top = jnp.concatenate([weights[mine, mine], weights[mine, theirs]], axis=1)
    low = jnp.concatenate([weights[theirs, mine], weights[theirs, theirs]], axis=1)
    agg_own = gather(own)
    agg[...] = agg_own
    both = jnp.concatenate([agg_own, gather(other)], axis=1)
    hidden = jnp.dot(both, jnp.concatenate([top, low], axis=0), preferred_element_type=F32)
    decay = jnp.exp(jnp.minimum(hidden, 0.0))
    cot = jnp.concatenate([cot_own[...], cot_other[...]], axis=1).astype(F32)
    g = (cot * decay).astype(BF16)
    spread[...] = lax.dot_general(
        top, g, (((1,), (1,)), ((), ())), preferred_element_type=F32
    ).astype(BF16)
    g_own[...] = g[:, :half]
    g_other[...] = g[:, half:]
    activated[...] = jnp.where(
        hidden[:, :half] > 0, hidden[:, :half], decay[:, :half] - 1.0
    ).astype(BF16)


def middle(weights, cot_own, cot_other, own, other):
    nodes, half = cot_own.shape
    whole = weights.shape[1]
    n_col = len(own)
    return pl.pallas_call(
        functools.partial(middle_kernel, n_col),
        out_shape=(jax.ShapeDtypeStruct((half, nodes), BF16),)
        + (jax.ShapeDtypeStruct((nodes, half), BF16),) * 4,
        in_specs=[vmem()] * (3 + 2 * n_col),
        out_specs=(vmem(),) * 5,
        compiler_params=params(),
        cost_estimate=COST,
        name="middle",
    )(weights, cot_own, cot_other, *own, *other)


def weight_kernel(agg, g_own, g_other, out):
    half = agg.shape[1]
    f = lax.axis_index("feat")
    turned = agg[...].astype(F32).T.astype(BF16)
    for columns, g in ((f * half, g_own), ((1 - f) * half, g_other)):
        columns = pl.ds(pl.multiple_of(columns, half), half)
        out[:, columns] = jnp.dot(turned, g[...], preferred_element_type=F32).astype(BF16)


def weight_term(agg, g_own, g_other):
    half = agg.shape[1]
    return pl.pallas_call(
        weight_kernel,
        out_shape=jax.ShapeDtypeStruct((half, 2 * half), BF16),
        in_specs=[vmem()] * 3,
        out_specs=vmem(),
        compiler_params=params(),
        cost_estimate=COST,
        name="weight_term",
    )(agg, g_own, g_other)


def backward_stream_kernel(n_col, a, *refs):
    pieces, out = refs[:n_col], refs[n_col]
    total = jnp.dot(pieces[0][...], a[0, 0], preferred_element_type=F32)
    for t in range(1, n_col):
        total = total + jnp.dot(pieces[t][...], a[0, t], preferred_element_type=F32)
    out[0] = total.astype(BF16)


def backward_stream(dense, parity, pieces):
    n_src, n_col, side, _ = dense.shape
    feats = pieces[0].shape[0]
    n_z = n_src // 2
    return pl.pallas_call(
        functools.partial(backward_stream_kernel, n_col),
        grid=(n_z,),
        out_shape=jax.ShapeDtypeStruct((n_z, feats, side), BF16),
        in_specs=[pl.BlockSpec((1, n_col, side, side), lambda s: (2 * s + parity, 0, 0, 0))]
        + [vmem()] * n_col,
        out_specs=pl.BlockSpec((1, feats, side), lambda s: (s, 0, 0)),
        compiler_params=params(32),
        cost_estimate=COST,
        name="backward",
    )(dense, *pieces)


def add_kernel(a, b, *rest):
    rest[-1][...] = (a[...].astype(F32) + b[...].astype(F32)).astype(BF16)


def add(a, b, *after):
    return pl.pallas_call(
        add_kernel,
        out_shape=jax.ShapeDtypeStruct(a.shape, BF16),
        in_specs=[vmem()] * 2 + [pl.BlockSpec(memory_space=pl.ANY)] * len(after),
        out_specs=vmem(),
        compiler_params=params(),
        cost_estimate=COST,
        name="add",
    )(a, b, *after)


def pair_kernel(own, arrived, *outs):
    for s, out in enumerate(outs):
        out[...] = (own[s].astype(F32) + arrived[s].astype(F32)).astype(BF16)


def pair_sums(own, arrived):
    n_z, side, feats = own.shape
    return pl.pallas_call(
        pair_kernel,
        out_shape=(jax.ShapeDtypeStruct((side, feats), BF16),) * n_z,
        in_specs=[vmem()] * 2,
        out_specs=(vmem(),) * n_z,
        compiler_params=params(),
        cost_estimate=COST,
        name="pair_sums",
    )(own, arrived)


def turned_kernel(*refs):
    total = refs[0][...].astype(F32)
    for part in refs[1:-1]:
        total = total + part[...].astype(F32)
    refs[-1][...] = total.T.astype(BF16)


def turned_sum(parts):
    feats, nodes = parts[0].shape
    return pl.pallas_call(
        turned_kernel,
        out_shape=jax.ShapeDtypeStruct((nodes, feats), BF16),
        in_specs=[vmem()] * len(parts),
        out_specs=vmem(),
        compiler_params=params(),
        cost_estimate=COST,
        name="turned_sum",
    )(*parts)


def shards(features, tile_rows, tile_cols, tile_count, tile_values, weights, cotangent):
    tile = tile_values.shape[-1]
    n_row, n_col = lax.axis_size("row"), lax.axis_size("col")
    n_z = n_row // 2
    nodes, half = features.shape
    blocks = nodes // tile
    node_total = nodes * n_row * n_col
    def sibling(v):
        return lax.ppermute(v, "row", [(i, i ^ 1) for i in range(n_row)])

    def along_z(v, s):
        return lax.ppermute(v, "row", [(i, i ^ (2 * s)) for i in range(n_row)])

    def other_feat(v):
        return lax.ppermute(v, "feat", [(0, 1), (1, 0)])

    def to_group(v, shift, flip):
        pairs = []
        for cc in range(n_col):
            for ff in range(2):
                pairs.append((2 * cc + ff, 2 * ((cc + shift) % n_col) + (ff ^ flip)))
        return lax.ppermute(v, ("col", "feat"), pairs)

    same = [features] + [along_z(features, s) for s in range(1, n_z)]
    cot_other = other_feat(cotangent)
    tiles = tile_values[0, 0]
    cell = (tile_rows, tile_cols, tile_count, tiles, n_z, n_col, blocks)
    if 2 * n_z * n_col * (blocks * tile) ** 2 <= 8 * MIB:
        dense = densify(*cell)
        totals = forward(dense, [0, 1], [features, sibling(features)], (), False)
        *same, cot_other = hold(same[1:] + [cot_other], totals[0])
        cross = [sibling(v) for v in same]
        totals = forward(dense, [2 * s for s in range(1, n_z)], same, totals, False)
        parts = forward(dense, [2 * s + 1 for s in range(1, n_z)], cross, totals, True)

        def back_of(pieces, after):
            return backward(dense, backward_own(dense, pieces[0]), pieces[1:], after)

    else:
        cross = [sibling(v) for v in same]
        dense = densify_stream(*cell)
        total = None
        for s in range(n_z):
            total = forward_stream(dense, s, same[s], cross[s], total)
        parts = total.astype(BF16).reshape(n_col, nodes, half)

        def back_of(pieces, after):
            return [backward_stream(dense, k, pieces) for k in range(2)]

    own = [parts[0]] + [to_group(parts[t], -t, 0) for t in range(1, n_col)]
    other = [to_group(parts[t], -t, 1) for t in range(n_col)]
    spread, activated, *rest = middle(weights, cotangent, cot_other, own, other)
    pieces = [spread] + [
        lax.ppermute(spread, "col", [(i, (i + t) % n_col) for i in range(n_col)])
        for t in range(1, n_col)
    ]
    term = weight_term(*rest)
    term = add(term, along_z(term, 1))

    even, odd = back_of(pieces, term)
    arrived = sibling(odd)
    sums = pair_sums(even, arrived)
    if n_z > 2:
        term = add(term, along_z(term, 2), sums[0])
    back = turned_sum([sums[0]] + [along_z(sums[s], s) for s in range(1, n_z)])

    def finish(_, v):
        for step in range(2, n_z.bit_length() - 1):
            v = add(v, along_z(v, 1 << step))
        total = v.astype(F32)
        for t in range(1, n_col):
            total = total + lax.ppermute(
                v, "col", [(i, (i + t) % n_col) for i in range(n_col)]
            ).astype(F32)
        v = total.astype(BF16)
        return add(v, sibling(v))

    once = lax.optimization_barrier(jnp.int32(1))
    whole = lax.fori_loop(0, once, finish, term)
    weight_grad = whole.astype(F32) * node_total ** (-0.5)
    return (activated, back, weight_grad)


def solution(mesh):
    return jax.shard_map(
        shards,
        mesh=mesh,
        in_specs=(
            P(("col", "row"), "feat"),
            P("row", "col", None),
            P("row", "col", None),
            P("row", "col"),
            P("row", "col", None, None, None),
            P(),
            P(("row", "col"), "feat"),
        ),
        out_specs=(P(("row", "col"), "feat"), P(("col", "row"), "feat"), P("feat", None)),
        check_vma=False,
    )
```

```python
import functools

import jax
import jax.numpy as jnp
from jax import lax
from jax.experimental import pallas as pl
from jax.experimental.pallas import tpu as pltpu
from jax.sharding import PartitionSpec as P

F32 = jnp.float32
BF16 = jnp.bfloat16
MIB = 1024 * 1024
COST = pl.CostEstimate(flops=1, bytes_accessed=1, transcendentals=0)


def params(mib=16):
    return pltpu.CompilerParams(vmem_limit_bytes=mib * MIB)


def vmem():
    return pl.BlockSpec(memory_space=pltpu.VMEM)


def smem():
    return pl.BlockSpec(memory_space=pltpu.SMEM)


def place_of(dims, block_row, block_col):
    n_z, n_col, blocks = dims
    bits, low = blocks.bit_length() - 1, blocks - 1
    j = (block_col >> bits) ^ lax.axis_index("row")
    t = (lax.axis_index("col") - (block_row >> bits)) & (n_col - 1)
    return ((((j * n_col + t) << bits) | (block_row & low)) << bits) | (block_col & low)


def densify_kernel(dims, groups, rows, cols, count, tiles, out, buffer, total, sems):
    n_z, n_col, blocks = dims
    slots, tile = buffer.shape[0], buffer.shape[1]
    per_group = slots // groups
    places = total.shape[0] - 1
    live = count[0, 0]

    def copy(g):
        part = pl.ds(g * per_group, per_group)
        return pltpu.make_async_copy(tiles.at[part], buffer.at[part], sems.at[g])

    def each_group(action):
        for g in range(groups):

            @pl.when(g * per_group < live)
            def _():
                action(g)

    each_group(lambda g: copy(g).start())

    def clear(i, carry):
        total[i] = jnp.zeros((tile, tile), F32)
        return carry

    lax.fori_loop(0, places, clear, 0, unroll=4)

    def add_group(g):
        copy(g).wait()

        def add(i, carry):
            slot = g * per_group + i
            place = place_of(dims, rows[0, 0, slot], cols[0, 0, slot])
            place = jnp.where(slot < live, place, places)
            total[place] += buffer[slot].astype(F32)
            return carry

        lax.fori_loop(0, per_group, add, 0, unroll=8)

    each_group(add_group)

    def settle(j, carry):
        for t in range(n_col):
            for a in range(blocks):
                for b in range(blocks):
                    value = total[((j * n_col + t) * blocks + a) * blocks + b]
                    out[j, t, a * tile : (a + 1) * tile, b * tile : (b + 1) * tile] = value.astype(BF16)
        return carry

    lax.fori_loop(0, 2 * n_z, settle, 0)


def densify(rows, cols, count, tiles, n_z, n_col, blocks):
    slots, tile = tiles.shape[0], tiles.shape[1]
    n_src = 2 * n_z
    groups = 8
    side = blocks * tile
    places = n_src * n_col * blocks * blocks
    return pl.pallas_call(
        functools.partial(densify_kernel, (n_z, n_col, blocks), groups),
        out_shape=pltpu.VMEM((n_src, n_col, side, side), BF16),
        in_specs=[smem(), smem(), smem(), pl.BlockSpec(memory_space=pltpu.HBM)],
        out_specs=vmem(),
        scratch_shapes=[
            pltpu.VMEM((slots, tile, tile), BF16),
            pltpu.VMEM((places + 1, tile, tile), F32),
            pltpu.SemaphoreType.DMA((groups,)),
        ],
        compiler_params=params(32),
        cost_estimate=COST,
        name="densify",
    )(in_hbm(rows), in_hbm(cols), count, in_hbm(tiles))


def in_hbm(v):
    return pltpu.with_memory_space_constraint(v, pltpu.HBM)


def resident(dense):
    return pltpu.with_memory_space_constraint(dense, pltpu.VMEM)


def hold(arrays, after):
    n = len(arrays)
    outs = pl.pallas_call(
        lambda *refs: None,
        out_shape=tuple(jax.ShapeDtypeStruct(v.shape, v.dtype) for v in arrays),
        in_specs=[pl.BlockSpec(memory_space=pl.ANY)] * n + [vmem()],
        out_specs=(pl.BlockSpec(memory_space=pl.ANY),) * n,
        input_output_aliases={i: i for i in range(n)},
        compiler_params=params(),
        cost_estimate=COST,
        name="hold",
    )(*arrays, resident(after))
    return list(outs)


def forward_kernel(places, last, dense, *refs):
    n = len(places)
    xs, refs = refs[:n], refs[n:]
    n_col, side = dense.shape[1], dense.shape[2]
    outs = refs[-n_col:]
    for t in range(n_col):
        total = jnp.dot(dense[places[0], t], xs[0][...], preferred_element_type=F32)
        for j, x in zip(places[1:], xs[1:]):
            total = total + jnp.dot(dense[j, t], x[...], preferred_element_type=F32)
        if len(refs) > n_col:
            total = total + refs[t][...]
        outs[t][...] = total.astype(BF16) if last else total


def forward(dense, places, xs, totals, last):
    _, n_col, side, _ = dense.shape
    feats = xs[0].shape[1]
    shape = jax.ShapeDtypeStruct((side, feats), BF16 if last else F32)
    return pl.pallas_call(
        functools.partial(forward_kernel, places, last),
        out_shape=(shape,) * n_col,
        in_specs=[vmem()] * (1 + len(xs) + len(totals)),
        out_specs=(vmem(),) * n_col,
        compiler_params=params(),
        cost_estimate=COST,
        name="forward",
    )(resident(dense), *xs, *totals)


def own_kernel(dense, piece, out):
    for j in range(dense.shape[0]):
        out[j] = jnp.dot(piece[...], dense[j, 0], preferred_element_type=F32)


def backward_own(dense, piece):
    n_src, _, side, _ = dense.shape
    return pl.pallas_call(
        own_kernel,
        out_shape=pltpu.VMEM((n_src, piece.shape[0], side), F32),
        in_specs=[vmem()] * 2,
        out_specs=vmem(),
        compiler_params=params(),
        cost_estimate=COST,
        name="backward_own",
    )(resident(dense), piece)


def backward_kernel(dense, own, *refs):
    pieces, outs = refs[: dense.shape[1] - 1], refs[-2:]
    for j in range(dense.shape[0]):
        total = own[j]
        for t, piece in enumerate(pieces):
            total = total + jnp.dot(piece[...], dense[j, t + 1], preferred_element_type=F32)
        outs[j % 2][j // 2] = total.astype(BF16)


def backward(dense, own, pieces, after):
    n_src, n_col, side, _ = dense.shape
    feats = own.shape[1]
    return pl.pallas_call(
        backward_kernel,
        out_shape=(jax.ShapeDtypeStruct((n_src // 2, feats, side), BF16),) * 2,
        in_specs=[vmem()] * (1 + n_col) + [pl.BlockSpec(memory_space=pl.ANY)],
        out_specs=(vmem(),) * 2,
        compiler_params=params(),
        cost_estimate=COST,
        name="backward",
    )(resident(dense), resident(own), *pieces, after)


def densify_stream_kernel(
    dims, rows, cols, count, tiles, out, buffer, head, following, sems
):
    n_z, n_col, blocks, slots, groups = dims
    chunk = pl.program_id(0)
    per_chunk = n_col * blocks * blocks
    per_group = slots // groups

    def copy(g):
        part = pl.ds(g * per_group, per_group)
        return pltpu.make_async_copy(tiles.at[part], buffer.at[part], sems.at[g])

    @pl.when(chunk == 0)
    def _():
        for g in range(groups):
            copy(g).start()

        def clear(i, carry):
            head[i] = slots
            return carry

        lax.fori_loop(0, 2 * n_z * per_chunk, clear, 0, unroll=8)
        following[slots] = slots
        buffer[slots] = jnp.zeros(buffer.shape[1:], buffer.dtype)

        def link(slot, carry):
            block_row, block_col = rows[0, 0, slot], cols[0, 0, slot]
            place = place_of((n_z, n_col, blocks), block_row, block_col)
            following[slot] = head[place]
            head[place] = slot
            return carry

        lax.fori_loop(0, count[0, 0], link, 0)
        for g in range(groups):
            copy(g).wait()

    tile = buffer.shape[1]

    def fill(i, carry):
        first = head[chunk * per_chunk + i]
        t = i // (blocks * blocks)
        a = pl.multiple_of((i // blocks) % blocks * tile, tile)
        b = pl.multiple_of(i % blocks * tile, tile)
        where = (0, t, pl.ds(a, tile), pl.ds(b, tile))
        out[where] = buffer[first]
        second = following[first]

        @pl.when(second != slots)
        def _():
            def more(state):
                slot, total = state
                return following[slot], total + buffer[slot].astype(F32)

            _, total = lax.while_loop(
                lambda state: state[0] != slots,
                more,
                (second, buffer[first].astype(F32)),
            )
            out[where] = total.astype(BF16)

        return carry

    lax.fori_loop(0, per_chunk, fill, 0)


def densify_stream(rows, cols, count, tiles, n_z, n_col, blocks):
    slots, tile = tiles.shape[0], tiles.shape[1]
    n_src = 2 * n_z
    groups = 8
    side = blocks * tile
    shape = (n_src, n_col, side, side)
    return pl.pallas_call(
        functools.partial(densify_stream_kernel, (n_z, n_col, blocks, slots, groups)),
        grid=(n_src,),
        out_shape=jax.ShapeDtypeStruct(shape, BF16),
        in_specs=[smem(), smem(), smem(), pl.BlockSpec(memory_space=pltpu.HBM)],
        out_specs=pl.BlockSpec((1, n_col, side, side), lambda j: (j, 0, 0, 0)),
        scratch_shapes=[
            pltpu.VMEM((slots + 1, tile, tile), BF16),
            pltpu.SMEM((n_src * n_col * blocks * blocks,), jnp.int32),
            pltpu.SMEM((slots + 1,), jnp.int32),
            pltpu.SemaphoreType.DMA((groups,)),
        ],
        compiler_params=params(32),
        cost_estimate=COST,
        name="densify",
    )(rows, cols, count, tiles)


def forward_stream_kernel(first, a, x0, x1, *rest):

    j = pl.program_id(1)

    @pl.when(j == 0)
    def _():
        value = jnp.dot(a[0, 0], x0[...], preferred_element_type=F32)
        if not first:
            value = value + rest[0][...]
        rest[-1][...] = value

    @pl.when(j == 1)
    def _():
        rest[-1][...] += jnp.dot(a[0, 0], x1[...], preferred_element_type=F32)


def forward_stream(dense, shift, x0, x1, total):
    _, n_col, side, _ = dense.shape
    feats = x0.shape[1]
    first = total is None
    block = pl.BlockSpec((side, feats), lambda t, j: (t, 0))
    return pl.pallas_call(
        functools.partial(forward_stream_kernel, first),
        grid=(n_col, 2),
        out_shape=jax.ShapeDtypeStruct((n_col * side, feats), F32),
        in_specs=[
            pl.BlockSpec((1, 1, side, side), lambda t, j: (2 * shift + j, t, 0, 0)),
            vmem(),
            vmem(),
        ]
        + ([] if first else [block]),
        out_specs=block,
        compiler_params=params(32),
        cost_estimate=COST,
        name="forward",
    )(dense, x0, x1, *([] if first else [total]))


def middle_kernel(n_col, weights, cot_own, cot_other, *refs):
    own = refs[:n_col]
    other = refs[n_col : 2 * n_col]
    spread, activated, agg, g_own, g_other = refs[2 * n_col :]
    half = cot_own.shape[1]
    f = lax.axis_index("feat")
    mine = pl.ds(pl.multiple_of(f * half, half), half)
    theirs = pl.ds(pl.multiple_of((1 - f) * half, half), half)

    def gather(parts):
        total = parts[0][...].astype(F32)
        for part in parts[1:]:
            total = total + part[...].astype(F32)
        return total.astype(BF16)

    top = jnp.concatenate([weights[mine, mine], weights[mine, theirs]], axis=1)
    low = jnp.concatenate([weights[theirs, mine], weights[theirs, theirs]], axis=1)
    agg_own = gather(own)
    agg[...] = agg_own
    both = jnp.concatenate([agg_own, gather(other)], axis=1)
    hidden = jnp.dot(both, jnp.concatenate([top, low], axis=0), preferred_element_type=F32)
    decay = jnp.exp(jnp.minimum(hidden, 0.0))
    cot = jnp.concatenate([cot_own[...], cot_other[...]], axis=1).astype(F32)
    g = (cot * decay).astype(BF16)
    spread[...] = lax.dot_general(
        top, g, (((1,), (1,)), ((), ())), preferred_element_type=F32
    ).astype(BF16)
    g_own[...] = g[:, :half]
    g_other[...] = g[:, half:]
    activated[...] = jnp.where(
        hidden[:, :half] > 0, hidden[:, :half], decay[:, :half] - 1.0
    ).astype(BF16)


def middle(weights, cot_own, cot_other, own, other):
    nodes, half = cot_own.shape
    whole = weights.shape[1]
    n_col = len(own)
    return pl.pallas_call(
        functools.partial(middle_kernel, n_col),
        out_shape=(jax.ShapeDtypeStruct((half, nodes), BF16),)
        + (jax.ShapeDtypeStruct((nodes, half), BF16),) * 4,
        in_specs=[vmem()] * (3 + 2 * n_col),
        out_specs=(vmem(),) * 5,
        compiler_params=params(),
        cost_estimate=COST,
        name="middle",
    )(weights, cot_own, cot_other, *own, *other)


def weight_kernel(agg, g_own, g_other, out):
    half = agg.shape[1]
    f = lax.axis_index("feat")
    turned = agg[...].astype(F32).T.astype(BF16)
    for columns, g in ((f * half, g_own), ((1 - f) * half, g_other)):
        columns = pl.ds(pl.multiple_of(columns, half), half)
        out[:, columns] = jnp.dot(turned, g[...], preferred_element_type=F32).astype(BF16)


def weight_term(agg, g_own, g_other):
    half = agg.shape[1]
    return pl.pallas_call(
        weight_kernel,
        out_shape=jax.ShapeDtypeStruct((half, 2 * half), BF16),
        in_specs=[vmem()] * 3,
        out_specs=vmem(),
        compiler_params=params(),
        cost_estimate=COST,
        name="weight_term",
    )(agg, g_own, g_other)


def backward_stream_kernel(n_col, a, *refs):
    pieces, out = refs[:n_col], refs[n_col]
    total = jnp.dot(pieces[0][...], a[0, 0], preferred_element_type=F32)
    for t in range(1, n_col):
        total = total + jnp.dot(pieces[t][...], a[0, t], preferred_element_type=F32)
    out[0] = total.astype(BF16)


def backward_stream(dense, parity, pieces):
    n_src, n_col, side, _ = dense.shape
    feats = pieces[0].shape[0]
    n_z = n_src // 2
    return pl.pallas_call(
        functools.partial(backward_stream_kernel, n_col),
        grid=(n_z,),
        out_shape=jax.ShapeDtypeStruct((n_z, feats, side), BF16),
        in_specs=[pl.BlockSpec((1, n_col, side, side), lambda s: (2 * s + parity, 0, 0, 0))]
        + [vmem()] * n_col,
        out_specs=pl.BlockSpec((1, feats, side), lambda s: (s, 0, 0)),
        compiler_params=params(32),
        cost_estimate=COST,
        name="backward",
    )(dense, *pieces)


def add_kernel(a, b, *rest):
    rest[-1][...] = (a[...].astype(F32) + b[...].astype(F32)).astype(BF16)


def add(a, b, *after):
    return pl.pallas_call(
        add_kernel,
        out_shape=jax.ShapeDtypeStruct(a.shape, BF16),
        in_specs=[vmem()] * 2 + [pl.BlockSpec(memory_space=pl.ANY)] * len(after),
        out_specs=vmem(),
        compiler_params=params(),
        cost_estimate=COST,
        name="add",
    )(a, b, *after)


def pair_kernel(own, arrived, *outs):
    for s, out in enumerate(outs):
        out[...] = (own[s].astype(F32) + arrived[s].astype(F32)).astype(BF16)


def pair_sums(own, arrived):
    n_z, side, feats = own.shape
    return pl.pallas_call(
        pair_kernel,
        out_shape=(jax.ShapeDtypeStruct((side, feats), BF16),) * n_z,
        in_specs=[vmem()] * 2,
        out_specs=(vmem(),) * n_z,
        compiler_params=params(),
        cost_estimate=COST,
        name="pair_sums",
    )(own, arrived)


def turned_kernel(*refs):
    total = refs[0][...].astype(F32)
    for part in refs[1:-1]:
        total = total + part[...].astype(F32)
    refs[-1][...] = total.T.astype(BF16)


def turned_sum(parts):
    feats, nodes = parts[0].shape
    return pl.pallas_call(
        turned_kernel,
        out_shape=jax.ShapeDtypeStruct((nodes, feats), BF16),
        in_specs=[vmem()] * len(parts),
        out_specs=vmem(),
        compiler_params=params(),
        cost_estimate=COST,
        name="turned_sum",
    )(*parts)


def shards(features, tile_rows, tile_cols, tile_count, tile_values, weights, cotangent):
    tile = tile_values.shape[-1]
    n_row, n_col = lax.axis_size("row"), lax.axis_size("col")
    n_z = n_row // 2
    nodes, half = features.shape
    blocks = nodes // tile
    node_total = nodes * n_row * n_col
    def sibling(v):
        return lax.ppermute(v, "row", [(i, i ^ 1) for i in range(n_row)])

    def along_z(v, s):
        return lax.ppermute(v, "row", [(i, i ^ (2 * s)) for i in range(n_row)])

    def other_feat(v):
        return lax.ppermute(v, "feat", [(0, 1), (1, 0)])

    def to_group(v, shift, flip):
        pairs = []
        for cc in range(n_col):
            for ff in range(2):
                pairs.append((2 * cc + ff, 2 * ((cc + shift) % n_col) + (ff ^ flip)))
        return lax.ppermute(v, ("col", "feat"), pairs)

    same = [features] + [along_z(features, s) for s in range(1, n_z)]
    cot_other = other_feat(cotangent)
    tiles = tile_values[0, 0]
    cell = (tile_rows, tile_cols, tile_count, tiles, n_z, n_col, blocks)
    if 2 * n_z * n_col * (blocks * tile) ** 2 <= 8 * MIB:
        dense = densify(*cell)
        totals = forward(dense, [0, 1], [features, sibling(features)], (), False)
        far = range(n_z - 1, 0, -1)
        *same, cot_other = hold([same[s] for s in far] + [cot_other], totals[0])
        same.reverse()
        cross = [sibling(v) for v in same]
        totals = forward(dense, [2 * s for s in range(1, n_z)], same, totals, False)
        parts = forward(dense, [2 * s + 1 for s in range(1, n_z)], cross, totals, True)

        def back_of(pieces, after):
            return backward(dense, backward_own(dense, pieces[0]), pieces[1:], after)

    else:
        cross = [sibling(v) for v in same]
        dense = densify_stream(*cell)
        total = None
        for s in range(n_z):
            total = forward_stream(dense, s, same[s], cross[s], total)
        parts = total.astype(BF16).reshape(n_col, nodes, half)

        def back_of(pieces, after):
            return [backward_stream(dense, k, pieces) for k in range(2)]

    own = [parts[0]] + [to_group(parts[t], -t, 0) for t in range(1, n_col)]
    other = [to_group(parts[t], -t, 1) for t in range(n_col)]
    spread, activated, *rest = middle(weights, cotangent, cot_other, own, other)
    pieces = [spread] + [
        lax.ppermute(spread, "col", [(i, (i + t) % n_col) for i in range(n_col)])
        for t in range(1, n_col)
    ]
    term = weight_term(*rest)
    term = add(term, along_z(term, 1))

    even, odd = back_of(pieces, term)
    arrived = sibling(odd)
    sums = pair_sums(even, arrived)
    if n_z > 2:
        term = add(term, along_z(term, 2), sums[0])
    order = sorted(range(1, n_z), key=lambda s: (s != n_z // 2, s))
    back = turned_sum([sums[0]] + [along_z(sums[s], s) for s in order])

    def finish(_, v):
        for step in range(2, n_z.bit_length() - 1):
            v = add(v, along_z(v, 1 << step))
        total = v.astype(F32)
        for t in range(1, n_col):
            total = total + lax.ppermute(
                v, "col", [(i, (i + t) % n_col) for i in range(n_col)]
            ).astype(F32)
        v = total.astype(BF16)
        return add(v, sibling(v))

    once = lax.optimization_barrier(jnp.int32(1))
    whole = lax.fori_loop(0, once, finish, term)
    weight_grad = whole.astype(F32) * node_total ** (-0.5)
    return (activated, back, weight_grad)


def solution(mesh):
    return jax.shard_map(
        shards,
        mesh=mesh,
        in_specs=(
            P(("col", "row"), "feat"),
            P("row", "col", None),
            P("row", "col", None),
            P("row", "col"),
            P("row", "col", None, None, None),
            P(),
            P(("row", "col"), "feat"),
        ),
        out_specs=(P(("row", "col"), "feat"), P(("col", "row"), "feat"), P("feat", None)),
        check_vma=False,
    )
```

```python
import functools

import jax
import jax.numpy as jnp
from jax import lax
from jax.experimental import pallas as pl
from jax.experimental.pallas import tpu as pltpu
from jax.sharding import PartitionSpec as P

F32 = jnp.float32
BF16 = jnp.bfloat16
MIB = 1024 * 1024
COST = pl.CostEstimate(flops=1, bytes_accessed=1, transcendentals=0)


def params(mib=16):
    return pltpu.CompilerParams(vmem_limit_bytes=mib * MIB)


def vmem():
    return pl.BlockSpec(memory_space=pltpu.VMEM)


def smem():
    return pl.BlockSpec(memory_space=pltpu.SMEM)


def place_of(dims, block_row, block_col):
    n_z, n_col, blocks = dims
    bits, low = blocks.bit_length() - 1, blocks - 1
    j = (block_col >> bits) ^ lax.axis_index("row")
    t = (lax.axis_index("col") - (block_row >> bits)) & (n_col - 1)
    return ((((j * n_col + t) << bits) | (block_row & low)) << bits) | (block_col & low)


def densify_kernel(dims, groups, rows, cols, count, tiles, out, buffer, total, sems):
    n_z, n_col, blocks = dims
    slots, tile = buffer.shape[0], buffer.shape[1]
    per_group = slots // groups
    places = total.shape[0] - 1
    live = count[0, 0]

    def copy(g):
        part = pl.ds(g * per_group, per_group)
        return pltpu.make_async_copy(tiles.at[part], buffer.at[part], sems.at[g])

    def each_group(action):
        for g in range(groups):

            @pl.when(g * per_group < live)
            def _():
                action(g)

    each_group(lambda g: copy(g).start())

    def clear(i, carry):
        total[i] = jnp.zeros((tile, tile), F32)
        return carry

    lax.fori_loop(0, places, clear, 0, unroll=4)

    def add_group(g):
        copy(g).wait()

        def add(i, carry):
            slot = g * per_group + i
            place = place_of(dims, rows[0, 0, slot], cols[0, 0, slot])
            place = jnp.where(slot < live, place, places)
            total[place] += buffer[slot].astype(F32)
            return carry

        lax.fori_loop(0, per_group, add, 0, unroll=8)

    each_group(add_group)

    def settle(j, carry):
        for t in range(n_col):
            for a in range(blocks):
                for b in range(blocks):
                    value = total[((j * n_col + t) * blocks + a) * blocks + b]
                    out[j, t, a * tile : (a + 1) * tile, b * tile : (b + 1) * tile] = value.astype(BF16)
        return carry

    lax.fori_loop(0, 2 * n_z, settle, 0)


def densify(rows, cols, count, tiles, n_z, n_col, blocks):
    slots, tile = tiles.shape[0], tiles.shape[1]
    n_src = 2 * n_z
    groups = 8
    side = blocks * tile
    places = n_src * n_col * blocks * blocks
    return pl.pallas_call(
        functools.partial(densify_kernel, (n_z, n_col, blocks), groups),
        out_shape=pltpu.VMEM((n_src, n_col, side, side), BF16),
        in_specs=[smem(), smem(), smem(), pl.BlockSpec(memory_space=pltpu.HBM)],
        out_specs=vmem(),
        scratch_shapes=[
            pltpu.VMEM((slots, tile, tile), BF16),
            pltpu.VMEM((places + 1, tile, tile), F32),
            pltpu.SemaphoreType.DMA((groups,)),
        ],
        compiler_params=params(32),
        cost_estimate=COST,
        name="densify",
    )(in_hbm(rows), in_hbm(cols), count, in_hbm(tiles))


def in_hbm(v):
    return pltpu.with_memory_space_constraint(v, pltpu.HBM)


def resident(dense):
    return pltpu.with_memory_space_constraint(dense, pltpu.VMEM)


def hold(arrays, after):
    n = len(arrays)
    outs = pl.pallas_call(
        lambda *refs: None,
        out_shape=tuple(jax.ShapeDtypeStruct(v.shape, v.dtype) for v in arrays),
        in_specs=[pl.BlockSpec(memory_space=pl.ANY)] * n + [vmem()],
        out_specs=(pl.BlockSpec(memory_space=pl.ANY),) * n,
        input_output_aliases={i: i for i in range(n)},
        compiler_params=params(),
        cost_estimate=COST,
        name="hold",
    )(*arrays, resident(after))
    return list(outs)


def forward_kernel(places, last, dense, *refs):
    n = len(places)
    xs, refs = refs[:n], refs[n:]
    n_col, side = dense.shape[1], dense.shape[2]
    outs = refs[-n_col:]
    for t in range(n_col):
        total = jnp.dot(dense[places[0], t], xs[0][...], preferred_element_type=F32)
        for j, x in zip(places[1:], xs[1:]):
            total = total + jnp.dot(dense[j, t], x[...], preferred_element_type=F32)
        if len(refs) > n_col:
            total = total + refs[t][...]
        outs[t][...] = total.astype(BF16) if last else total


def forward(dense, places, xs, totals, last):
    _, n_col, side, _ = dense.shape
    feats = xs[0].shape[1]
    shape = jax.ShapeDtypeStruct((side, feats), BF16 if last else F32)
    return pl.pallas_call(
        functools.partial(forward_kernel, places, last),
        out_shape=(shape,) * n_col,
        in_specs=[vmem()] * (1 + len(xs) + len(totals)),
        out_specs=(vmem(),) * n_col,
        compiler_params=params(),
        cost_estimate=COST,
        name="forward",
    )(resident(dense), *xs, *totals)


def elu(h):
    return jnp.where(h > 0, h, jnp.exp(jnp.minimum(h, 0.0)) - 1.0).astype(BF16)


def own_kernel(dense, piece, hidden, out, activated):
    activated[...] = elu(hidden[...])
    for j in range(dense.shape[0]):
        out[j] = jnp.dot(piece[...], dense[j, 0], preferred_element_type=F32)


def backward_own(dense, piece, hidden):
    n_src, _, side, _ = dense.shape
    return pl.pallas_call(
        own_kernel,
        out_shape=(
            pltpu.VMEM((n_src, piece.shape[0], side), F32),
            jax.ShapeDtypeStruct(hidden.shape, BF16),
        ),
        in_specs=[vmem()] * 3,
        out_specs=(vmem(),) * 2,
        compiler_params=params(),
        cost_estimate=COST,
        name="backward_own",
    )(resident(dense), piece, hidden)


def backward_kernel(dense, own, *refs):
    pieces, outs = refs[: dense.shape[1] - 1], refs[-2:]
    for j in range(dense.shape[0]):
        total = own[j]
        for t, piece in enumerate(pieces):
            total = total + jnp.dot(piece[...], dense[j, t + 1], preferred_element_type=F32)
        outs[j % 2][j // 2] = total.astype(BF16)


def backward(dense, own, pieces):
    n_src, n_col, side, _ = dense.shape
    feats = own.shape[1]
    return pl.pallas_call(
        backward_kernel,
        out_shape=(jax.ShapeDtypeStruct((n_src // 2, feats, side), BF16),) * 2,
        in_specs=[vmem()] * (1 + n_col),
        out_specs=(vmem(),) * 2,
        compiler_params=params(),
        cost_estimate=COST,
        name="backward",
    )(resident(dense), resident(own), *pieces)


def densify_stream_kernel(
    dims, rows, cols, count, tiles, out, buffer, head, following, sems
):
    n_z, n_col, blocks, slots, groups = dims
    chunk = pl.program_id(0)
    per_chunk = n_col * blocks * blocks
    per_group = slots // groups

    def copy(g):
        part = pl.ds(g * per_group, per_group)
        return pltpu.make_async_copy(tiles.at[part], buffer.at[part], sems.at[g])

    @pl.when(chunk == 0)
    def _():
        for g in range(groups):
            copy(g).start()

        def clear(i, carry):
            head[i] = slots
            return carry

        lax.fori_loop(0, 2 * n_z * per_chunk, clear, 0, unroll=8)
        following[slots] = slots
        buffer[slots] = jnp.zeros(buffer.shape[1:], buffer.dtype)

        def link(slot, carry):
            block_row, block_col = rows[0, 0, slot], cols[0, 0, slot]
            place = place_of((n_z, n_col, blocks), block_row, block_col)
            following[slot] = head[place]
            head[place] = slot
            return carry

        lax.fori_loop(0, count[0, 0], link, 0)
        for g in range(groups):
            copy(g).wait()

    tile = buffer.shape[1]

    def fill(i, carry):
        first = head[chunk * per_chunk + i]
        t = i // (blocks * blocks)
        a = pl.multiple_of((i // blocks) % blocks * tile, tile)
        b = pl.multiple_of(i % blocks * tile, tile)
        where = (0, t, pl.ds(a, tile), pl.ds(b, tile))
        out[where] = buffer[first]
        second = following[first]

        @pl.when(second != slots)
        def _():
            def more(state):
                slot, total = state
                return following[slot], total + buffer[slot].astype(F32)

            _, total = lax.while_loop(
                lambda state: state[0] != slots,
                more,
                (second, buffer[first].astype(F32)),
            )
            out[where] = total.astype(BF16)

        return carry

    lax.fori_loop(0, per_chunk, fill, 0)


def densify_stream(rows, cols, count, tiles, n_z, n_col, blocks):
    slots, tile = tiles.shape[0], tiles.shape[1]
    n_src = 2 * n_z
    groups = 8
    side = blocks * tile
    shape = (n_src, n_col, side, side)
    return pl.pallas_call(
        functools.partial(densify_stream_kernel, (n_z, n_col, blocks, slots, groups)),
        grid=(n_src,),
        out_shape=jax.ShapeDtypeStruct(shape, BF16),
        in_specs=[smem(), smem(), smem(), pl.BlockSpec(memory_space=pltpu.HBM)],
        out_specs=pl.BlockSpec((1, n_col, side, side), lambda j: (j, 0, 0, 0)),
        scratch_shapes=[
            pltpu.VMEM((slots + 1, tile, tile), BF16),
            pltpu.SMEM((n_src * n_col * blocks * blocks,), jnp.int32),
            pltpu.SMEM((slots + 1,), jnp.int32),
            pltpu.SemaphoreType.DMA((groups,)),
        ],
        compiler_params=params(32),
        cost_estimate=COST,
        name="densify",
    )(rows, cols, count, tiles)


def forward_stream_kernel(first, a, x0, x1, *rest):

    j = pl.program_id(1)

    @pl.when(j == 0)
    def _():
        value = jnp.dot(a[0, 0], x0[...], preferred_element_type=F32)
        if not first:
            value = value + rest[0][...]
        rest[-1][...] = value

    @pl.when(j == 1)
    def _():
        rest[-1][...] += jnp.dot(a[0, 0], x1[...], preferred_element_type=F32)


def forward_stream(dense, shift, x0, x1, total):
    _, n_col, side, _ = dense.shape
    feats = x0.shape[1]
    first = total is None
    block = pl.BlockSpec((side, feats), lambda t, j: (t, 0))
    return pl.pallas_call(
        functools.partial(forward_stream_kernel, first),
        grid=(n_col, 2),
        out_shape=jax.ShapeDtypeStruct((n_col * side, feats), F32),
        in_specs=[
            pl.BlockSpec((1, 1, side, side), lambda t, j: (2 * shift + j, t, 0, 0)),
            vmem(),
            vmem(),
        ]
        + ([] if first else [block]),
        out_specs=block,
        compiler_params=params(32),
        cost_estimate=COST,
        name="forward",
    )(dense, x0, x1, *([] if first else [total]))


def middle_kernel(n_col, weights, cot_own, cot_other, *refs):
    own = refs[:n_col]
    other = refs[n_col : 2 * n_col]
    spread, kept, agg, g_own, g_other = refs[2 * n_col :]
    half = cot_own.shape[1]
    f = lax.axis_index("feat")
    mine = pl.ds(pl.multiple_of(f * half, half), half)
    theirs = pl.ds(pl.multiple_of((1 - f) * half, half), half)

    def gather(parts):
        total = parts[0][...].astype(F32)
        for part in parts[1:]:
            total = total + part[...].astype(F32)
        return total.astype(BF16)

    top = jnp.concatenate([weights[mine, mine], weights[mine, theirs]], axis=1)
    low = jnp.concatenate([weights[theirs, mine], weights[theirs, theirs]], axis=1)
    agg_own = gather(own)
    agg[...] = agg_own
    both = jnp.concatenate([agg_own, gather(other)], axis=1)
    hidden = jnp.dot(both, jnp.concatenate([top, low], axis=0), preferred_element_type=F32)
    decay = jnp.exp(jnp.minimum(hidden, 0.0))
    cot = jnp.concatenate([cot_own[...], cot_other[...]], axis=1).astype(F32)
    g = (cot * decay).astype(BF16)
    spread[...] = lax.dot_general(
        top, g, (((1,), (1,)), ((), ())), preferred_element_type=F32
    ).astype(BF16)
    g_own[...] = g[:, :half]
    g_other[...] = g[:, half:]
    kept[...] = hidden[:, :half]


def middle(weights, cot_own, cot_other, own, other):
    nodes, half = cot_own.shape
    whole = weights.shape[1]
    n_col = len(own)
    return pl.pallas_call(
        functools.partial(middle_kernel, n_col),
        out_shape=(
            jax.ShapeDtypeStruct((half, nodes), BF16),
            jax.ShapeDtypeStruct((nodes, half), F32),
        )
        + (jax.ShapeDtypeStruct((nodes, half), BF16),) * 3,
        in_specs=[vmem()] * (3 + 2 * n_col),
        out_specs=(vmem(),) * 5,
        compiler_params=params(),
        cost_estimate=COST,
        name="middle",
    )(weights, cot_own, cot_other, *own, *other)


def weight_kernel(agg, g_own, g_other, keep, send, whole):
    half, rows = agg.shape[1], keep.shape[0]
    core, f = lax.axis_index("row") % 2, lax.axis_index("feat")
    turned = agg[...].astype(F32).T.astype(BF16)
    for columns, g in ((f * half, g_own), ((1 - f) * half, g_other)):
        columns = pl.ds(pl.multiple_of(columns, half), half)
        whole[:, columns] = jnp.dot(turned, g[...], preferred_element_type=F32)
        term = whole[:, columns].astype(BF16)
        first, second = term[:rows], term[rows:]
        keep[:, columns] = jnp.where(core == 0, first, second)
        send[:, columns] = jnp.where(core == 0, second, first)


def weight_term(agg, g_own, g_other):
    half = agg.shape[1]
    return pl.pallas_call(
        weight_kernel,
        out_shape=(jax.ShapeDtypeStruct((half // 2, 2 * half), BF16),) * 2
        + (pltpu.VMEM((half, 2 * half), F32),),
        in_specs=[vmem()] * 3,
        out_specs=(vmem(),) * 3,
        compiler_params=params(),
        cost_estimate=COST,
        name="weight_term",
    )(agg, g_own, g_other)


def assemble_kernel(scale, mine, theirs, out):
    rows = mine.shape[0]
    core = lax.axis_index("row") % 2
    own, other = mine[...].astype(F32) * scale, theirs[...].astype(F32) * scale
    out[:rows, :] = jnp.where(core == 0, own, other)
    out[rows:, :] = jnp.where(core == 0, other, own)


def assemble(scale, mine, theirs):
    rows, whole = mine.shape
    return pl.pallas_call(
        functools.partial(assemble_kernel, scale),
        out_shape=jax.ShapeDtypeStruct((2 * rows, whole), F32),
        in_specs=[vmem()] * 2,
        out_specs=vmem(),
        compiler_params=params(),
        cost_estimate=COST,
        name="assemble",
    )(mine, theirs)


def backward_stream_kernel(n_col, a, *refs):
    pieces, out = refs[:n_col], refs[n_col]
    total = jnp.dot(pieces[0][...], a[0, 0], preferred_element_type=F32)
    for t in range(1, n_col):
        total = total + jnp.dot(pieces[t][...], a[0, t], preferred_element_type=F32)
    out[0] = total.astype(BF16)


def backward_stream(dense, parity, pieces):
    n_src, n_col, side, _ = dense.shape
    feats = pieces[0].shape[0]
    n_z = n_src // 2
    return pl.pallas_call(
        functools.partial(backward_stream_kernel, n_col),
        grid=(n_z,),
        out_shape=jax.ShapeDtypeStruct((n_z, feats, side), BF16),
        in_specs=[pl.BlockSpec((1, n_col, side, side), lambda s: (2 * s + parity, 0, 0, 0))]
        + [vmem()] * n_col,
        out_specs=pl.BlockSpec((1, feats, side), lambda s: (s, 0, 0)),
        compiler_params=params(32),
        cost_estimate=COST,
        name="backward",
    )(dense, *pieces)


def add_kernel(a, b, *rest):
    rest[-1][...] = (a[...].astype(F32) + b[...].astype(F32)).astype(BF16)


def add(a, b, *after):
    return pl.pallas_call(
        add_kernel,
        out_shape=jax.ShapeDtypeStruct(a.shape, BF16),
        in_specs=[vmem()] * 2 + [pl.BlockSpec(memory_space=pl.ANY)] * len(after),
        out_specs=vmem(),
        compiler_params=params(),
        cost_estimate=COST,
        name="add",
    )(a, b, *after)


def pair_kernel(own, arrived, *outs):
    for s, out in enumerate(outs):
        out[...] = (own[s].astype(F32) + arrived[s].astype(F32)).astype(BF16)


def pair_sums(own, arrived):
    n_z, side, feats = own.shape
    return pl.pallas_call(
        pair_kernel,
        out_shape=(jax.ShapeDtypeStruct((side, feats), BF16),) * n_z,
        in_specs=[vmem()] * 2,
        out_specs=(vmem(),) * n_z,
        compiler_params=params(),
        cost_estimate=COST,
        name="pair_sums",
    )(own, arrived)


def turned_kernel(*refs):
    total = refs[0][...].astype(F32)
    for part in refs[1:-2]:
        total = total + part[...].astype(F32)
    refs[-1][...] = total.T.astype(BF16)


def turned_sum(parts, after):
    feats, nodes = parts[0].shape
    return pl.pallas_call(
        turned_kernel,
        out_shape=jax.ShapeDtypeStruct((nodes, feats), BF16),
        in_specs=[vmem()] * len(parts) + [pl.BlockSpec(memory_space=pl.ANY)],
        out_specs=vmem(),
        compiler_params=params(),
        cost_estimate=COST,
        name="turned_sum",
    )(*parts, after)


def shards(features, tile_rows, tile_cols, tile_count, tile_values, weights, cotangent):
    tile = tile_values.shape[-1]
    n_row, n_col = lax.axis_size("row"), lax.axis_size("col")
    n_z = n_row // 2
    nodes, half = features.shape
    blocks = nodes // tile
    node_total = nodes * n_row * n_col
    def sibling(v):
        return lax.ppermute(v, "row", [(i, i ^ 1) for i in range(n_row)])

    def along_z(v, s):
        return lax.ppermute(v, "row", [(i, i ^ (2 * s)) for i in range(n_row)])

    def other_feat(v):
        return lax.ppermute(v, "feat", [(0, 1), (1, 0)])

    def to_group(v, shift, flip):
        pairs = []
        for cc in range(n_col):
            for ff in range(2):
                pairs.append((2 * cc + ff, 2 * ((cc + shift) % n_col) + (ff ^ flip)))
        return lax.ppermute(v, ("col", "feat"), pairs)

    same = [features] + [along_z(features, s) for s in range(1, n_z)]
    cot_other = other_feat(cotangent)
    tiles = tile_values[0, 0]
    cell = (tile_rows, tile_cols, tile_count, tiles, n_z, n_col, blocks)
    if 2 * n_z * n_col * (blocks * tile) ** 2 <= 8 * MIB:
        dense = densify(*cell)
        totals = forward(dense, [0, 1], [features, sibling(features)], (), False)
        far = range(n_z - 1, 0, -1)
        *same, cot_other = hold([same[s] for s in far] + [cot_other], totals[0])
        same.reverse()
        cross = [sibling(v) for v in same]
        totals = forward(dense, [2 * s for s in range(1, n_z)], same, totals, False)
        parts = forward(dense, [2 * s + 1 for s in range(1, n_z)], cross, totals, True)

        def back_of(pieces, hidden):
            own, activated = backward_own(dense, pieces[0], hidden)
            return *backward(dense, own, pieces[1:]), activated

    else:
        cross = [sibling(v) for v in same]
        dense = densify_stream(*cell)
        total = None
        for s in range(n_z):
            total = forward_stream(dense, s, same[s], cross[s], total)
        parts = total.astype(BF16).reshape(n_col, nodes, half)

        def back_of(pieces, hidden):
            even, odd = (backward_stream(dense, k, pieces) for k in range(2))
            return even, odd, elu(hidden)

    own = [parts[0]] + [to_group(parts[t], -t, 0) for t in range(1, n_col)]
    other = [to_group(parts[t], -t, 1) for t in range(n_col)]
    spread, hidden, *rest = middle(weights, cotangent, cot_other, own, other)
    pieces = [spread] + [
        lax.ppermute(spread, "col", [(i, (i + t) % n_col) for i in range(n_col)])
        for t in range(1, n_col)
    ]
    keep, send, weight_grad = weight_term(*rest)
    term = add(keep, sibling(send))
    even, odd, activated = back_of(pieces, hidden)
    term = add(term, along_z(term, 1), odd)
    (odd,) = hold([odd], term)
    arrived = sibling(odd)
    sums = pair_sums(even, arrived)
    if n_z > 2:
        term = add(term, along_z(term, 2), sums[0])
    order = sorted(range(1, n_z), key=lambda s: (s != n_z // 2, s))

    def finish(_, state):
        v = state[0]
        for step in range(2, n_z.bit_length() - 1):
            v = add(v, along_z(v, 1 << step))
        total = v.astype(F32)
        for t in range(1, n_col):
            total = total + lax.ppermute(
                v, "col", [(i, (i + t) % n_col) for i in range(n_col)]
            ).astype(F32)
        v = total.astype(BF16)
        return v, assemble(node_total ** (-0.5), v, sibling(v))

    once = lax.optimization_barrier(jnp.int32(1))
    _, weight_grad = lax.fori_loop(0, once, finish, (term, weight_grad))
    back = turned_sum([sums[0]] + [along_z(sums[s], s) for s in order], weight_grad)
    return (activated, back, weight_grad)


def solution(mesh):
    return jax.shard_map(
        shards,
        mesh=mesh,
        in_specs=(
            P(("col", "row"), "feat"),
            P("row", "col", None),
            P("row", "col", None),
            P("row", "col"),
            P("row", "col", None, None, None),
            P(),
            P(("row", "col"), "feat"),
        ),
        out_specs=(P(("row", "col"), "feat"), P(("col", "row"), "feat"), P("feat", None)),
        check_vma=False,
    )
```

```python
import functools

import jax
import jax.numpy as jnp
from jax import lax
from jax.experimental import pallas as pl
from jax.experimental.pallas import tpu as pltpu
from jax.sharding import PartitionSpec as P

F32 = jnp.float32
BF16 = jnp.bfloat16
MIB = 1024 * 1024
COST = pl.CostEstimate(flops=1, bytes_accessed=1, transcendentals=0)


def params(mib=16):
    return pltpu.CompilerParams(vmem_limit_bytes=mib * MIB)


def vmem():
    return pl.BlockSpec(memory_space=pltpu.VMEM)


def smem():
    return pl.BlockSpec(memory_space=pltpu.SMEM)


def place_of(dims, block_row, block_col):
    n_z, n_col, blocks = dims
    bits, low = blocks.bit_length() - 1, blocks - 1
    j = (block_col >> bits) ^ lax.axis_index("row")
    t = (lax.axis_index("col") - (block_row >> bits)) & (n_col - 1)
    return ((((j * n_col + t) << bits) | (block_row & low)) << bits) | (block_col & low)


def densify_kernel(dims, groups, rows, cols, count, tiles, out, buffer, total, sems):
    n_z, n_col, blocks = dims
    slots, tile = buffer.shape[0], buffer.shape[1]
    per_group = slots // groups
    places = total.shape[0] - 1
    live = count[0, 0]

    def copy(g):
        part = pl.ds(g * per_group, per_group)
        return pltpu.make_async_copy(tiles.at[part], buffer.at[part], sems.at[g])

    def each_group(action):
        for g in range(groups):

            @pl.when(g * per_group < live)
            def _():
                action(g)

    each_group(lambda g: copy(g).start())

    def clear(i, carry):
        total[i] = jnp.zeros((tile, tile), F32)
        return carry

    lax.fori_loop(0, places, clear, 0, unroll=4)

    def add_group(g):
        copy(g).wait()

        def add(i, carry):
            slot = g * per_group + i
            place = place_of(dims, rows[0, 0, slot], cols[0, 0, slot])
            place = jnp.where(slot < live, place, places)
            total[place] += buffer[slot].astype(F32)
            return carry

        lax.fori_loop(0, per_group, add, 0, unroll=8)

    each_group(add_group)

    def settle(j, carry):
        for t in range(n_col):
            for a in range(blocks):
                for b in range(blocks):
                    value = total[((j * n_col + t) * blocks + a) * blocks + b]
                    out[j, t, a * tile : (a + 1) * tile, b * tile : (b + 1) * tile] = value.astype(BF16)
        return carry

    lax.fori_loop(0, 2 * n_z, settle, 0)


def densify(rows, cols, count, tiles, n_z, n_col, blocks):
    slots, tile = tiles.shape[0], tiles.shape[1]
    n_src = 2 * n_z
    groups = 8
    side = blocks * tile
    places = n_src * n_col * blocks * blocks
    return pl.pallas_call(
        functools.partial(densify_kernel, (n_z, n_col, blocks), groups),
        out_shape=pltpu.VMEM((n_src, n_col, side, side), BF16),
        in_specs=[smem(), smem(), smem(), pl.BlockSpec(memory_space=pltpu.HBM)],
        out_specs=vmem(),
        scratch_shapes=[
            pltpu.VMEM((slots, tile, tile), BF16),
            pltpu.VMEM((places + 1, tile, tile), F32),
            pltpu.SemaphoreType.DMA((groups,)),
        ],
        compiler_params=params(32),
        cost_estimate=COST,
        name="densify",
    )(in_hbm(rows), in_hbm(cols), count, in_hbm(tiles))


def in_hbm(v):
    return pltpu.with_memory_space_constraint(v, pltpu.HBM)


def resident(dense):
    return pltpu.with_memory_space_constraint(dense, pltpu.VMEM)


def hold(arrays, after):
    n = len(arrays)
    outs = pl.pallas_call(
        lambda *refs: None,
        out_shape=tuple(jax.ShapeDtypeStruct(v.shape, v.dtype) for v in arrays),
        in_specs=[pl.BlockSpec(memory_space=pl.ANY)] * n + [vmem()],
        out_specs=(pl.BlockSpec(memory_space=pl.ANY),) * n,
        input_output_aliases={i: i for i in range(n)},
        compiler_params=params(),
        cost_estimate=COST,
        name="hold",
    )(*arrays, resident(after))
    return list(outs)


def forward_kernel(places, last, dense, *refs):
    n = len(places)
    xs, refs = refs[:n], refs[n:]
    n_col, side = dense.shape[1], dense.shape[2]
    outs = refs[-n_col:]
    for t in range(n_col):
        total = jnp.dot(dense[places[0], t], xs[0][...], preferred_element_type=F32)
        for j, x in zip(places[1:], xs[1:]):
            total = total + jnp.dot(dense[j, t], x[...], preferred_element_type=F32)
        if len(refs) > n_col:
            total = total + refs[t][...]
        outs[t][...] = total.astype(BF16) if last else total


def forward(dense, places, xs, totals, last):
    _, n_col, side, _ = dense.shape
    feats = xs[0].shape[1]
    shape = jax.ShapeDtypeStruct((side, feats), BF16 if last else F32)
    return pl.pallas_call(
        functools.partial(forward_kernel, places, last),
        out_shape=(shape,) * n_col,
        in_specs=[vmem()] * (1 + len(xs) + len(totals)),
        out_specs=(vmem(),) * n_col,
        compiler_params=params(),
        cost_estimate=COST,
        name="forward",
    )(resident(dense), *xs, *totals)


def elu(h):
    return jnp.where(h > 0, h, jnp.exp(jnp.minimum(h, 0.0)) - 1.0).astype(BF16)


def own_kernel(dense, piece, hidden, out, activated):
    activated[...] = elu(hidden[...])
    for j in range(dense.shape[0]):
        out[j] = jnp.dot(piece[...], dense[j, 0], preferred_element_type=F32)


def backward_own(dense, piece, hidden):
    n_src, _, side, _ = dense.shape
    return pl.pallas_call(
        own_kernel,
        out_shape=(
            pltpu.VMEM((n_src, piece.shape[0], side), F32),
            jax.ShapeDtypeStruct(hidden.shape, BF16),
        ),
        in_specs=[vmem()] * 3,
        out_specs=(vmem(),) * 2,
        compiler_params=params(),
        cost_estimate=COST,
        name="backward_own",
    )(resident(dense), piece, hidden)


def backward_kernel(dense, own, *refs):
    pieces, outs = refs[: dense.shape[1] - 1], refs[-2:]
    for j in range(dense.shape[0]):
        total = own[j]
        for t, piece in enumerate(pieces):
            total = total + jnp.dot(piece[...], dense[j, t + 1], preferred_element_type=F32)
        outs[j % 2][j // 2] = total.astype(BF16)


def backward(dense, own, pieces):
    n_src, n_col, side, _ = dense.shape
    feats = own.shape[1]
    return pl.pallas_call(
        backward_kernel,
        out_shape=(jax.ShapeDtypeStruct((n_src // 2, feats, side), BF16),) * 2,
        in_specs=[vmem()] * (1 + n_col),
        out_specs=(vmem(),) * 2,
        compiler_params=params(),
        cost_estimate=COST,
        name="backward",
    )(resident(dense), resident(own), *pieces)


def densify_stream_kernel(
    dims, rows, cols, count, tiles, out, buffer, head, following, sems
):
    n_z, n_col, blocks, slots, groups = dims
    chunk = pl.program_id(0)
    per_chunk = n_col * blocks * blocks
    per_group = slots // groups

    def copy(g):
        part = pl.ds(g * per_group, per_group)
        return pltpu.make_async_copy(tiles.at[part], buffer.at[part], sems.at[g])

    @pl.when(chunk == 0)
    def _():
        for g in range(groups):
            copy(g).start()

        def clear(i, carry):
            head[i] = slots
            return carry

        lax.fori_loop(0, 2 * n_z * per_chunk, clear, 0, unroll=8)
        following[slots] = slots
        buffer[slots] = jnp.zeros(buffer.shape[1:], buffer.dtype)

        def link(slot, carry):
            block_row, block_col = rows[0, 0, slot], cols[0, 0, slot]
            place = place_of((n_z, n_col, blocks), block_row, block_col)
            following[slot] = head[place]
            head[place] = slot
            return carry

        lax.fori_loop(0, count[0, 0], link, 0)
        for g in range(groups):
            copy(g).wait()

    tile = buffer.shape[1]

    def fill(i, carry):
        first = head[chunk * per_chunk + i]
        t = i // (blocks * blocks)
        a = pl.multiple_of((i // blocks) % blocks * tile, tile)
        b = pl.multiple_of(i % blocks * tile, tile)
        where = (0, t, pl.ds(a, tile), pl.ds(b, tile))
        out[where] = buffer[first]
        second = following[first]

        @pl.when(second != slots)
        def _():
            def more(state):
                slot, total = state
                return following[slot], total + buffer[slot].astype(F32)

            _, total = lax.while_loop(
                lambda state: state[0] != slots,
                more,
                (second, buffer[first].astype(F32)),
            )
            out[where] = total.astype(BF16)

        return carry

    lax.fori_loop(0, per_chunk, fill, 0)


def densify_stream(rows, cols, count, tiles, n_z, n_col, blocks):
    slots, tile = tiles.shape[0], tiles.shape[1]
    n_src = 2 * n_z
    groups = 8
    side = blocks * tile
    shape = (n_src, n_col, side, side)
    return pl.pallas_call(
        functools.partial(densify_stream_kernel, (n_z, n_col, blocks, slots, groups)),
        grid=(n_src,),
        out_shape=jax.ShapeDtypeStruct(shape, BF16),
        in_specs=[smem(), smem(), smem(), pl.BlockSpec(memory_space=pltpu.HBM)],
        out_specs=pl.BlockSpec((1, n_col, side, side), lambda j: (j, 0, 0, 0)),
        scratch_shapes=[
            pltpu.VMEM((slots + 1, tile, tile), BF16),
            pltpu.SMEM((n_src * n_col * blocks * blocks,), jnp.int32),
            pltpu.SMEM((slots + 1,), jnp.int32),
            pltpu.SemaphoreType.DMA((groups,)),
        ],
        compiler_params=params(32),
        cost_estimate=COST,
        name="densify",
    )(rows, cols, count, tiles)


def forward_stream_kernel(first, a, x0, x1, *rest):

    j = pl.program_id(1)

    @pl.when(j == 0)
    def _():
        value = jnp.dot(a[0, 0], x0[...], preferred_element_type=F32)
        if not first:
            value = value + rest[0][...]
        rest[-1][...] = value

    @pl.when(j == 1)
    def _():
        rest[-1][...] += jnp.dot(a[0, 0], x1[...], preferred_element_type=F32)


def forward_stream(dense, shift, x0, x1, total):
    _, n_col, side, _ = dense.shape
    feats = x0.shape[1]
    first = total is None
    block = pl.BlockSpec((side, feats), lambda t, j: (t, 0))
    return pl.pallas_call(
        functools.partial(forward_stream_kernel, first),
        grid=(n_col, 2),
        out_shape=jax.ShapeDtypeStruct((n_col * side, feats), F32),
        in_specs=[
            pl.BlockSpec((1, 1, side, side), lambda t, j: (2 * shift + j, t, 0, 0)),
            vmem(),
            vmem(),
        ]
        + ([] if first else [block]),
        out_specs=block,
        compiler_params=params(32),
        cost_estimate=COST,
        name="forward",
    )(dense, x0, x1, *([] if first else [total]))


def middle_kernel(n_col, weights, cot_own, cot_other, *refs):
    other = refs[:n_col]
    own = refs[n_col : 2 * n_col]
    spread, kept, agg, g_own, g_other = refs[2 * n_col :]
    half = cot_own.shape[1]
    f = lax.axis_index("feat")
    mine = pl.ds(pl.multiple_of(f * half, half), half)
    theirs = pl.ds(pl.multiple_of((1 - f) * half, half), half)

    def gather(parts):
        total = parts[0][...].astype(F32)
        for part in parts[1:]:
            total = total + part[...].astype(F32)
        return total.astype(BF16)

    top = jnp.concatenate([weights[mine, mine], weights[mine, theirs]], axis=1)
    low = jnp.concatenate([weights[theirs, mine], weights[theirs, theirs]], axis=1)
    agg_own = gather(own)
    agg[...] = agg_own
    both = jnp.concatenate([agg_own, gather(other)], axis=1)
    hidden = jnp.dot(both, jnp.concatenate([top, low], axis=0), preferred_element_type=F32)
    decay = jnp.exp(jnp.minimum(hidden, 0.0))
    cot = jnp.concatenate([cot_own[...], cot_other[...]], axis=1).astype(F32)
    g = (cot * decay).astype(BF16)
    spread[...] = lax.dot_general(
        top, g, (((1,), (1,)), ((), ())), preferred_element_type=F32
    ).astype(BF16)
    g_own[...] = g[:, :half]
    g_other[...] = g[:, half:]
    kept[...] = hidden[:, :half]


def middle(weights, cot_own, cot_other, own, other):
    nodes, half = cot_own.shape
    whole = weights.shape[1]
    n_col = len(own)
    return pl.pallas_call(
        functools.partial(middle_kernel, n_col),
        out_shape=(
            jax.ShapeDtypeStruct((half, nodes), BF16),
            jax.ShapeDtypeStruct((nodes, half), F32),
        )
        + (jax.ShapeDtypeStruct((nodes, half), BF16),) * 3,
        in_specs=[vmem()] * (3 + 2 * n_col),
        out_specs=(vmem(),) * 5,
        compiler_params=params(),
        cost_estimate=COST,
        name="middle",
    )(weights, cot_own, cot_other, *other, *own)


def weight_kernel(agg, g_own, g_other, keep, send, whole):
    half, rows = agg.shape[1], keep.shape[0]
    core, f = lax.axis_index("row") % 2, lax.axis_index("feat")
    turned = agg[...].astype(F32).T.astype(BF16)
    for columns, g in ((f * half, g_own), ((1 - f) * half, g_other)):
        columns = pl.ds(pl.multiple_of(columns, half), half)
        whole[:, columns] = jnp.dot(turned, g[...], preferred_element_type=F32)
        term = whole[:, columns].astype(BF16)
        first, second = term[:rows], term[rows:]
        keep[:, columns] = jnp.where(core == 0, first, second)
        send[:, columns] = jnp.where(core == 0, second, first)


def weight_term(agg, g_own, g_other):
    half = agg.shape[1]
    return pl.pallas_call(
        weight_kernel,
        out_shape=(jax.ShapeDtypeStruct((half // 2, 2 * half), BF16),) * 2
        + (pltpu.VMEM((half, 2 * half), F32),),
        in_specs=[vmem()] * 3,
        out_specs=(vmem(),) * 3,
        compiler_params=params(),
        cost_estimate=COST,
        name="weight_term",
    )(agg, g_own, g_other)


def assemble_kernel(scale, mine, theirs, out):
    rows = mine.shape[0]
    core = lax.axis_index("row") % 2
    own, other = mine[...].astype(F32) * scale, theirs[...].astype(F32) * scale
    out[:rows, :] = jnp.where(core == 0, own, other)
    out[rows:, :] = jnp.where(core == 0, other, own)


def assemble(scale, mine, theirs):
    rows, whole = mine.shape
    return pl.pallas_call(
        functools.partial(assemble_kernel, scale),
        out_shape=jax.ShapeDtypeStruct((2 * rows, whole), F32),
        in_specs=[vmem()] * 2,
        out_specs=vmem(),
        compiler_params=params(),
        cost_estimate=COST,
        name="assemble",
    )(mine, theirs)


def backward_stream_kernel(n_col, a, *refs):
    pieces, out = refs[:n_col], refs[n_col]
    total = jnp.dot(pieces[0][...], a[0, 0], preferred_element_type=F32)
    for t in range(1, n_col):
        total = total + jnp.dot(pieces[t][...], a[0, t], preferred_element_type=F32)
    out[0] = total.astype(BF16)


def backward_stream(dense, parity, pieces):
    n_src, n_col, side, _ = dense.shape
    feats = pieces[0].shape[0]
    n_z = n_src // 2
    return pl.pallas_call(
        functools.partial(backward_stream_kernel, n_col),
        grid=(n_z,),
        out_shape=jax.ShapeDtypeStruct((n_z, feats, side), BF16),
        in_specs=[pl.BlockSpec((1, n_col, side, side), lambda s: (2 * s + parity, 0, 0, 0))]
        + [vmem()] * n_col,
        out_specs=pl.BlockSpec((1, feats, side), lambda s: (s, 0, 0)),
        compiler_params=params(32),
        cost_estimate=COST,
        name="backward",
    )(dense, *pieces)


def add_kernel(a, b, *rest):
    rest[-1][...] = (a[...].astype(F32) + b[...].astype(F32)).astype(BF16)


def add(a, b, *after):
    return pl.pallas_call(
        add_kernel,
        out_shape=jax.ShapeDtypeStruct(a.shape, BF16),
        in_specs=[vmem()] * 2 + [pl.BlockSpec(memory_space=pl.ANY)] * len(after),
        out_specs=vmem(),
        compiler_params=params(),
        cost_estimate=COST,
        name="add",
    )(a, b, *after)


def pair_kernel(own, arrived, *outs):
    for s, out in enumerate(outs):
        out[...] = (own[s].astype(F32) + arrived[s].astype(F32)).astype(BF16)


def pair_sums(own, arrived):
    n_z, side, feats = own.shape
    return pl.pallas_call(
        pair_kernel,
        out_shape=(jax.ShapeDtypeStruct((side, feats), BF16),) * n_z,
        in_specs=[vmem()] * 2,
        out_specs=(vmem(),) * n_z,
        compiler_params=params(),
        cost_estimate=COST,
        name="pair_sums",
    )(own, arrived)


def turned_kernel(*refs):
    total = refs[0][...].astype(F32)
    for part in refs[1:-2]:
        total = total + part[...].astype(F32)
    refs[-1][...] = total.T.astype(BF16)


def turned_sum(parts, after):
    feats, nodes = parts[0].shape
    return pl.pallas_call(
        turned_kernel,
        out_shape=jax.ShapeDtypeStruct((nodes, feats), BF16),
        in_specs=[vmem()] * len(parts) + [pl.BlockSpec(memory_space=pl.ANY)],
        out_specs=vmem(),
        compiler_params=params(),
        cost_estimate=COST,
        name="turned_sum",
    )(*parts, after)


def shards(features, tile_rows, tile_cols, tile_count, tile_values, weights, cotangent):
    tile = tile_values.shape[-1]
    n_row, n_col = lax.axis_size("row"), lax.axis_size("col")
    n_z = n_row // 2
    nodes, half = features.shape
    blocks = nodes // tile
    node_total = nodes * n_row * n_col
    def sibling(v):
        return lax.ppermute(v, "row", [(i, i ^ 1) for i in range(n_row)])

    def along_z(v, s):
        return lax.ppermute(v, "row", [(i, i ^ (2 * s)) for i in range(n_row)])

    def other_feat(v):
        return lax.ppermute(v, "feat", [(0, 1), (1, 0)])

    def to_group(v, shift, flip):
        pairs = []
        for cc in range(n_col):
            for ff in range(2):
                pairs.append((2 * cc + ff, 2 * ((cc + shift) % n_col) + (ff ^ flip)))
        return lax.ppermute(v, ("col", "feat"), pairs)

    same = [features] + [along_z(features, s) for s in range(1, n_z)]
    cot_other = other_feat(cotangent)
    tiles = tile_values[0, 0]
    cell = (tile_rows, tile_cols, tile_count, tiles, n_z, n_col, blocks)
    if 2 * n_z * n_col * (blocks * tile) ** 2 <= 8 * MIB:
        dense = densify(*cell)
        totals = forward(dense, [0, 1], [features, sibling(features)], (), False)
        far = range(n_z - 1, 0, -1)
        *same, cot_other = hold([same[s] for s in far] + [cot_other], totals[0])
        same.reverse()
        cross = [sibling(v) for v in same]
        totals = forward(dense, [2 * s for s in range(1, n_z)], same, totals, False)
        parts = forward(dense, [2 * s + 1 for s in range(1, n_z)], cross, totals, True)

        def back_of(pieces, hidden):
            own, activated = backward_own(dense, pieces[0], hidden)
            return *backward(dense, own, pieces[1:]), activated

    else:
        cross = [sibling(v) for v in same]
        dense = densify_stream(*cell)
        total = None
        for s in range(n_z):
            total = forward_stream(dense, s, same[s], cross[s], total)
        parts = total.astype(BF16).reshape(n_col, nodes, half)

        def back_of(pieces, hidden):
            even, odd = (backward_stream(dense, k, pieces) for k in range(2))
            return even, odd, elu(hidden)

    other = [to_group(parts[t], -t, 1) for t in range(n_col - 1, -1, -1)]
    own = [parts[0]] + [to_group(parts[t], -t, 0) for t in range(1, n_col)]
    spread, hidden, *rest = middle(weights, cotangent, cot_other, own, other)
    pieces = [spread] + [
        lax.ppermute(spread, "col", [(i, (i + t) % n_col) for i in range(n_col)])
        for t in range(1, n_col)
    ]
    keep, send, weight_grad = weight_term(*rest)
    term = add(keep, sibling(send))
    even, odd, activated = back_of(pieces, hidden)
    term = add(term, along_z(term, 1), odd)
    (odd,) = hold([odd], term)
    arrived = sibling(odd)
    sums = pair_sums(even, arrived)
    if n_z > 2:
        term = add(term, along_z(term, 2), sums[0])
    order = sorted(range(1, n_z), key=lambda s: (s != n_z // 2, s))

    def finish(_, state):
        v = state[0]
        for step in range(2, n_z.bit_length() - 1):
            v = add(v, along_z(v, 1 << step))
        total = v.astype(F32)
        for t in range(1, n_col):
            total = total + lax.ppermute(
                v, "col", [(i, (i + t) % n_col) for i in range(n_col)]
            ).astype(F32)
        v = total.astype(BF16)
        return v, assemble(node_total ** (-0.5), v, sibling(v))

    once = lax.optimization_barrier(jnp.int32(1))
    _, weight_grad = lax.fori_loop(0, once, finish, (term, weight_grad))
    back = turned_sum([sums[0]] + [along_z(sums[s], s) for s in order], weight_grad)
    return (activated, back, weight_grad)


def solution(mesh):
    return jax.shard_map(
        shards,
        mesh=mesh,
        in_specs=(
            P(("col", "row"), "feat"),
            P("row", "col", None),
            P("row", "col", None),
            P("row", "col"),
            P("row", "col", None, None, None),
            P(),
            P(("row", "col"), "feat"),
        ),
        out_specs=(P(("row", "col"), "feat"), P(("col", "row"), "feat"), P("feat", None)),
        check_vma=False,
    )
```

```python
import functools

import jax
import jax.numpy as jnp
from jax import lax
from jax.experimental import pallas as pl
from jax.experimental.pallas import tpu as pltpu
from jax.sharding import PartitionSpec as P

F32 = jnp.float32
BF16 = jnp.bfloat16
MIB = 1024 * 1024
COST = pl.CostEstimate(flops=1, bytes_accessed=1, transcendentals=0)


def params(mib=16):
    return pltpu.CompilerParams(vmem_limit_bytes=mib * MIB)


def vmem():
    return pl.BlockSpec(memory_space=pltpu.VMEM)


def smem():
    return pl.BlockSpec(memory_space=pltpu.SMEM)


def place_of(dims, block_row, block_col):
    n_z, n_col, blocks = dims
    bits, low = blocks.bit_length() - 1, blocks - 1
    j = (block_col >> bits) ^ lax.axis_index("row")
    t = (lax.axis_index("col") - (block_row >> bits)) & (n_col - 1)
    return ((((j * n_col + t) << bits) | (block_row & low)) << bits) | (block_col & low)


def densify_kernel(dims, groups, rows, cols, count, tiles, out, buffer, total, sems):
    n_z, n_col, blocks = dims
    slots, tile = buffer.shape[0], buffer.shape[1]
    per_group = slots // groups
    places = total.shape[0] - 1
    live = count[0, 0]

    def copy(g):
        part = pl.ds(g * per_group, per_group)
        return pltpu.make_async_copy(tiles.at[part], buffer.at[part], sems.at[g])

    def each_group(action):
        for g in range(groups):

            @pl.when(g * per_group < live)
            def _():
                action(g)

    each_group(lambda g: copy(g).start())

    def clear(i, carry):
        total[i] = jnp.zeros((tile, tile), F32)
        return carry

    lax.fori_loop(0, places, clear, 0, unroll=4)

    def add_group(g):
        copy(g).wait()

        def add(i, carry):
            slot = g * per_group + i
            place = place_of(dims, rows[0, 0, slot], cols[0, 0, slot])
            place = jnp.where(slot < live, place, places)
            total[place] += buffer[slot].astype(F32)
            return carry

        lax.fori_loop(0, per_group, add, 0, unroll=8)

    each_group(add_group)

    def settle(j, carry):
        for t in range(n_col):
            for a in range(blocks):
                for b in range(blocks):
                    value = total[((j * n_col + t) * blocks + a) * blocks + b]
                    out[j, t, a * tile : (a + 1) * tile, b * tile : (b + 1) * tile] = value.astype(BF16)
        return carry

    lax.fori_loop(0, 2 * n_z, settle, 0)


def densify(rows, cols, count, tiles, n_z, n_col, blocks):
    slots, tile = tiles.shape[0], tiles.shape[1]
    n_src = 2 * n_z
    groups = 8
    side = blocks * tile
    places = n_src * n_col * blocks * blocks
    return pl.pallas_call(
        functools.partial(densify_kernel, (n_z, n_col, blocks), groups),
        out_shape=pltpu.VMEM((n_src, n_col, side, side), BF16),
        in_specs=[smem(), smem(), smem(), pl.BlockSpec(memory_space=pltpu.HBM)],
        out_specs=vmem(),
        scratch_shapes=[
            pltpu.VMEM((slots, tile, tile), BF16),
            pltpu.VMEM((places + 1, tile, tile), F32),
            pltpu.SemaphoreType.DMA((groups,)),
        ],
        compiler_params=params(32),
        cost_estimate=COST,
        name="densify",
    )(in_hbm(rows), in_hbm(cols), count, in_hbm(tiles))


def in_hbm(v):
    return pltpu.with_memory_space_constraint(v, pltpu.HBM)


def resident(dense):
    return pltpu.with_memory_space_constraint(dense, pltpu.VMEM)


def hold(arrays, after):
    n = len(arrays)
    outs = pl.pallas_call(
        lambda *refs: None,
        out_shape=tuple(jax.ShapeDtypeStruct(v.shape, v.dtype) for v in arrays),
        in_specs=[pl.BlockSpec(memory_space=pl.ANY)] * n + [vmem()],
        out_specs=(pl.BlockSpec(memory_space=pl.ANY),) * n,
        input_output_aliases={i: i for i in range(n)},
        compiler_params=params(),
        cost_estimate=COST,
        name="hold",
    )(*arrays, resident(after))
    return list(outs)


def forward_kernel(places, last, dense, *refs):
    n = len(places)
    xs, refs = refs[:n], refs[n:]
    n_col, side = dense.shape[1], dense.shape[2]
    outs = refs[-n_col:]
    for t in range(n_col):
        total = jnp.dot(dense[places[0], t], xs[0][...], preferred_element_type=F32)
        for j, x in zip(places[1:], xs[1:]):
            total = total + jnp.dot(dense[j, t], x[...], preferred_element_type=F32)
        if len(refs) > n_col:
            total = total + refs[t][...]
        outs[t][...] = total.astype(BF16) if last else total


def forward(dense, places, xs, totals, last):
    _, n_col, side, _ = dense.shape
    feats = xs[0].shape[1]
    shape = jax.ShapeDtypeStruct((side, feats), BF16 if last else F32)
    return pl.pallas_call(
        functools.partial(forward_kernel, places, last),
        out_shape=(shape,) * n_col,
        in_specs=[vmem()] * (1 + len(xs) + len(totals)),
        out_specs=(vmem(),) * n_col,
        compiler_params=params(),
        cost_estimate=COST,
        name="forward",
    )(resident(dense), *xs, *totals)


def elu(h):
    return jnp.where(h > 0, h, jnp.exp(jnp.minimum(h, 0.0)) - 1.0).astype(BF16)


def own_kernel(dense, piece, hidden, out, activated):
    activated[...] = elu(hidden[...])
    for j in range(dense.shape[0]):
        out[j] = jnp.dot(piece[...], dense[j, 0], preferred_element_type=F32)


def backward_own(dense, piece, hidden):
    n_src, _, side, _ = dense.shape
    return pl.pallas_call(
        own_kernel,
        out_shape=(
            pltpu.VMEM((n_src, piece.shape[0], side), F32),
            jax.ShapeDtypeStruct(hidden.shape, BF16),
        ),
        in_specs=[vmem()] * 3,
        out_specs=(vmem(),) * 2,
        compiler_params=params(),
        cost_estimate=COST,
        name="backward_own",
    )(resident(dense), piece, hidden)


def backward_kernel(dense, own, *refs):
    pieces, outs = refs[: dense.shape[1] - 1], refs[-2:]
    for j in range(dense.shape[0]):
        total = own[j]
        for t, piece in enumerate(pieces):
            total = total + jnp.dot(piece[...], dense[j, t + 1], preferred_element_type=F32)
        outs[j % 2][j // 2] = total.astype(BF16)


def backward(dense, own, pieces):
    n_src, n_col, side, _ = dense.shape
    feats = own.shape[1]
    return pl.pallas_call(
        backward_kernel,
        out_shape=(jax.ShapeDtypeStruct((n_src // 2, feats, side), BF16),) * 2,
        in_specs=[vmem()] * (1 + n_col),
        out_specs=(vmem(),) * 2,
        compiler_params=params(),
        cost_estimate=COST,
        name="backward",
    )(resident(dense), resident(own), *pieces)


def densify_stream_kernel(
    dims, rows, cols, count, tiles, out, buffer, head, following, sems
):
    n_z, n_col, blocks, slots, groups = dims
    chunk = pl.program_id(0)
    per_chunk = n_col * blocks * blocks
    per_group = slots // groups

    def copy(g):
        part = pl.ds(g * per_group, per_group)
        return pltpu.make_async_copy(tiles.at[part], buffer.at[part], sems.at[g])

    @pl.when(chunk == 0)
    def _():
        for g in range(groups):
            copy(g).start()

        def clear(i, carry):
            head[i] = slots
            return carry

        lax.fori_loop(0, 2 * n_z * per_chunk, clear, 0, unroll=8)
        following[slots] = slots
        buffer[slots] = jnp.zeros(buffer.shape[1:], buffer.dtype)

        def link(slot, carry):
            block_row, block_col = rows[0, 0, slot], cols[0, 0, slot]
            place = place_of((n_z, n_col, blocks), block_row, block_col)
            following[slot] = head[place]
            head[place] = slot
            return carry

        lax.fori_loop(0, count[0, 0], link, 0)
        for g in range(groups):
            copy(g).wait()

    tile = buffer.shape[1]

    def fill(i, carry):
        first = head[chunk * per_chunk + i]
        t = i // (blocks * blocks)
        a = pl.multiple_of((i // blocks) % blocks * tile, tile)
        b = pl.multiple_of(i % blocks * tile, tile)
        where = (0, t, pl.ds(a, tile), pl.ds(b, tile))
        out[where] = buffer[first]
        second = following[first]

        @pl.when(second != slots)
        def _():
            def more(state):
                slot, total = state
                return following[slot], total + buffer[slot].astype(F32)

            _, total = lax.while_loop(
                lambda state: state[0] != slots,
                more,
                (second, buffer[first].astype(F32)),
            )
            out[where] = total.astype(BF16)

        return carry

    lax.fori_loop(0, per_chunk, fill, 0)


def densify_stream(rows, cols, count, tiles, n_z, n_col, blocks):
    slots, tile = tiles.shape[0], tiles.shape[1]
    n_src = 2 * n_z
    groups = 8
    side = blocks * tile
    shape = (n_src, n_col, side, side)
    return pl.pallas_call(
        functools.partial(densify_stream_kernel, (n_z, n_col, blocks, slots, groups)),
        grid=(n_src,),
        out_shape=jax.ShapeDtypeStruct(shape, BF16),
        in_specs=[smem(), smem(), smem(), pl.BlockSpec(memory_space=pltpu.HBM)],
        out_specs=pl.BlockSpec((1, n_col, side, side), lambda j: (j, 0, 0, 0)),
        scratch_shapes=[
            pltpu.VMEM((slots + 1, tile, tile), BF16),
            pltpu.SMEM((n_src * n_col * blocks * blocks,), jnp.int32),
            pltpu.SMEM((slots + 1,), jnp.int32),
            pltpu.SemaphoreType.DMA((groups,)),
        ],
        compiler_params=params(32),
        cost_estimate=COST,
        name="densify",
    )(rows, cols, count, tiles)


def forward_stream_kernel(first, a, x0, x1, *rest):

    j = pl.program_id(1)

    @pl.when(j == 0)
    def _():
        value = jnp.dot(a[0, 0], x0[...], preferred_element_type=F32)
        if not first:
            value = value + rest[0][...]
        rest[-1][...] = value

    @pl.when(j == 1)
    def _():
        rest[-1][...] += jnp.dot(a[0, 0], x1[...], preferred_element_type=F32)


def forward_stream(dense, shift, x0, x1, total):
    _, n_col, side, _ = dense.shape
    feats = x0.shape[1]
    first = total is None
    block = pl.BlockSpec((side, feats), lambda t, j: (t, 0))
    return pl.pallas_call(
        functools.partial(forward_stream_kernel, first),
        grid=(n_col, 2),
        out_shape=jax.ShapeDtypeStruct((n_col * side, feats), F32),
        in_specs=[
            pl.BlockSpec((1, 1, side, side), lambda t, j: (2 * shift + j, t, 0, 0)),
            vmem(),
            vmem(),
        ]
        + ([] if first else [block]),
        out_specs=block,
        compiler_params=params(32),
        cost_estimate=COST,
        name="forward",
    )(dense, x0, x1, *([] if first else [total]))


def middle_kernel(n_col, weights, cot_own, cot_other, *refs):
    other = refs[:n_col]
    own = refs[n_col : 2 * n_col]
    spread, kept, agg, g_own, g_other = refs[2 * n_col :]
    half = cot_own.shape[1]
    f = lax.axis_index("feat")
    mine = pl.ds(pl.multiple_of(f * half, half), half)
    theirs = pl.ds(pl.multiple_of((1 - f) * half, half), half)

    def gather(parts):
        total = parts[0][...].astype(F32)
        for part in parts[1:]:
            total = total + part[...].astype(F32)
        return total.astype(BF16)

    top = jnp.concatenate([weights[mine, mine], weights[mine, theirs]], axis=1)
    low = jnp.concatenate([weights[theirs, mine], weights[theirs, theirs]], axis=1)
    agg_own = gather(own)
    agg[...] = agg_own
    both = jnp.concatenate([agg_own, gather(other)], axis=1)
    hidden = jnp.dot(both, jnp.concatenate([top, low], axis=0), preferred_element_type=F32)
    decay = jnp.exp(jnp.minimum(hidden, 0.0))
    cot = jnp.concatenate([cot_own[...], cot_other[...]], axis=1).astype(F32)
    g = (cot * decay).astype(BF16)
    spread[...] = lax.dot_general(
        top, g, (((1,), (1,)), ((), ())), preferred_element_type=F32
    ).astype(BF16)
    g_own[...] = g[:, :half]
    g_other[...] = g[:, half:]
    kept[...] = hidden[:, :half]


def middle(weights, cot_own, cot_other, own, other):
    nodes, half = cot_own.shape
    whole = weights.shape[1]
    n_col = len(own)
    return pl.pallas_call(
        functools.partial(middle_kernel, n_col),
        out_shape=(
            jax.ShapeDtypeStruct((half, nodes), BF16),
            jax.ShapeDtypeStruct((nodes, half), F32),
        )
        + (jax.ShapeDtypeStruct((nodes, half), BF16),) * 3,
        in_specs=[vmem()] * (3 + 2 * n_col),
        out_specs=(vmem(),) * 5,
        compiler_params=params(),
        cost_estimate=COST,
        name="middle",
    )(weights, cot_own, cot_other, *other, *own)


def weight_kernel(agg, g_own, g_other, out):
    half = agg.shape[1]
    f = lax.axis_index("feat")
    turned = agg[...].astype(F32).T.astype(BF16)
    for columns, g in ((f * half, g_own), ((1 - f) * half, g_other)):
        columns = pl.ds(pl.multiple_of(columns, half), half)
        out[:, columns] = jnp.dot(turned, g[...], preferred_element_type=F32).astype(BF16)


def weight_term(agg, g_own, g_other):
    half = agg.shape[1]
    return pl.pallas_call(
        weight_kernel,
        out_shape=jax.ShapeDtypeStruct((half, 2 * half), BF16),
        in_specs=[vmem()] * 3,
        out_specs=vmem(),
        compiler_params=params(),
        cost_estimate=COST,
        name="weight_term",
    )(agg, g_own, g_other)


def backward_stream_kernel(n_col, a, *refs):
    pieces, out = refs[:n_col], refs[n_col]
    total = jnp.dot(pieces[0][...], a[0, 0], preferred_element_type=F32)
    for t in range(1, n_col):
        total = total + jnp.dot(pieces[t][...], a[0, t], preferred_element_type=F32)
    out[0] = total.astype(BF16)


def backward_stream(dense, parity, pieces):
    n_src, n_col, side, _ = dense.shape
    feats = pieces[0].shape[0]
    n_z = n_src // 2
    return pl.pallas_call(
        functools.partial(backward_stream_kernel, n_col),
        grid=(n_z,),
        out_shape=jax.ShapeDtypeStruct((n_z, feats, side), BF16),
        in_specs=[pl.BlockSpec((1, n_col, side, side), lambda s: (2 * s + parity, 0, 0, 0))]
        + [vmem()] * n_col,
        out_specs=pl.BlockSpec((1, feats, side), lambda s: (s, 0, 0)),
        compiler_params=params(32),
        cost_estimate=COST,
        name="backward",
    )(dense, *pieces)


def add_kernel(a, b, *rest):
    rest[-1][...] = (a[...].astype(F32) + b[...].astype(F32)).astype(BF16)


def add(a, b, *after):
    return pl.pallas_call(
        add_kernel,
        out_shape=jax.ShapeDtypeStruct(a.shape, BF16),
        in_specs=[vmem()] * 2 + [pl.BlockSpec(memory_space=pl.ANY)] * len(after),
        out_specs=vmem(),
        compiler_params=params(),
        cost_estimate=COST,
        name="add",
    )(a, b, *after)


def pair_kernel(own, arrived, *outs):
    for s, out in enumerate(outs):
        out[...] = (own[s].astype(F32) + arrived[s].astype(F32)).astype(BF16)


def pair_sums(own, arrived):
    n_z, side, feats = own.shape
    return pl.pallas_call(
        pair_kernel,
        out_shape=(jax.ShapeDtypeStruct((side, feats), BF16),) * n_z,
        in_specs=[vmem()] * 2,
        out_specs=(vmem(),) * n_z,
        compiler_params=params(),
        cost_estimate=COST,
        name="pair_sums",
    )(own, arrived)


def turned_kernel(*refs):
    total = refs[0][...].astype(F32)
    for part in refs[1:-1]:
        total = total + part[...].astype(F32)
    refs[-1][...] = total.T.astype(BF16)


def turned_sum(parts):
    feats, nodes = parts[0].shape
    return pl.pallas_call(
        turned_kernel,
        out_shape=jax.ShapeDtypeStruct((nodes, feats), BF16),
        in_specs=[vmem()] * len(parts),
        out_specs=vmem(),
        compiler_params=params(),
        cost_estimate=COST,
        name="turned_sum",
    )(*parts)


def shards(features, tile_rows, tile_cols, tile_count, tile_values, weights, cotangent):
    tile = tile_values.shape[-1]
    n_row, n_col = lax.axis_size("row"), lax.axis_size("col")
    n_z = n_row // 2
    nodes, half = features.shape
    blocks = nodes // tile
    node_total = nodes * n_row * n_col

    def sibling(v):
        return lax.ppermute(v, "row", [(i, i ^ 1) for i in range(n_row)])

    def along_z(v, s):
        return lax.ppermute(v, "row", [(i, i ^ (2 * s)) for i in range(n_row)])

    def other_feat(v):
        return lax.ppermute(v, "feat", [(0, 1), (1, 0)])

    def to_group(v, shift, flip):
        pairs = []
        for cc in range(n_col):
            for ff in range(2):
                pairs.append((2 * cc + ff, 2 * ((cc + shift) % n_col) + (ff ^ flip)))
        return lax.ppermute(v, ("col", "feat"), pairs)

    same = [features] + [along_z(features, s) for s in range(1, n_z)]
    cot_other = other_feat(cotangent)
    tiles = tile_values[0, 0]
    cell = (tile_rows, tile_cols, tile_count, tiles, n_z, n_col, blocks)
    if 2 * n_z * n_col * (blocks * tile) ** 2 <= 8 * MIB:
        dense = densify(*cell)
        totals = forward(dense, [0, 1], [features, sibling(features)], (), False)
        *held, cot_other = hold([same[-1]] + same[1:-1] + [cot_other], totals[0])
        same = held[1:] + held[:1]
        cross = [sibling(v) for v in same]
        totals = forward(dense, [2 * s for s in range(1, n_z)], same, totals, False)
        parts = forward(dense, [2 * s + 1 for s in range(1, n_z)], cross, totals, True)

        def back_of(pieces, hidden):
            own, activated = backward_own(dense, pieces[0], hidden)
            return *backward(dense, own, pieces[1:]), activated

    else:
        cross = [sibling(v) for v in same]
        dense = densify_stream(*cell)
        total = None
        for s in range(n_z):
            total = forward_stream(dense, s, same[s], cross[s], total)
        parts = total.astype(BF16).reshape(n_col, nodes, half)

        def back_of(pieces, hidden):
            even, odd = (backward_stream(dense, k, pieces) for k in range(2))
            return even, odd, elu(hidden)

    other = [to_group(parts[t], -t, 1) for t in range(n_col - 1, -1, -1)]
    own = [parts[0]] + [to_group(parts[t], -t, 0) for t in range(1, n_col)]
    spread, hidden, *rest = middle(weights, cotangent, cot_other, own, other)
    pieces = [spread] + [
        lax.ppermute(spread, "col", [(i, (i + t) % n_col) for i in range(n_col)])
        for t in range(1, n_col)
    ]
    term = weight_term(*rest)
    even, odd, activated = back_of(pieces, hidden)
    term = add(term, along_z(term, 1), odd)
    (odd,) = hold([odd], term)
    arrived = sibling(odd)
    sums = pair_sums(even, arrived)
    if n_z > 2:
        term = add(term, along_z(term, 2), sums[0])
    order = sorted(range(1, n_z), key=lambda s: (s != n_z // 2, s))
    back = turned_sum([sums[0]] + [along_z(sums[s], s) for s in order])

    def finish(_, v):
        for step in range(2, n_z.bit_length() - 1):
            v = add(v, along_z(v, 1 << step))
        for step in range(n_col.bit_length() - 1):
            pairs = [(i, i ^ (1 << step)) for i in range(n_col)]
            v = add(v, lax.ppermute(v, "col", pairs))
        return add(v, sibling(v))

    once = lax.optimization_barrier(jnp.int32(1))
    whole = lax.fori_loop(0, once, finish, term)
    weight_grad = whole.astype(F32) * node_total ** (-0.5)
    return (activated, back, weight_grad)


def solution(mesh):
    return jax.shard_map(
        shards,
        mesh=mesh,
        in_specs=(
            P(("col", "row"), "feat"),
            P("row", "col", None),
            P("row", "col", None),
            P("row", "col"),
            P("row", "col", None, None, None),
            P(),
            P(("row", "col"), "feat"),
        ),
        out_specs=(P(("row", "col"), "feat"), P(("col", "row"), "feat"), P("feat", None)),
        check_vma=False,
    )
```

```python
import functools

import jax
import jax.numpy as jnp
from jax import lax
from jax.experimental import pallas as pl
from jax.experimental.pallas import tpu as pltpu
from jax.sharding import PartitionSpec as P

F32 = jnp.float32
BF16 = jnp.bfloat16
MIB = 1024 * 1024
COST = pl.CostEstimate(flops=1, bytes_accessed=1, transcendentals=0)


def params(mib=16):
    return pltpu.CompilerParams(vmem_limit_bytes=mib * MIB)


def vmem():
    return pl.BlockSpec(memory_space=pltpu.VMEM)


def smem():
    return pl.BlockSpec(memory_space=pltpu.SMEM)


def place_of(dims, block_row, block_col):
    n_z, n_col, blocks = dims
    bits, low = blocks.bit_length() - 1, blocks - 1
    j = (block_col >> bits) ^ lax.axis_index("row")
    t = (lax.axis_index("col") - (block_row >> bits)) & (n_col - 1)
    return ((((j * n_col + t) << bits) | (block_row & low)) << bits) | (block_col & low)


def densify_kernel(dims, groups, rows, cols, count, tiles, out, buffer, total, sems):
    n_z, n_col, blocks = dims
    slots, tile = buffer.shape[0], buffer.shape[1]
    per_group = slots // groups
    places = total.shape[0] - 1
    live = count[0, 0]

    def copy(g):
        part = pl.ds(g * per_group, per_group)
        return pltpu.make_async_copy(tiles.at[part], buffer.at[part], sems.at[g])

    def each_group(action):
        for g in range(groups):

            @pl.when(g * per_group < live)
            def _():
                action(g)

    each_group(lambda g: copy(g).start())

    def clear(i, carry):
        total[i] = jnp.zeros((tile, tile), F32)
        return carry

    lax.fori_loop(0, places, clear, 0, unroll=4)

    def add_group(g):
        copy(g).wait()

        def add(i, carry):
            slot = g * per_group + i
            place = place_of(dims, rows[0, 0, slot], cols[0, 0, slot])
            place = jnp.where(slot < live, place, places)
            total[place] += buffer[slot].astype(F32)
            return carry

        lax.fori_loop(0, per_group, add, 0, unroll=8)

    each_group(add_group)

    def settle(j, carry):
        for t in range(n_col):
            for a in range(blocks):
                for b in range(blocks):
                    value = total[((j * n_col + t) * blocks + a) * blocks + b]
                    out[j, t, a * tile : (a + 1) * tile, b * tile : (b + 1) * tile] = value.astype(BF16)
        return carry

    lax.fori_loop(0, 2 * n_z, settle, 0)


def densify(rows, cols, count, tiles, n_z, n_col, blocks):
    slots, tile = tiles.shape[0], tiles.shape[1]
    n_src = 2 * n_z
    groups = 8
    side = blocks * tile
    places = n_src * n_col * blocks * blocks
    return pl.pallas_call(
        functools.partial(densify_kernel, (n_z, n_col, blocks), groups),
        out_shape=pltpu.VMEM((n_src, n_col, side, side), BF16),
        in_specs=[smem(), smem(), smem(), pl.BlockSpec(memory_space=pltpu.HBM)],
        out_specs=vmem(),
        scratch_shapes=[
            pltpu.VMEM((slots, tile, tile), BF16),
            pltpu.VMEM((places + 1, tile, tile), F32),
            pltpu.SemaphoreType.DMA((groups,)),
        ],
        compiler_params=params(32),
        cost_estimate=COST,
        name="densify",
    )(in_hbm(rows), in_hbm(cols), count, in_hbm(tiles))


def in_hbm(v):
    return pltpu.with_memory_space_constraint(v, pltpu.HBM)


def resident(dense):
    return pltpu.with_memory_space_constraint(dense, pltpu.VMEM)


def hold(arrays, after):
    n = len(arrays)
    outs = pl.pallas_call(
        lambda *refs: None,
        out_shape=tuple(jax.ShapeDtypeStruct(v.shape, v.dtype) for v in arrays),
        in_specs=[pl.BlockSpec(memory_space=pl.ANY)] * n + [vmem()],
        out_specs=(pl.BlockSpec(memory_space=pl.ANY),) * n,
        input_output_aliases={i: i for i in range(n)},
        compiler_params=params(),
        cost_estimate=COST,
        name="hold",
    )(*arrays, resident(after))
    return list(outs)


def forward_kernel(places, last, dense, *refs):
    n = len(places)
    xs, refs = refs[:n], refs[n:]
    n_col, side = dense.shape[1], dense.shape[2]
    outs = refs[-n_col:]
    for t in range(n_col):
        total = jnp.dot(dense[places[0], t], xs[0][...], preferred_element_type=F32)
        for j, x in zip(places[1:], xs[1:]):
            total = total + jnp.dot(dense[j, t], x[...], preferred_element_type=F32)
        if len(refs) > n_col:
            total = total + refs[t][...]
        outs[t][...] = total.astype(BF16) if last else total


def forward(dense, places, xs, totals, last):
    _, n_col, side, _ = dense.shape
    feats = xs[0].shape[1]
    shape = jax.ShapeDtypeStruct((side, feats), BF16 if last else F32)
    return pl.pallas_call(
        functools.partial(forward_kernel, places, last),
        out_shape=(shape,) * n_col,
        in_specs=[vmem()] * (1 + len(xs) + len(totals)),
        out_specs=(vmem(),) * n_col,
        compiler_params=params(),
        cost_estimate=COST,
        name="forward",
    )(resident(dense), *xs, *totals)


def elu(h):
    return jnp.where(h > 0, h, jnp.exp(jnp.minimum(h, 0.0)) - 1.0).astype(BF16)


def own_kernel(dense, piece, hidden, out, activated):
    activated[...] = elu(hidden[...])
    for j in range(dense.shape[0]):
        out[j] = jnp.dot(piece[...], dense[j, 0], preferred_element_type=F32)


def backward_own(dense, piece, hidden):
    n_src, _, side, _ = dense.shape
    return pl.pallas_call(
        own_kernel,
        out_shape=(
            pltpu.VMEM((n_src, piece.shape[0], side), F32),
            jax.ShapeDtypeStruct(hidden.shape, BF16),
        ),
        in_specs=[vmem()] * 3,
        out_specs=(vmem(),) * 2,
        compiler_params=params(),
        cost_estimate=COST,
        name="backward_own",
    )(resident(dense), piece, hidden)


def backward_kernel(dense, own, *refs):
    pieces, outs = refs[: dense.shape[1] - 1], refs[-4:]
    for j in range(dense.shape[0]):
        total = own[j]
        for t, piece in enumerate(pieces):
            total = total + jnp.dot(piece[...], dense[j, t + 1], preferred_element_type=F32)
        if j < 2:
            outs[j][...] = total.astype(BF16)
        else:
            outs[2 + j % 2][j // 2 - 1] = total.astype(BF16)


def backward(dense, own, pieces):
    n_src, n_col, side, _ = dense.shape
    feats = own.shape[1]
    return pl.pallas_call(
        backward_kernel,
        out_shape=(jax.ShapeDtypeStruct((feats, side), BF16),) * 2
        + (jax.ShapeDtypeStruct((n_src // 2 - 1, feats, side), BF16),) * 2,
        in_specs=[vmem()] * (1 + n_col),
        out_specs=(vmem(),) * 4,
        compiler_params=params(),
        cost_estimate=COST,
        name="backward",
    )(resident(dense), resident(own), *pieces)


def densify_stream_kernel(
    dims, rows, cols, count, tiles, out, buffer, head, following, sems
):
    n_z, n_col, blocks, slots, groups = dims
    chunk = pl.program_id(0)
    per_chunk = n_col * blocks * blocks
    per_group = slots // groups

    def copy(g):
        part = pl.ds(g * per_group, per_group)
        return pltpu.make_async_copy(tiles.at[part], buffer.at[part], sems.at[g])

    @pl.when(chunk == 0)
    def _():
        for g in range(groups):
            copy(g).start()

        def clear(i, carry):
            head[i] = slots
            return carry

        lax.fori_loop(0, 2 * n_z * per_chunk, clear, 0, unroll=8)
        following[slots] = slots
        buffer[slots] = jnp.zeros(buffer.shape[1:], buffer.dtype)

        def link(slot, carry):
            block_row, block_col = rows[0, 0, slot], cols[0, 0, slot]
            place = place_of((n_z, n_col, blocks), block_row, block_col)
            following[slot] = head[place]
            head[place] = slot
            return carry

        lax.fori_loop(0, count[0, 0], link, 0)
        for g in range(groups):
            copy(g).wait()

    tile = buffer.shape[1]

    def fill(i, carry):
        first = head[chunk * per_chunk + i]
        t = i // (blocks * blocks)
        a = pl.multiple_of((i // blocks) % blocks * tile, tile)
        b = pl.multiple_of(i % blocks * tile, tile)
        where = (0, t, pl.ds(a, tile), pl.ds(b, tile))
        out[where] = buffer[first]
        second = following[first]

        @pl.when(second != slots)
        def _():
            def more(state):
                slot, total = state
                return following[slot], total + buffer[slot].astype(F32)

            _, total = lax.while_loop(
                lambda state: state[0] != slots,
                more,
                (second, buffer[first].astype(F32)),
            )
            out[where] = total.astype(BF16)

        return carry

    lax.fori_loop(0, per_chunk, fill, 0)


def densify_stream(rows, cols, count, tiles, n_z, n_col, blocks):
    slots, tile = tiles.shape[0], tiles.shape[1]
    n_src = 2 * n_z
    groups = 8
    side = blocks * tile
    shape = (n_src, n_col, side, side)
    return pl.pallas_call(
        functools.partial(densify_stream_kernel, (n_z, n_col, blocks, slots, groups)),
        grid=(n_src,),
        out_shape=jax.ShapeDtypeStruct(shape, BF16),
        in_specs=[smem(), smem(), smem(), pl.BlockSpec(memory_space=pltpu.HBM)],
        out_specs=pl.BlockSpec((1, n_col, side, side), lambda j: (j, 0, 0, 0)),
        scratch_shapes=[
            pltpu.VMEM((slots + 1, tile, tile), BF16),
            pltpu.SMEM((n_src * n_col * blocks * blocks,), jnp.int32),
            pltpu.SMEM((slots + 1,), jnp.int32),
            pltpu.SemaphoreType.DMA((groups,)),
        ],
        compiler_params=params(32),
        cost_estimate=COST,
        name="densify",
    )(rows, cols, count, tiles)


def forward_stream_kernel(first, a, x0, x1, *rest):

    j = pl.program_id(1)

    @pl.when(j == 0)
    def _():
        value = jnp.dot(a[0, 0], x0[...], preferred_element_type=F32)
        if not first:
            value = value + rest[0][...]
        rest[-1][...] = value

    @pl.when(j == 1)
    def _():
        rest[-1][...] += jnp.dot(a[0, 0], x1[...], preferred_element_type=F32)


def forward_stream(dense, shift, x0, x1, total):
    _, n_col, side, _ = dense.shape
    feats = x0.shape[1]
    first = total is None
    block = pl.BlockSpec((side, feats), lambda t, j: (t, 0))
    return pl.pallas_call(
        functools.partial(forward_stream_kernel, first),
        grid=(n_col, 2),
        out_shape=jax.ShapeDtypeStruct((n_col * side, feats), F32),
        in_specs=[
            pl.BlockSpec((1, 1, side, side), lambda t, j: (2 * shift + j, t, 0, 0)),
            vmem(),
            vmem(),
        ]
        + ([] if first else [block]),
        out_specs=block,
        compiler_params=params(32),
        cost_estimate=COST,
        name="forward",
    )(dense, x0, x1, *([] if first else [total]))


def middle_kernel(n_col, weights, cot_own, cot_other, *refs):
    other = refs[:n_col]
    own = refs[n_col : 2 * n_col]
    spread, kept, agg, g_own, g_other = refs[2 * n_col :]
    half = cot_own.shape[1]
    f = lax.axis_index("feat")
    mine = pl.ds(pl.multiple_of(f * half, half), half)
    theirs = pl.ds(pl.multiple_of((1 - f) * half, half), half)

    def gather(parts):
        total = parts[0][...].astype(F32)
        for part in parts[1:]:
            total = total + part[...].astype(F32)
        return total.astype(BF16)

    top = jnp.concatenate([weights[mine, mine], weights[mine, theirs]], axis=1)
    low = jnp.concatenate([weights[theirs, mine], weights[theirs, theirs]], axis=1)
    agg_own = gather(own)
    agg[...] = agg_own
    both = jnp.concatenate([agg_own, gather(other)], axis=1)
    hidden = jnp.dot(both, jnp.concatenate([top, low], axis=0), preferred_element_type=F32)
    decay = jnp.exp(jnp.minimum(hidden, 0.0))
    cot = jnp.concatenate([cot_own[...], cot_other[...]], axis=1).astype(F32)
    g = (cot * decay).astype(BF16)
    spread[...] = lax.dot_general(
        top, g, (((1,), (1,)), ((), ())), preferred_element_type=F32
    ).astype(BF16)
    g_own[...] = g[:, :half]
    g_other[...] = g[:, half:]
    kept[...] = hidden[:, :half]


def middle(weights, cot_own, cot_other, own, other):
    nodes, half = cot_own.shape
    whole = weights.shape[1]
    n_col = len(own)
    return pl.pallas_call(
        functools.partial(middle_kernel, n_col),
        out_shape=(
            jax.ShapeDtypeStruct((half, nodes), BF16),
            jax.ShapeDtypeStruct((nodes, half), F32),
        )
        + (jax.ShapeDtypeStruct((nodes, half), BF16),) * 3,
        in_specs=[vmem()] * (3 + 2 * n_col),
        out_specs=(vmem(),) * 5,
        compiler_params=params(),
        cost_estimate=COST,
        name="middle",
    )(weights, cot_own, cot_other, *other, *own)


def weight_kernel(agg, g_own, g_other, out):
    half = agg.shape[1]
    f = lax.axis_index("feat")
    turned = agg[...].astype(F32).T.astype(BF16)
    for columns, g in ((f * half, g_own), ((1 - f) * half, g_other)):
        columns = pl.ds(pl.multiple_of(columns, half), half)
        out[:, columns] = jnp.dot(turned, g[...], preferred_element_type=F32).astype(BF16)


def weight_term(agg, g_own, g_other):
    half = agg.shape[1]
    return pl.pallas_call(
        weight_kernel,
        out_shape=jax.ShapeDtypeStruct((half, 2 * half), BF16),
        in_specs=[vmem()] * 3,
        out_specs=vmem(),
        compiler_params=params(),
        cost_estimate=COST,
        name="weight_term",
    )(agg, g_own, g_other)


def backward_stream_kernel(n_col, a, *refs):
    pieces, out = refs[:n_col], refs[n_col]
    total = jnp.dot(pieces[0][...], a[0, 0], preferred_element_type=F32)
    for t in range(1, n_col):
        total = total + jnp.dot(pieces[t][...], a[0, t], preferred_element_type=F32)
    out[0] = total.astype(BF16)


def backward_stream(dense, parity, pieces):
    n_src, n_col, side, _ = dense.shape
    feats = pieces[0].shape[0]
    n_z = n_src // 2
    return pl.pallas_call(
        functools.partial(backward_stream_kernel, n_col),
        grid=(n_z,),
        out_shape=jax.ShapeDtypeStruct((n_z, feats, side), BF16),
        in_specs=[pl.BlockSpec((1, n_col, side, side), lambda s: (2 * s + parity, 0, 0, 0))]
        + [vmem()] * n_col,
        out_specs=pl.BlockSpec((1, feats, side), lambda s: (s, 0, 0)),
        compiler_params=params(32),
        cost_estimate=COST,
        name="backward",
    )(dense, *pieces)


def add_kernel(a, b, *rest):
    rest[-1][...] = (a[...].astype(F32) + b[...].astype(F32)).astype(BF16)


def add(a, b, *after):
    return pl.pallas_call(
        add_kernel,
        out_shape=jax.ShapeDtypeStruct(a.shape, BF16),
        in_specs=[vmem()] * 2 + [pl.BlockSpec(memory_space=pl.ANY)] * len(after),
        out_specs=vmem(),
        compiler_params=params(),
        cost_estimate=COST,
        name="add",
    )(a, b, *after)


def pair_kernel(own, arrived, *outs):
    for s, out in enumerate(outs):
        out[...] = (own[s].astype(F32) + arrived[s].astype(F32)).astype(BF16)


def pair_sums(own, arrived):
    n_z, side, feats = own.shape
    return pl.pallas_call(
        pair_kernel,
        out_shape=(jax.ShapeDtypeStruct((side, feats), BF16),) * n_z,
        in_specs=[vmem()] * 2,
        out_specs=(vmem(),) * n_z,
        compiler_params=params(),
        cost_estimate=COST,
        name="pair_sums",
    )(own, arrived)


def turned_kernel(*refs):
    total = refs[0][...].astype(F32)
    for part in refs[1:-1]:
        total = total + part[...].astype(F32)
    refs[-1][...] = total.T.astype(BF16)


def turned_sum(parts):
    feats, nodes = parts[0].shape
    return pl.pallas_call(
        turned_kernel,
        out_shape=jax.ShapeDtypeStruct((nodes, feats), BF16),
        in_specs=[vmem()] * len(parts),
        out_specs=vmem(),
        compiler_params=params(),
        cost_estimate=COST,
        name="turned_sum",
    )(*parts)


def shards(features, tile_rows, tile_cols, tile_count, tile_values, weights, cotangent):
    tile = tile_values.shape[-1]
    n_row, n_col = lax.axis_size("row"), lax.axis_size("col")
    n_z = n_row // 2
    nodes, half = features.shape
    blocks = nodes // tile
    node_total = nodes * n_row * n_col

    def sibling(v):
        return lax.ppermute(v, "row", [(i, i ^ 1) for i in range(n_row)])

    def along_z(v, s):
        return lax.ppermute(v, "row", [(i, i ^ (2 * s)) for i in range(n_row)])

    def other_feat(v):
        return lax.ppermute(v, "feat", [(0, 1), (1, 0)])

    def to_group(v, shift, flip):
        pairs = []
        for cc in range(n_col):
            for ff in range(2):
                pairs.append((2 * cc + ff, 2 * ((cc + shift) % n_col) + (ff ^ flip)))
        return lax.ppermute(v, ("col", "feat"), pairs)

    same = [features] + [along_z(features, s) for s in range(1, n_z)]
    cot_other = other_feat(cotangent)
    tiles = tile_values[0, 0]
    cell = (tile_rows, tile_cols, tile_count, tiles, n_z, n_col, blocks)
    if 2 * n_z * n_col * (blocks * tile) ** 2 <= 8 * MIB:
        dense = densify(*cell)
        totals = forward(dense, [0, 1], [features, sibling(features)], (), False)
        *held, cot_other = hold([same[-1]] + same[1:-1] + [cot_other], totals[0])
        same = held[1:] + held[:1]
        cross = [sibling(v) for v in same]
        totals = forward(dense, [2 * s for s in range(1, n_z)], same, totals, False)
        parts = forward(dense, [2 * s + 1 for s in range(1, n_z)], cross, totals, True)

        def back_of(pieces, hidden):
            own, activated = backward_own(dense, pieces[0], hidden)
            return *backward(dense, own, pieces[1:]), activated

    else:
        cross = [sibling(v) for v in same]
        dense = densify_stream(*cell)
        total = None
        for s in range(n_z):
            total = forward_stream(dense, s, same[s], cross[s], total)
        parts = total.astype(BF16).reshape(n_col, nodes, half)

        def back_of(pieces, hidden):
            even, odd = (backward_stream(dense, k, pieces) for k in range(2))
            return even[0], odd[0], even[1:], odd[1:], elu(hidden)

    other = [to_group(parts[t], -t, 1) for t in range(n_col - 1, -1, -1)]
    own = [parts[0]] + [to_group(parts[t], -t, 0) for t in range(1, n_col)]
    spread, hidden, *rest = middle(weights, cotangent, cot_other, own, other)
    pieces = [spread] + [
        lax.ppermute(spread, "col", [(i, (i + t) % n_col) for i in range(n_col)])
        for t in range(1, n_col)
    ]
    term = weight_term(*rest)
    here, there, even, odd, activated = back_of(pieces, hidden)
    term = add(term, along_z(term, 1), odd)
    (odd,) = hold([odd], term)
    sums = pair_sums(even, sibling(odd))
    if n_z > 2:
        term = add(term, along_z(term, 2), sums[0])
    order = sorted(range(1, n_z), key=lambda s: (s != n_z // 2, s))
    back = turned_sum([here, sibling(there)] + [along_z(sums[s - 1], s) for s in order])

    def finish(_, v):
        for step in range(2, n_z.bit_length() - 1):
            v = add(v, along_z(v, 1 << step))
        for step in range(n_col.bit_length() - 1):
            pairs = [(i, i ^ (1 << step)) for i in range(n_col)]
            v = add(v, lax.ppermute(v, "col", pairs))
        return add(v, sibling(v))

    once = lax.optimization_barrier(jnp.int32(1))
    whole = lax.fori_loop(0, once, finish, term)
    weight_grad = whole.astype(F32) * node_total ** (-0.5)
    return (activated, back, weight_grad)


def solution(mesh):
    return jax.shard_map(
        shards,
        mesh=mesh,
        in_specs=(
            P(("col", "row"), "feat"),
            P("row", "col", None),
            P("row", "col", None),
            P("row", "col"),
            P("row", "col", None, None, None),
            P(),
            P(("row", "col"), "feat"),
        ),
        out_specs=(P(("row", "col"), "feat"), P(("col", "row"), "feat"), P("feat", None)),
        check_vma=False,
    )
```

```python
import functools

import jax
import jax.numpy as jnp
from jax import lax
from jax.experimental import pallas as pl
from jax.experimental.pallas import tpu as pltpu
from jax.sharding import PartitionSpec as P

F32 = jnp.float32
BF16 = jnp.bfloat16
MIB = 1024 * 1024
COST = pl.CostEstimate(flops=1, bytes_accessed=1, transcendentals=0)


def params(mib=16):
    return pltpu.CompilerParams(vmem_limit_bytes=mib * MIB)


def vmem():
    return pl.BlockSpec(memory_space=pltpu.VMEM)


def smem():
    return pl.BlockSpec(memory_space=pltpu.SMEM)


def place_of(dims, block_row, block_col):
    n_z, n_col, blocks = dims
    bits, low = blocks.bit_length() - 1, blocks - 1
    j = (block_col >> bits) ^ lax.axis_index("row")
    t = (lax.axis_index("col") - (block_row >> bits)) & (n_col - 1)
    return ((((j * n_col + t) << bits) | (block_row & low)) << bits) | (block_col & low)


def densify_kernel(dims, groups, rows, cols, count, tiles, out, buffer, total, sems):
    n_z, n_col, blocks = dims
    slots, tile = buffer.shape[0], buffer.shape[1]
    per_group = slots // groups
    places = total.shape[0] - 1
    live = count[0, 0]

    def copy(g):
        part = pl.ds(g * per_group, per_group)
        return pltpu.make_async_copy(tiles.at[part], buffer.at[part], sems.at[g])

    def each_group(action):
        for g in range(groups):

            @pl.when(g * per_group < live)
            def _():
                action(g)

    each_group(lambda g: copy(g).start())

    def clear(i, carry):
        total[i] = jnp.zeros((tile, tile), F32)
        return carry

    lax.fori_loop(0, places, clear, 0, unroll=4)

    def add_group(g):
        copy(g).wait()

        def add(i, carry):
            slot = g * per_group + i
            place = place_of(dims, rows[0, 0, slot], cols[0, 0, slot])
            place = jnp.where(slot < live, place, places)
            total[place] += buffer[slot].astype(F32)
            return carry

        lax.fori_loop(0, per_group, add, 0, unroll=8)

    each_group(add_group)

    def settle(j, carry):
        for t in range(n_col):
            for a in range(blocks):
                for b in range(blocks):
                    value = total[((j * n_col + t) * blocks + a) * blocks + b]
                    out[j, t, a * tile : (a + 1) * tile, b * tile : (b + 1) * tile] = value.astype(BF16)
        return carry

    lax.fori_loop(0, 2 * n_z, settle, 0)


def densify(rows, cols, count, tiles, n_z, n_col, blocks):
    slots, tile = tiles.shape[0], tiles.shape[1]
    n_src = 2 * n_z
    groups = 8
    side = blocks * tile
    places = n_src * n_col * blocks * blocks
    return pl.pallas_call(
        functools.partial(densify_kernel, (n_z, n_col, blocks), groups),
        out_shape=pltpu.VMEM((n_src, n_col, side, side), BF16),
        in_specs=[smem(), smem(), smem(), pl.BlockSpec(memory_space=pltpu.HBM)],
        out_specs=vmem(),
        scratch_shapes=[
            pltpu.VMEM((slots, tile, tile), BF16),
            pltpu.VMEM((places + 1, tile, tile), F32),
            pltpu.SemaphoreType.DMA((groups,)),
        ],
        compiler_params=params(32),
        cost_estimate=COST,
        name="densify",
    )(in_hbm(rows), in_hbm(cols), count, in_hbm(tiles))


def in_hbm(v):
    return pltpu.with_memory_space_constraint(v, pltpu.HBM)


def resident(dense):
    return pltpu.with_memory_space_constraint(dense, pltpu.VMEM)


def hold(arrays, after):
    n = len(arrays)
    outs = pl.pallas_call(
        lambda *refs: None,
        out_shape=tuple(jax.ShapeDtypeStruct(v.shape, v.dtype) for v in arrays),
        in_specs=[pl.BlockSpec(memory_space=pl.ANY)] * n + [vmem()],
        out_specs=(pl.BlockSpec(memory_space=pl.ANY),) * n,
        input_output_aliases={i: i for i in range(n)},
        compiler_params=params(),
        cost_estimate=COST,
        name="hold",
    )(*arrays, resident(after))
    return list(outs)


def forward_kernel(places, last, dense, *refs):
    n = len(places)
    xs, refs = refs[:n], refs[n:]
    n_col, side = dense.shape[1], dense.shape[2]
    outs = refs[-n_col:]
    for t in range(n_col):
        total = jnp.dot(dense[places[0], t], xs[0][...], preferred_element_type=F32)
        for j, x in zip(places[1:], xs[1:]):
            total = total + jnp.dot(dense[j, t], x[...], preferred_element_type=F32)
        if len(refs) > n_col:
            total = total + refs[t][...]
        outs[t][...] = total.astype(BF16) if last else total


def forward(dense, places, xs, totals, last):
    _, n_col, side, _ = dense.shape
    feats = xs[0].shape[1]
    shape = jax.ShapeDtypeStruct((side, feats), BF16 if last else F32)
    return pl.pallas_call(
        functools.partial(forward_kernel, places, last),
        out_shape=(shape,) * n_col,
        in_specs=[vmem()] * (1 + len(xs) + len(totals)),
        out_specs=(vmem(),) * n_col,
        compiler_params=params(),
        cost_estimate=COST,
        name="forward",
    )(resident(dense), *xs, *totals)


def elu(h):
    return jnp.where(h > 0, h, jnp.exp(jnp.minimum(h, 0.0)) - 1.0).astype(BF16)


def own_kernel(dense, piece, hidden, out, activated):
    activated[...] = elu(hidden[...])
    for j in range(dense.shape[0]):
        out[j] = jnp.dot(piece[...], dense[j, 0], preferred_element_type=F32)


def backward_own(dense, piece, hidden):
    n_src, _, side, _ = dense.shape
    return pl.pallas_call(
        own_kernel,
        out_shape=(
            pltpu.VMEM((n_src, piece.shape[0], side), F32),
            jax.ShapeDtypeStruct(hidden.shape, BF16),
        ),
        in_specs=[vmem()] * 3,
        out_specs=(vmem(),) * 2,
        compiler_params=params(),
        cost_estimate=COST,
        name="backward_own",
    )(resident(dense), piece, hidden)


def backward_kernel(dense, own, *refs):
    pieces, outs = refs[: dense.shape[1] - 1], refs[-4:]
    for j in range(dense.shape[0]):
        total = own[j]
        for t, piece in enumerate(pieces):
            total = total + jnp.dot(piece[...], dense[j, t + 1], preferred_element_type=F32)
        if j < 2:
            outs[j][...] = total.astype(BF16)
        else:
            outs[2 + j % 2][j // 2 - 1] = total.astype(BF16)


def backward(dense, own, pieces):
    n_src, n_col, side, _ = dense.shape
    feats = own.shape[1]
    return pl.pallas_call(
        backward_kernel,
        out_shape=(jax.ShapeDtypeStruct((feats, side), BF16),) * 2
        + (jax.ShapeDtypeStruct((n_src // 2 - 1, feats, side), BF16),) * 2,
        in_specs=[vmem()] * (1 + n_col),
        out_specs=(vmem(),) * 4,
        compiler_params=params(),
        cost_estimate=COST,
        name="backward",
    )(resident(dense), resident(own), *pieces)


def densify_stream_kernel(
    dims, rows, cols, count, tiles, out, buffer, head, following, sems
):
    n_z, n_col, blocks, slots, groups = dims
    chunk = pl.program_id(0)
    per_chunk = n_col * blocks * blocks
    per_group = slots // groups

    def copy(g):
        part = pl.ds(g * per_group, per_group)
        return pltpu.make_async_copy(tiles.at[part], buffer.at[part], sems.at[g])

    @pl.when(chunk == 0)
    def _():
        for g in range(groups):
            copy(g).start()

        def clear(i, carry):
            head[i] = slots
            return carry

        lax.fori_loop(0, 2 * n_z * per_chunk, clear, 0, unroll=8)
        following[slots] = slots
        buffer[slots] = jnp.zeros(buffer.shape[1:], buffer.dtype)

        def link(slot, carry):
            block_row, block_col = rows[0, 0, slot], cols[0, 0, slot]
            place = place_of((n_z, n_col, blocks), block_row, block_col)
            following[slot] = head[place]
            head[place] = slot
            return carry

        lax.fori_loop(0, count[0, 0], link, 0)
        for g in range(groups):
            copy(g).wait()

    tile = buffer.shape[1]

    def fill(i, carry):
        first = head[chunk * per_chunk + i]
        t = i // (blocks * blocks)
        a = pl.multiple_of((i // blocks) % blocks * tile, tile)
        b = pl.multiple_of(i % blocks * tile, tile)
        where = (0, t, pl.ds(a, tile), pl.ds(b, tile))
        out[where] = buffer[first]
        second = following[first]

        @pl.when(second != slots)
        def _():
            def more(state):
                slot, total = state
                return following[slot], total + buffer[slot].astype(F32)

            _, total = lax.while_loop(
                lambda state: state[0] != slots,
                more,
                (second, buffer[first].astype(F32)),
            )
            out[where] = total.astype(BF16)

        return carry

    lax.fori_loop(0, per_chunk, fill, 0)


def densify_stream(rows, cols, count, tiles, n_z, n_col, blocks):
    slots, tile = tiles.shape[0], tiles.shape[1]
    n_src = 2 * n_z
    groups = 8
    side = blocks * tile
    shape = (n_src, n_col, side, side)
    return pl.pallas_call(
        functools.partial(densify_stream_kernel, (n_z, n_col, blocks, slots, groups)),
        grid=(n_src,),
        out_shape=jax.ShapeDtypeStruct(shape, BF16),
        in_specs=[smem(), smem(), smem(), pl.BlockSpec(memory_space=pltpu.HBM)],
        out_specs=pl.BlockSpec((1, n_col, side, side), lambda j: (j, 0, 0, 0)),
        scratch_shapes=[
            pltpu.VMEM((slots + 1, tile, tile), BF16),
            pltpu.SMEM((n_src * n_col * blocks * blocks,), jnp.int32),
            pltpu.SMEM((slots + 1,), jnp.int32),
            pltpu.SemaphoreType.DMA((groups,)),
        ],
        compiler_params=params(32),
        cost_estimate=COST,
        name="densify",
    )(rows, cols, count, tiles)


def forward_stream_kernel(first, a, x0, x1, *rest):

    j = pl.program_id(1)

    @pl.when(j == 0)
    def _():
        value = jnp.dot(a[0, 0], x0[...], preferred_element_type=F32)
        if not first:
            value = value + rest[0][...]
        rest[-1][...] = value

    @pl.when(j == 1)
    def _():
        rest[-1][...] += jnp.dot(a[0, 0], x1[...], preferred_element_type=F32)


def forward_stream(dense, shift, x0, x1, total):
    _, n_col, side, _ = dense.shape
    feats = x0.shape[1]
    first = total is None
    block = pl.BlockSpec((side, feats), lambda t, j: (t, 0))
    return pl.pallas_call(
        functools.partial(forward_stream_kernel, first),
        grid=(n_col, 2),
        out_shape=jax.ShapeDtypeStruct((n_col * side, feats), F32),
        in_specs=[
            pl.BlockSpec((1, 1, side, side), lambda t, j: (2 * shift + j, t, 0, 0)),
            vmem(),
            vmem(),
        ]
        + ([] if first else [block]),
        out_specs=block,
        compiler_params=params(32),
        cost_estimate=COST,
        name="forward",
    )(dense, x0, x1, *([] if first else [total]))


def middle_kernel(n_col, weights, cot_own, cot_other, *refs):
    other = refs[:n_col]
    own = refs[n_col : 2 * n_col]
    spread, kept, agg, g_own, g_other = refs[2 * n_col :]
    half = cot_own.shape[1]
    f = lax.axis_index("feat")
    mine = pl.ds(pl.multiple_of(f * half, half), half)
    theirs = pl.ds(pl.multiple_of((1 - f) * half, half), half)

    def gather(parts):
        total = parts[0][...].astype(F32)
        for part in parts[1:]:
            total = total + part[...].astype(F32)
        return total.astype(BF16)

    top = jnp.concatenate([weights[mine, mine], weights[mine, theirs]], axis=1)
    low = jnp.concatenate([weights[theirs, mine], weights[theirs, theirs]], axis=1)
    agg_own = gather(own)
    agg[...] = agg_own
    both = jnp.concatenate([agg_own, gather(other)], axis=1)
    hidden = jnp.dot(both, jnp.concatenate([top, low], axis=0), preferred_element_type=F32)
    decay = jnp.exp(jnp.minimum(hidden, 0.0))
    cot = jnp.concatenate([cot_own[...], cot_other[...]], axis=1).astype(F32)
    g = (cot * decay).astype(BF16)
    spread[...] = lax.dot_general(
        top, g, (((1,), (1,)), ((), ())), preferred_element_type=F32
    ).astype(BF16)
    g_own[...] = g[:, :half]
    g_other[...] = g[:, half:]
    kept[...] = hidden[:, :half]


def middle(weights, cot_own, cot_other, own, other):
    nodes, half = cot_own.shape
    whole = weights.shape[1]
    n_col = len(own)
    return pl.pallas_call(
        functools.partial(middle_kernel, n_col),
        out_shape=(
            jax.ShapeDtypeStruct((half, nodes), BF16),
            jax.ShapeDtypeStruct((nodes, half), F32),
        )
        + (jax.ShapeDtypeStruct((nodes, half), BF16),) * 3,
        in_specs=[vmem()] * (3 + 2 * n_col),
        out_specs=(vmem(),) * 5,
        compiler_params=params(),
        cost_estimate=COST,
        name="middle",
    )(weights, cot_own, cot_other, *other, *own)


def weight_kernel(agg, g_own, g_other, out):
    half = agg.shape[1]
    f = lax.axis_index("feat")
    turned = agg[...].astype(F32).T.astype(BF16)
    for columns, g in ((f * half, g_own), ((1 - f) * half, g_other)):
        columns = pl.ds(pl.multiple_of(columns, half), half)
        out[:, columns] = jnp.dot(turned, g[...], preferred_element_type=F32).astype(BF16)


def weight_term(agg, g_own, g_other):
    half = agg.shape[1]
    return pl.pallas_call(
        weight_kernel,
        out_shape=jax.ShapeDtypeStruct((half, 2 * half), BF16),
        in_specs=[vmem()] * 3,
        out_specs=vmem(),
        compiler_params=params(),
        cost_estimate=COST,
        name="weight_term",
    )(agg, g_own, g_other)


def backward_stream_kernel(n_col, a, *refs):
    pieces, out = refs[:n_col], refs[n_col]
    total = jnp.dot(pieces[0][...], a[0, 0], preferred_element_type=F32)
    for t in range(1, n_col):
        total = total + jnp.dot(pieces[t][...], a[0, t], preferred_element_type=F32)
    out[0] = total.astype(BF16)


def backward_stream(dense, parity, pieces):
    n_src, n_col, side, _ = dense.shape
    feats = pieces[0].shape[0]
    n_z = n_src // 2
    return pl.pallas_call(
        functools.partial(backward_stream_kernel, n_col),
        grid=(n_z,),
        out_shape=jax.ShapeDtypeStruct((n_z, feats, side), BF16),
        in_specs=[pl.BlockSpec((1, n_col, side, side), lambda s: (2 * s + parity, 0, 0, 0))]
        + [vmem()] * n_col,
        out_specs=pl.BlockSpec((1, feats, side), lambda s: (s, 0, 0)),
        compiler_params=params(32),
        cost_estimate=COST,
        name="backward",
    )(dense, *pieces)


def add_kernel(a, b, *rest):
    rest[-1][...] = (a[...].astype(F32) + b[...].astype(F32)).astype(BF16)


def add(a, b, *after):
    return pl.pallas_call(
        add_kernel,
        out_shape=jax.ShapeDtypeStruct(a.shape, BF16),
        in_specs=[vmem()] * 2 + [pl.BlockSpec(memory_space=pl.ANY)] * len(after),
        out_specs=vmem(),
        compiler_params=params(),
        cost_estimate=COST,
        name="add",
    )(a, b, *after)


def pair_kernel(own, arrived, *outs):
    for s, out in enumerate(outs):
        out[...] = (own[s].astype(F32) + arrived[s].astype(F32)).astype(BF16)


def pair_sums(own, arrived):
    n_z, side, feats = own.shape
    return pl.pallas_call(
        pair_kernel,
        out_shape=(jax.ShapeDtypeStruct((side, feats), BF16),) * n_z,
        in_specs=[vmem()] * 2,
        out_specs=(vmem(),) * n_z,
        compiler_params=params(),
        cost_estimate=COST,
        name="pair_sums",
    )(own, arrived)


def turned_kernel(*refs):
    total = refs[0][...].astype(F32)
    for part in refs[1:-1]:
        total = total + part[...].astype(F32)
    refs[-1][...] = total.T.astype(BF16)


def turned_sum(parts):
    feats, nodes = parts[0].shape
    return pl.pallas_call(
        turned_kernel,
        out_shape=jax.ShapeDtypeStruct((nodes, feats), BF16),
        in_specs=[vmem()] * len(parts),
        out_specs=vmem(),
        compiler_params=params(),
        cost_estimate=COST,
        name="turned_sum",
    )(*parts)


def shards(features, tile_rows, tile_cols, tile_count, tile_values, weights, cotangent):
    tile = tile_values.shape[-1]
    n_row, n_col = lax.axis_size("row"), lax.axis_size("col")
    n_z = n_row // 2
    nodes, half = features.shape
    blocks = nodes // tile
    node_total = nodes * n_row * n_col

    def sibling(v):
        return lax.ppermute(v, "row", [(i, i ^ 1) for i in range(n_row)])

    def along_z(v, s):
        return lax.ppermute(v, "row", [(i, i ^ (2 * s)) for i in range(n_row)])

    def other_feat(v):
        return lax.ppermute(v, "feat", [(0, 1), (1, 0)])

    def to_group(v, shift, flip):
        pairs = []
        for cc in range(n_col):
            for ff in range(2):
                pairs.append((2 * cc + ff, 2 * ((cc + shift) % n_col) + (ff ^ flip)))
        return lax.ppermute(v, ("col", "feat"), pairs)

    same = [features] + [along_z(features, s) for s in range(1, n_z)]
    cot_other = other_feat(cotangent)
    tiles = tile_values[0, 0]
    cell = (tile_rows, tile_cols, tile_count, tiles, n_z, n_col, blocks)
    if 2 * n_z * n_col * (blocks * tile) ** 2 <= 8 * MIB:
        dense = densify(*cell)
        totals = forward(dense, [0, 1], [features, sibling(features)], (), False)
        *held, cot_other = hold([same[-1]] + same[1:-1] + [cot_other], totals[0])
        same = held[1:] + held[:1]
        cross = [sibling(v) for v in same]
        totals = forward(dense, [2 * s for s in range(1, n_z)], same, totals, False)
        parts = forward(dense, [2 * s + 1 for s in range(1, n_z)], cross, totals, True)

        def back_of(pieces, hidden):
            own, activated = backward_own(dense, pieces[0], hidden)
            return *backward(dense, own, pieces[1:]), activated

    else:
        cross = [sibling(v) for v in same]
        dense = densify_stream(*cell)
        total = None
        for s in range(n_z):
            total = forward_stream(dense, s, same[s], cross[s], total)
        parts = total.astype(BF16).reshape(n_col, nodes, half)

        def back_of(pieces, hidden):
            even, odd = (backward_stream(dense, k, pieces) for k in range(2))
            return even[0], odd[0], even[1:], odd[1:], elu(hidden)

    other = [to_group(parts[t], -t, 1) for t in range(n_col - 1, -1, -1)]
    own = [parts[0]] + [to_group(parts[t], -t, 0) for t in range(1, n_col)]
    spread, hidden, *rest = middle(weights, cotangent, cot_other, own, other)
    pieces = [spread] + [
        lax.ppermute(spread, "col", [(i, (i + t) % n_col) for i in range(n_col)])
        for t in range(1, n_col)
    ]
    term = weight_term(*rest)
    here, there, even, odd, activated = back_of(pieces, hidden)
    term = add(term, along_z(term, 1), odd)
    (odd,) = hold([odd], term)
    sums = pair_sums(even, sibling(odd))
    if n_z > 2:
        term = add(term, along_z(term, 3), sums[0])
    order = sorted(range(1, n_z), key=lambda s: (s != n_z // 2, s))
    back = turned_sum([here, sibling(there)] + [along_z(sums[s - 1], s) for s in order])

    def finish(_, v):
        for step in range(2, n_z.bit_length() - 1):
            v = add(v, along_z(v, 1 << step))
        for step in range(n_col.bit_length() - 1):
            pairs = [(i, i ^ (1 << step)) for i in range(n_col)]
            v = add(v, lax.ppermute(v, "col", pairs))
        return add(v, sibling(v))

    once = lax.optimization_barrier(jnp.int32(1))
    whole = lax.fori_loop(0, once, finish, term)
    weight_grad = whole.astype(F32) * node_total ** (-0.5)
    return (activated, back, weight_grad)


def solution(mesh):
    return jax.shard_map(
        shards,
        mesh=mesh,
        in_specs=(
            P(("col", "row"), "feat"),
            P("row", "col", None),
            P("row", "col", None),
            P("row", "col"),
            P("row", "col", None, None, None),
            P(),
            P(("row", "col"), "feat"),
        ),
        out_specs=(P(("row", "col"), "feat"), P(("col", "row"), "feat"), P("feat", None)),
        check_vma=False,
    )
```

```python
import functools

import jax
import jax.numpy as jnp
from jax import lax
from jax.experimental import pallas as pl
from jax.experimental.pallas import tpu as pltpu
from jax.sharding import PartitionSpec as P

F32 = jnp.float32
BF16 = jnp.bfloat16
MIB = 1024 * 1024
COST = pl.CostEstimate(flops=1, bytes_accessed=1, transcendentals=0)


def params(mib=16):
    return pltpu.CompilerParams(vmem_limit_bytes=mib * MIB)


def vmem():
    return pl.BlockSpec(memory_space=pltpu.VMEM)


def smem():
    return pl.BlockSpec(memory_space=pltpu.SMEM)


def place_of(dims, block_row, block_col):
    n_z, n_col, blocks = dims
    bits, low = blocks.bit_length() - 1, blocks - 1
    j = (block_col >> bits) ^ lax.axis_index("row")
    t = (lax.axis_index("col") - (block_row >> bits)) & (n_col - 1)
    return ((((j * n_col + t) << bits) | (block_row & low)) << bits) | (block_col & low)


def densify_kernel(dims, groups, rows, cols, count, tiles, out, buffer, total, sems):
    n_z, n_col, blocks = dims
    slots, tile = buffer.shape[0], buffer.shape[1]
    per_group = slots // groups
    places = total.shape[0] - 1
    live = count[0, 0]

    def copy(g):
        part = pl.ds(g * per_group, per_group)
        return pltpu.make_async_copy(tiles.at[part], buffer.at[part], sems.at[g])

    def each_group(action):
        for g in range(groups):

            @pl.when(g * per_group < live)
            def _():
                action(g)

    each_group(lambda g: copy(g).start())

    def clear(i, carry):
        total[i] = jnp.zeros((tile, tile), F32)
        return carry

    lax.fori_loop(0, places, clear, 0, unroll=4)

    def add_group(g):
        copy(g).wait()

        def add(i, carry):
            slot = g * per_group + i
            place = place_of(dims, rows[0, 0, slot], cols[0, 0, slot])
            place = jnp.where(slot < live, place, places)
            total[place] += buffer[slot].astype(F32)
            return carry

        lax.fori_loop(0, per_group, add, 0, unroll=8)

    each_group(add_group)

    def settle(j, carry):
        for t in range(n_col):
            for a in range(blocks):
                for b in range(blocks):
                    value = total[((j * n_col + t) * blocks + a) * blocks + b]
                    out[j, t, a * tile : (a + 1) * tile, b * tile : (b + 1) * tile] = value.astype(BF16)
        return carry

    lax.fori_loop(0, 2 * n_z, settle, 0)


def densify(rows, cols, count, tiles, n_z, n_col, blocks):
    slots, tile = tiles.shape[0], tiles.shape[1]
    n_src = 2 * n_z
    groups = 8
    side = blocks * tile
    places = n_src * n_col * blocks * blocks
    return pl.pallas_call(
        functools.partial(densify_kernel, (n_z, n_col, blocks), groups),
        out_shape=pltpu.VMEM((n_src, n_col, side, side), BF16),
        in_specs=[smem(), smem(), smem(), pl.BlockSpec(memory_space=pltpu.HBM)],
        out_specs=vmem(),
        scratch_shapes=[
            pltpu.VMEM((slots, tile, tile), BF16),
            pltpu.VMEM((places + 1, tile, tile), F32),
            pltpu.SemaphoreType.DMA((groups,)),
        ],
        compiler_params=params(32),
        cost_estimate=COST,
        name="densify",
    )(in_hbm(rows), in_hbm(cols), count, in_hbm(tiles))


def in_hbm(v):
    return pltpu.with_memory_space_constraint(v, pltpu.HBM)


def resident(dense):
    return pltpu.with_memory_space_constraint(dense, pltpu.VMEM)


def hold(arrays, after):
    n = len(arrays)
    outs = pl.pallas_call(
        lambda *refs: None,
        out_shape=tuple(jax.ShapeDtypeStruct(v.shape, v.dtype) for v in arrays),
        in_specs=[pl.BlockSpec(memory_space=pl.ANY)] * n + [vmem()],
        out_specs=(pl.BlockSpec(memory_space=pl.ANY),) * n,
        input_output_aliases={i: i for i in range(n)},
        compiler_params=params(),
        cost_estimate=COST,
        name="hold",
    )(*arrays, resident(after))
    return list(outs)


def forward_kernel(places, last, dense, *refs):
    n = len(places)
    xs, refs = refs[:n], refs[n:]
    n_col, side = dense.shape[1], dense.shape[2]
    outs = refs[-n_col:]
    for t in range(n_col):
        total = jnp.dot(dense[places[0], t], xs[0][...], preferred_element_type=F32)
        for j, x in zip(places[1:], xs[1:]):
            total = total + jnp.dot(dense[j, t], x[...], preferred_element_type=F32)
        if len(refs) > n_col:
            total = total + refs[t][...]
        outs[t][...] = total.astype(BF16) if last else total


def forward(dense, places, xs, totals, last):
    _, n_col, side, _ = dense.shape
    feats = xs[0].shape[1]
    shape = jax.ShapeDtypeStruct((side, feats), BF16 if last else F32)
    return pl.pallas_call(
        functools.partial(forward_kernel, places, last),
        out_shape=(shape,) * n_col,
        in_specs=[vmem()] * (1 + len(xs) + len(totals)),
        out_specs=(vmem(),) * n_col,
        compiler_params=params(),
        cost_estimate=COST,
        name="forward",
    )(resident(dense), *xs, *totals)


def elu(h):
    return jnp.where(h > 0, h, jnp.exp(jnp.minimum(h, 0.0)) - 1.0).astype(BF16)


def own_kernel(dense, piece, hidden, out, activated):
    activated[...] = elu(hidden[...])
    for j in range(dense.shape[0]):
        out[j] = jnp.dot(piece[...], dense[j, 0], preferred_element_type=F32)


def backward_own(dense, piece, hidden):
    n_src, _, side, _ = dense.shape
    return pl.pallas_call(
        own_kernel,
        out_shape=(
            pltpu.VMEM((n_src, piece.shape[0], side), F32),
            jax.ShapeDtypeStruct(hidden.shape, BF16),
        ),
        in_specs=[vmem()] * 3,
        out_specs=(vmem(),) * 2,
        compiler_params=params(),
        cost_estimate=COST,
        name="backward_own",
    )(resident(dense), piece, hidden)


def backward_kernel(dense, own, *refs):
    pieces, outs = refs[: dense.shape[1] - 1], refs[-4:]
    for j in range(dense.shape[0]):
        total = own[j]
        for t, piece in enumerate(pieces):
            total = total + jnp.dot(piece[...], dense[j, t + 1], preferred_element_type=F32)
        if j < 2:
            outs[j][...] = total.astype(BF16)
        else:
            outs[2 + j % 2][j // 2 - 1] = total.astype(BF16)


def backward(dense, own, pieces):
    n_src, n_col, side, _ = dense.shape
    feats = own.shape[1]
    return pl.pallas_call(
        backward_kernel,
        out_shape=(jax.ShapeDtypeStruct((feats, side), BF16),) * 2
        + (jax.ShapeDtypeStruct((n_src // 2 - 1, feats, side), BF16),) * 2,
        in_specs=[vmem()] * (1 + n_col),
        out_specs=(vmem(),) * 4,
        compiler_params=params(),
        cost_estimate=COST,
        name="backward",
    )(resident(dense), resident(own), *pieces)


def densify_stream_kernel(
    dims, rows, cols, count, tiles, out, buffer, head, following, sems
):
    n_z, n_col, blocks, slots, groups = dims
    chunk = pl.program_id(0)
    per_chunk = n_col * blocks * blocks
    per_group = slots // groups

    def copy(g):
        part = pl.ds(g * per_group, per_group)
        return pltpu.make_async_copy(tiles.at[part], buffer.at[part], sems.at[g])

    @pl.when(chunk == 0)
    def _():
        for g in range(groups):
            copy(g).start()

        def clear(i, carry):
            head[i] = slots
            return carry

        lax.fori_loop(0, 2 * n_z * per_chunk, clear, 0, unroll=8)
        following[slots] = slots
        buffer[slots] = jnp.zeros(buffer.shape[1:], buffer.dtype)

        def link(slot, carry):
            block_row, block_col = rows[0, 0, slot], cols[0, 0, slot]
            place = place_of((n_z, n_col, blocks), block_row, block_col)
            following[slot] = head[place]
            head[place] = slot
            return carry

        lax.fori_loop(0, count[0, 0], link, 0)
        for g in range(groups):
            copy(g).wait()

    tile = buffer.shape[1]

    def fill(i, carry):
        first = head[chunk * per_chunk + i]
        t = i // (blocks * blocks)
        a = pl.multiple_of((i // blocks) % blocks * tile, tile)
        b = pl.multiple_of(i % blocks * tile, tile)
        where = (0, t, pl.ds(a, tile), pl.ds(b, tile))
        out[where] = buffer[first]
        second = following[first]

        @pl.when(second != slots)
        def _():
            def more(state):
                slot, total = state
                return following[slot], total + buffer[slot].astype(F32)

            _, total = lax.while_loop(
                lambda state: state[0] != slots,
                more,
                (second, buffer[first].astype(F32)),
            )
            out[where] = total.astype(BF16)

        return carry

    lax.fori_loop(0, per_chunk, fill, 0)


def densify_stream(rows, cols, count, tiles, n_z, n_col, blocks):
    slots, tile = tiles.shape[0], tiles.shape[1]
    n_src = 2 * n_z
    groups = 8
    side = blocks * tile
    shape = (n_src, n_col, side, side)
    return pl.pallas_call(
        functools.partial(densify_stream_kernel, (n_z, n_col, blocks, slots, groups)),
        grid=(n_src,),
        out_shape=jax.ShapeDtypeStruct(shape, BF16),
        in_specs=[smem(), smem(), smem(), pl.BlockSpec(memory_space=pltpu.HBM)],
        out_specs=pl.BlockSpec((1, n_col, side, side), lambda j: (j, 0, 0, 0)),
        scratch_shapes=[
            pltpu.VMEM((slots + 1, tile, tile), BF16),
            pltpu.SMEM((n_src * n_col * blocks * blocks,), jnp.int32),
            pltpu.SMEM((slots + 1,), jnp.int32),
            pltpu.SemaphoreType.DMA((groups,)),
        ],
        compiler_params=params(32),
        cost_estimate=COST,
        name="densify",
    )(rows, cols, count, tiles)


def forward_stream_kernel(first, a, x0, x1, *rest):

    j = pl.program_id(1)

    @pl.when(j == 0)
    def _():
        value = jnp.dot(a[0, 0], x0[...], preferred_element_type=F32)
        if not first:
            value = value + rest[0][...]
        rest[-1][...] = value

    @pl.when(j == 1)
    def _():
        rest[-1][...] += jnp.dot(a[0, 0], x1[...], preferred_element_type=F32)


def forward_stream(dense, shift, x0, x1, total):
    _, n_col, side, _ = dense.shape
    feats = x0.shape[1]
    first = total is None
    block = pl.BlockSpec((side, feats), lambda t, j: (t, 0))
    return pl.pallas_call(
        functools.partial(forward_stream_kernel, first),
        grid=(n_col, 2),
        out_shape=jax.ShapeDtypeStruct((n_col * side, feats), F32),
        in_specs=[
            pl.BlockSpec((1, 1, side, side), lambda t, j: (2 * shift + j, t, 0, 0)),
            vmem(),
            vmem(),
        ]
        + ([] if first else [block]),
        out_specs=block,
        compiler_params=params(32),
        cost_estimate=COST,
        name="forward",
    )(dense, x0, x1, *([] if first else [total]))


def middle_kernel(n_col, weights, cot_own, cot_other, *refs):
    other = refs[:n_col]
    own = refs[n_col : 2 * n_col]
    spread, kept, agg, g_own, g_other = refs[2 * n_col :]
    half = cot_own.shape[1]
    f = lax.axis_index("feat")
    mine = pl.ds(pl.multiple_of(f * half, half), half)
    theirs = pl.ds(pl.multiple_of((1 - f) * half, half), half)

    def gather(parts):
        total = parts[0][...].astype(F32)
        for part in parts[1:]:
            total = total + part[...].astype(F32)
        return total.astype(BF16)

    top = jnp.concatenate([weights[mine, mine], weights[mine, theirs]], axis=1)
    low = jnp.concatenate([weights[theirs, mine], weights[theirs, theirs]], axis=1)
    agg_own = gather(own)
    agg[...] = agg_own
    both = jnp.concatenate([agg_own, gather(other)], axis=1)
    hidden = jnp.dot(both, jnp.concatenate([top, low], axis=0), preferred_element_type=F32)
    decay = jnp.exp(jnp.minimum(hidden, 0.0))
    cot = jnp.concatenate([cot_own[...], cot_other[...]], axis=1).astype(F32)
    g = (cot * decay).astype(BF16)
    spread[...] = lax.dot_general(
        top, g, (((1,), (1,)), ((), ())), preferred_element_type=F32
    ).astype(BF16)
    g_own[...] = g[:, :half]
    g_other[...] = g[:, half:]
    kept[...] = hidden[:, :half]


def middle(weights, cot_own, cot_other, own, other):
    nodes, half = cot_own.shape
    whole = weights.shape[1]
    n_col = len(own)
    return pl.pallas_call(
        functools.partial(middle_kernel, n_col),
        out_shape=(
            jax.ShapeDtypeStruct((half, nodes), BF16),
            jax.ShapeDtypeStruct((nodes, half), F32),
        )
        + (jax.ShapeDtypeStruct((nodes, half), BF16),) * 3,
        in_specs=[vmem()] * (3 + 2 * n_col),
        out_specs=(vmem(),) * 5,
        compiler_params=params(),
        cost_estimate=COST,
        name="middle",
    )(weights, cot_own, cot_other, *other, *own)


def weight_kernel(agg, g_own, g_other, out):
    half = agg.shape[1]
    f = lax.axis_index("feat")
    turned = agg[...].astype(F32).T.astype(BF16)
    for columns, g in ((f * half, g_own), ((1 - f) * half, g_other)):
        columns = pl.ds(pl.multiple_of(columns, half), half)
        out[:, columns] = jnp.dot(turned, g[...], preferred_element_type=F32).astype(BF16)


def weight_term(agg, g_own, g_other):
    half = agg.shape[1]
    return pl.pallas_call(
        weight_kernel,
        out_shape=jax.ShapeDtypeStruct((half, 2 * half), BF16),
        in_specs=[vmem()] * 3,
        out_specs=vmem(),
        compiler_params=params(),
        cost_estimate=COST,
        name="weight_term",
    )(agg, g_own, g_other)


def backward_stream_kernel(n_col, a, *refs):
    pieces, out = refs[:n_col], refs[n_col]
    total = jnp.dot(pieces[0][...], a[0, 0], preferred_element_type=F32)
    for t in range(1, n_col):
        total = total + jnp.dot(pieces[t][...], a[0, t], preferred_element_type=F32)
    out[0] = total.astype(BF16)


def backward_stream(dense, parity, pieces):
    n_src, n_col, side, _ = dense.shape
    feats = pieces[0].shape[0]
    n_z = n_src // 2
    return pl.pallas_call(
        functools.partial(backward_stream_kernel, n_col),
        grid=(n_z,),
        out_shape=jax.ShapeDtypeStruct((n_z, feats, side), BF16),
        in_specs=[pl.BlockSpec((1, n_col, side, side), lambda s: (2 * s + parity, 0, 0, 0))]
        + [vmem()] * n_col,
        out_specs=pl.BlockSpec((1, feats, side), lambda s: (s, 0, 0)),
        compiler_params=params(32),
        cost_estimate=COST,
        name="backward",
    )(dense, *pieces)


def add_kernel(a, b, *rest):
    rest[-1][...] = (a[...].astype(F32) + b[...].astype(F32)).astype(BF16)


def add(a, b, *after):
    return pl.pallas_call(
        add_kernel,
        out_shape=jax.ShapeDtypeStruct(a.shape, BF16),
        in_specs=[vmem()] * 2 + [pl.BlockSpec(memory_space=pl.ANY)] * len(after),
        out_specs=vmem(),
        compiler_params=params(),
        cost_estimate=COST,
        name="add",
    )(a, b, *after)


def pair_kernel(own, arrived, *outs):
    for s, out in enumerate(outs):
        out[...] = (own[s].astype(F32) + arrived[s].astype(F32)).astype(BF16)


def pair_sums(own, arrived):
    n_z, side, feats = own.shape
    return pl.pallas_call(
        pair_kernel,
        out_shape=(jax.ShapeDtypeStruct((side, feats), BF16),) * n_z,
        in_specs=[vmem()] * 2,
        out_specs=(vmem(),) * n_z,
        compiler_params=params(),
        cost_estimate=COST,
        name="pair_sums",
    )(own, arrived)


def turned_kernel(*refs):
    total = refs[0][...].astype(F32)
    for part in refs[1:-1]:
        total = total + part[...].astype(F32)
    refs[-1][...] = total.T.astype(BF16)


def turned_sum(parts):
    feats, nodes = parts[0].shape
    return pl.pallas_call(
        turned_kernel,
        out_shape=jax.ShapeDtypeStruct((nodes, feats), BF16),
        in_specs=[vmem()] * len(parts),
        out_specs=vmem(),
        compiler_params=params(),
        cost_estimate=COST,
        name="turned_sum",
    )(*parts)


def shards(features, tile_rows, tile_cols, tile_count, tile_values, weights, cotangent):
    tile = tile_values.shape[-1]
    n_row, n_col = lax.axis_size("row"), lax.axis_size("col")
    n_z = n_row // 2
    nodes, half = features.shape
    blocks = nodes // tile
    node_total = nodes * n_row * n_col

    def sibling(v):
        return lax.ppermute(v, "row", [(i, i ^ 1) for i in range(n_row)])

    def along_z(v, s):
        return lax.ppermute(v, "row", [(i, i ^ (2 * s)) for i in range(n_row)])

    def other_feat(v):
        return lax.ppermute(v, "feat", [(0, 1), (1, 0)])

    def to_group(v, shift, flip):
        pairs = []
        for cc in range(n_col):
            for ff in range(2):
                pairs.append((2 * cc + ff, 2 * ((cc + shift) % n_col) + (ff ^ flip)))
        return lax.ppermute(v, ("col", "feat"), pairs)

    same = [features] + [along_z(features, s) for s in range(1, n_z)]
    cot_other = other_feat(cotangent)
    tiles = tile_values[0, 0]
    cell = (tile_rows, tile_cols, tile_count, tiles, n_z, n_col, blocks)
    if 2 * n_z * n_col * (blocks * tile) ** 2 <= 8 * MIB:
        dense = densify(*cell)
        totals = forward(dense, [0, 1], [features, sibling(features)], (), False)
        *held, cot_other = hold(same[:0:-1] + [cot_other], totals[0])
        same = held[::-1]
        cross = [sibling(v) for v in same]
        totals = forward(dense, [2 * s for s in range(1, n_z)], same, totals, False)
        parts = forward(dense, [2 * s + 1 for s in range(1, n_z)], cross, totals, True)

        def back_of(pieces, hidden):
            own, activated = backward_own(dense, pieces[0], hidden)
            return *backward(dense, own, pieces[1:]), activated

    else:
        cross = [sibling(v) for v in same]
        dense = densify_stream(*cell)
        total = None
        for s in range(n_z):
            total = forward_stream(dense, s, same[s], cross[s], total)
        parts = total.astype(BF16).reshape(n_col, nodes, half)

        def back_of(pieces, hidden):
            even, odd = (backward_stream(dense, k, pieces) for k in range(2))
            return even[0], odd[0], even[1:], odd[1:], elu(hidden)

    other = [to_group(parts[t], -t, 1) for t in range(n_col - 1, -1, -1)]
    own = [parts[0]] + [to_group(parts[t], -t, 0) for t in range(1, n_col)]
    spread, hidden, *rest = middle(weights, cotangent, cot_other, own, other)
    pieces = [spread] + [
        lax.ppermute(spread, "col", [(i, (i + t) % n_col) for i in range(n_col)])
        for t in range(1, n_col)
    ]
    term = weight_term(*rest)
    here, there, even, odd, activated = back_of(pieces, hidden)
    term = add(term, along_z(term, 1), odd)
    (odd,) = hold([odd], term)
    sums = pair_sums(even, sibling(odd))
    if n_z > 2:
        term = add(term, along_z(term, 3), sums[0])
    order = sorted(range(1, n_z), key=lambda s: (s != n_z // 2, s))
    back = turned_sum([here, sibling(there)] + [along_z(sums[s - 1], s) for s in order])

    def finish(_, v):
        for step in range(2, n_z.bit_length() - 1):
            v = add(v, along_z(v, 1 << step))
        for step in range(n_col.bit_length() - 1):
            pairs = [(i, i ^ (1 << step)) for i in range(n_col)]
            v = add(v, lax.ppermute(v, "col", pairs))
        return add(v, sibling(v))

    once = lax.optimization_barrier(jnp.int32(1))
    whole = lax.fori_loop(0, once, finish, term)
    weight_grad = whole.astype(F32) * node_total ** (-0.5)
    return (activated, back, weight_grad)


def solution(mesh):
    return jax.shard_map(
        shards,
        mesh=mesh,
        in_specs=(
            P(("col", "row"), "feat"),
            P("row", "col", None),
            P("row", "col", None),
            P("row", "col"),
            P("row", "col", None, None, None),
            P(),
            P(("row", "col"), "feat"),
        ),
        out_specs=(P(("row", "col"), "feat"), P(("col", "row"), "feat"), P("feat", None)),
        check_vma=False,
    )
```
